128 devices in a mesh: lon: 32 (over x, z, core), lat: 4 (over y).
Axes of the slice: x: 4, y: 4, z: 4, core: 2. Of those that a mesh axis runs over, the one named last changes fastest.
Arguments:
- tracer: float32 [8, 1280, 4096], P(None, 'lat', 'lon'), may hold values from -6 to 6
- east_vel: float32 [8, 1280, 4096], P(None, 'lat', 'lon'), may hold values from -5 to 5
- north_vel: float32 [8, 1280, 4096], P(None, 'lat', 'lon'), may hold values from -5 to 5
- levels: int32 [1280, 4096], P('lat', 'lon'), may hold values from 0 to 8
- forcing: float32 [1280, 4096], P('lat', 'lon'), may hold values from -8 to 8
- storage: float32 [1280, 4096], P('lat', 'lon'), may hold values from 0.02 to 0.2
Outputs:
- new_tracer: float32 [8, 1280, 4096], P(None, 'lat', 'lon')
- surface: float32 [1280, 4096], P('lat', 'lon')
- residual: float32 [1280, 4096], P('lat', 'lon')
The draws below stay inside these ranges and needn't reach their ends.
Inputs may be any that keep to these rules, and one draw needn't show every extreme that they name: `levels`: 0 marks land; 8 marks a column wet at every level of the window.
All inputs are finite; a program needn't handle non-finite values.
Results may differ from the reference program's by a relative error of at most 0.0003.
Values sent between devices are 32-bit elements; how exact they have to be, the bound alone decides.
A program may use at most 128 MiB of HBM per device.

```python
import math
import jax
import jax.numpy as jnp
from jax import lax

KL = 8
ITERS = 5
NLAT = 1280
NLON = 4096


def draw_forcing(key, part):
    key = jax.random.fold_in(key, 11)
    first_key = jax.random.fold_in(key, 0)
    values = jax.random.normal(first_key, (NLAT, NLON), jnp.float32)
    return jnp.clip(values, -8.0, 8.0)


def set_ends(values, key, low, high):
    index_at = [jax.random.randint(jax.random.fold_in(key, axis), (), 0, length) for axis, length in enumerate(values.shape)]
    main_axis = values.shape.index(max(values.shape))
    beside = index_at[:main_axis] + [(index_at[main_axis] + 1) % values.shape[main_axis]] + index_at[main_axis + 1:]
    return values.at[tuple(index_at)].set(low).at[tuple(beside)].set(high)


def block_levels(stream_key, shape, pieces, least, top_value):
    loudness = 1.0
    for position, shards_of in pieces:
        draws = jax.random.uniform(jax.random.fold_in(jax.random.fold_in(stream_key, 6), position), (shards_of,), jnp.float32, least / len(pieces), top_value / len(pieces))
        loudness = loudness * jnp.repeat(jnp.exp(draws), shape[position] // shards_of).reshape((-1,) + (1,) * (len(shape) - 1 - position))
    return loudness


def noise(stream_key, shape, width, bound, shards=(), kind=jnp.bfloat16):
    drawn = jax.random.normal(stream_key, shape, jnp.float32) * width
    if len(shards) > 0:
        drawn = block_levels(stream_key, shape, shards, -0.22, 0.18) * drawn
    return jnp.clip(drawn, min=-bound, max=bound).astype(kind)


def setup_inputs(seed: int = 0) -> dict:
    seeds = jax.random.split(jax.random.key(seed), 7)
    tracer = noise(seeds[0], (KL, NLAT, NLON), 1.0, 6.0, ((1, 4), (2, 32)), jnp.float32)
    east_vel = noise(seeds[1], (KL, NLAT, NLON), 0.8, 5.0, ((1, 4), (2, 32)), jnp.float32)
    north_vel = noise(seeds[2], (KL, NLAT, NLON), 0.8, 5.0, ((1, 4), (2, 32)), jnp.float32)
    levels = set_ends(jax.random.randint(seeds[3], (NLAT, NLON), 0, KL + 1), jax.random.fold_in(seeds[3], 1), 0, KL).astype(jnp.int32)
    forcing = draw_forcing(jax.random.fold_in(seeds[6], 71), 0)
    storage = jnp.clip(jnp.exp(math.log(0.2) - 2.3025851 * jax.random.uniform(seeds[5], (NLAT, NLON), jnp.float32) ** block_levels(seeds[5], (NLAT, NLON), ((0, 4), (1, 32)), -0.2, 0.2)), 0.02, 0.2)
    return dict(tracer=tracer, east_vel=east_vel, north_vel=north_vel, levels=levels, forcing=forcing, storage=storage)


ADVECT = 0.25
SPREAD = 0.12
VERTICAL = 0.1
CORNER = 0.25
OFFSETS = ((1, 0), (-1, 0), (0, 1), (0, -1), (1, 1), (1, -1), (-1, 1), (-1, -1))

def fold_pad(source):
    north_row = source[..., -1:, ::-1]
    south_row = jnp.zeros_like(north_row)
    tall_field = jnp.concatenate([south_row, source, north_row], axis=-2)
    return jnp.concatenate([tall_field[..., -1:], tall_field, tall_field[..., :1]], axis=-1)

def neighbour(padded, step_lat, step_lon):
    row_count = padded.shape[-2] - 2
    col_count = padded.shape[-1] - 2
    return padded[..., 1 + step_lat:1 + step_lat + row_count, 1 + step_lon:1 + step_lon + col_count]

def tendency(padded, not_top):
    temp_pad, wet_pad, east_pad, north_pad = (padded[0], padded[1], padded[2], padded[3])
    temp_mid = neighbour(temp_pad, 0, 0)
    temp_east = neighbour(temp_pad, 0, 1)
    temp_west = neighbour(temp_pad, 0, -1)
    temp_north = neighbour(temp_pad, 1, 0)
    temp_south = neighbour(temp_pad, -1, 0)
    wet_mid = neighbour(wet_pad, 0, 0)
    open_east = wet_mid * neighbour(wet_pad, 0, 1)
    open_west = wet_mid * neighbour(wet_pad, 0, -1)
    open_north = wet_mid * neighbour(wet_pad, 1, 0)
    open_south = wet_mid * neighbour(wet_pad, -1, 0)
    vel_mid = neighbour(east_pad, 0, 0)
    flux_east = 0.25 * (vel_mid + neighbour(east_pad, 0, 1)) * open_east * (temp_mid + temp_east)
    flux_west = 0.25 * (neighbour(east_pad, 0, -1) + vel_mid) * open_west * (temp_west + temp_mid)
    merid_mid = neighbour(north_pad, 0, 0)
    flux_north = 0.25 * (merid_mid + neighbour(north_pad, 1, 0)) * open_north * not_top * (temp_mid + temp_north)
    flux_south = 0.25 * (neighbour(north_pad, -1, 0) + merid_mid) * open_south * (temp_south + temp_mid)
    lateral = open_east * (temp_east - temp_mid) + open_west * (temp_west - temp_mid) + open_north * (temp_north - temp_mid) + open_south * (temp_south - temp_mid)
    zeroes = jnp.zeros_like(temp_mid[:1])
    temp_up = jnp.concatenate([temp_mid[1:], zeroes], axis=0)
    wet_up = jnp.concatenate([wet_mid[1:], zeroes], axis=0)
    temp_down = jnp.concatenate([zeroes, temp_mid[:-1]], axis=0)
    wet_down = jnp.concatenate([zeroes, wet_mid[:-1]], axis=0)
    vertical = wet_mid * wet_up * (temp_up - temp_mid) + wet_mid * wet_down * (temp_down - temp_mid)
    change = ADVECT * (flux_west - flux_east + flux_south - flux_north) + SPREAD * lateral + VERTICAL * vertical
    return temp_mid + wet_mid * change

def couplings(depth_pad, not_top):
    centre = neighbour(depth_pad, 0, 0)
    result = []
    for step_lat, step_lon in OFFSETS:
        beside = neighbour(depth_pad, step_lat, step_lon)
        weight = centre * beside / (centre + beside + 1.0)
        if step_lat != 0 and step_lon != 0:
            weight = CORNER * weight
        if step_lat == 1 and step_lon != 0:
            weight = weight * not_top
        result.append(weight)
    return result

def operate(padded, source, diagonal, weights):
    result = diagonal * source
    for (step_lat, step_lon), weight in zip(OFFSETS, weights):
        result = result - weight * neighbour(padded, step_lat, step_lon)
    return result

def reference(tracer, east_vel, north_vel, levels, forcing, storage):
    layer_index = jnp.arange(KL, dtype=jnp.int32)[:, None, None]
    wet_mask = (layer_index < levels[None]).astype(jnp.float32)
    stacked = jnp.stack([tracer, wet_mask, east_vel, north_vel])
    row_index = jnp.arange(NLAT, dtype=jnp.int32)[:, None]
    not_top = (row_index < NLAT - 1).astype(jnp.float32)
    new_tracer = tendency(fold_pad(stacked), not_top)
    column_wet = (levels > 0).astype(jnp.float32)
    right_side = forcing * column_wet + lax.optimization_barrier(jnp.sum(wet_mask * new_tracer, axis=0)) / jnp.sqrt(jnp.float32(KL))
    weights = couplings(fold_pad(levels.astype(jnp.float32)), not_top)
    diagonal = storage
    for weight in weights:
        diagonal = diagonal + weight
    surface = jnp.zeros_like(right_side)
    residual = right_side
    scaled = residual / diagonal
    direction = scaled
    norm_now = jnp.sum(residual * scaled)
    for turn_index in range(ITERS):
        image = operate(fold_pad(direction), direction, diagonal, weights)
        step_size = norm_now / jnp.sum(direction * image)
        surface = surface + step_size * direction
        residual = residual - step_size * image
        scaled = residual / diagonal
        norm_next = jnp.sum(residual * scaled)
        direction = scaled + norm_next / norm_now * direction
        norm_now = norm_next
    return (new_tracer, surface, residual)
```

```python
import functools

import jax
import jax.numpy as jnp
from jax import lax
from jax.experimental import pallas as pl
from jax.experimental.pallas import tpu as pltpu
from jax.sharding import PartitionSpec as P

ITERS = 5
LEVELS = 8
GHOST = 8
BASE = 2 * GHOST
LANES = 128
EDGE = 6
SCALE = 0.8
MESH = pl.DeviceIdType.MESH

GAIN = (-1.0, 1.0 / SCALE, 2.0 / SCALE, 2.0 / SCALE, 2.0 / SCALE)
SHIFT = (1.0, 0.0, 0.0, 0.0, 0.0)
BACK = (0.0, 0.0, SCALE / 2, SCALE / 2, SCALE / 2)
PAIRS = tuple((i, j) for j in range(ITERS + 1) for i in range(j + 1) if (i, j) != (ITERS, ITERS))


def roll(x, shift):
    return pltpu.roll(x, shift % x.shape[-1], x.ndim - 1)


def lane_of(shape):
    return lax.broadcasted_iota(jnp.int32, shape, len(shape) - 1)


def row_of(shape):
    return lax.broadcasted_iota(jnp.int32, shape, len(shape) - 2)


def face_flux(here, there, vel_here, vel_there, shared, level, factor=None):
    carried = (vel_here + vel_there) * (here + there)
    if factor is not None:
        carried = carried * factor
    return jnp.where(shared > level, 1.92 * (there - here) - carried, 0.0)


def ring_east(main, strip, lane):
    a, b = roll(main, -1), roll(strip, -1)
    last = lane == LANES - 1
    return jnp.where(last, b, a), jnp.where(last, a, b)


def ring_west(main, strip, lane):
    a, b = roll(main, 1), roll(strip, 1)
    first = lane == 0
    return jnp.where(first, b, a), jnp.where(first, a, b)


def solve(gram):
    size = ITERS + 1

    def product(left, right):
        total = None
        for i, a in enumerate(left):
            if a is None:
                continue
            inner = None
            for j, b in enumerate(right):
                if b is None:
                    continue
                term = gram[min(i, j), max(i, j)] * b
                inner = term if inner is None else inner + term
            total = a * inner if total is None else total + a * inner
        return total

    def operate(coeffs):
        out = [None] * size

        def add(k, value):
            out[k] = value if out[k] is None else out[k] + value

        for k in range(ITERS):
            if coeffs[k] is None:
                continue
            add(k + 1, coeffs[k] * (-1.0 / GAIN[k]))
            if SHIFT[k] != 1.0:
                add(k, coeffs[k] * (1.0 - SHIFT[k]))
            if BACK[k] != 0.0:
                add(k - 1, coeffs[k] * (-BACK[k]))
        return out

    one = jnp.ones_like(gram[0, 0])
    scaled = [one] + [None] * ITERS
    direction = list(scaled)
    surface = [None] * size
    rho = product(scaled, scaled)
    for turn in range(ITERS):
        image = operate(direction)
        step = rho / product(direction, image)
        for k in range(size):
            if direction[k] is not None:
                move = step * direction[k]
                surface[k] = move if surface[k] is None else surface[k] + move
            if image[k] is not None:
                move = step * image[k]
                scaled[k] = -move if scaled[k] is None else scaled[k] - move
        if turn == ITERS - 1:
            break
        rho_new = product(scaled, scaled)
        ratio = rho_new / rho
        direction = [
            s if d is None else s + ratio * d for s, d in zip(scaled, direction)
        ]
        rho = rho_new
    return surface[:ITERS], scaled


def kernel(
    lon_count, lat_count, rows,
    t_in, u_in, v_in, lev_in, forc_in, stor_in,
    new_out, surf_out, res_out,
    tr, ur, vr, lv, fo, st,
    pk_e, pk_w, rc_w, rc_e,
    ts, us, vs, ls, sn, total,
    nt, w_e, w_n, w_ne, w_nw, w_er, w_ner, w_nwr, rdiag, diag, basis,
    surf, resid, red1, red2,
    in_sem, ghost_send, ghost_recv, strip_send, strip_recv,
    red1_send, red1_recv, red2_send, red2_recv, out_sem,
):
    lon, lat = lax.axis_index("lon"), lax.axis_index("lat")
    is_top = lat == lat_count - 1
    not_bottom = lat > 0
    top = BASE + rows
    south = BASE - GHOST
    own = pl.ds(BASE, rows)
    tile = (8, LANES)
    lane = lane_of(tile)
    row = row_of(tile)
    groups = rows // 8

    fields_in = (t_in, u_in, v_in, lev_in, forc_in, stor_in)
    fields = (tr, ur, vr, lv, fo, st)

    def rows_at(ref, where):
        return ref.at[:, where, :] if len(ref.shape) == 3 else ref.at[where, :]

    loads = [
        pltpu.make_async_copy(src, rows_at(dst, own), in_sem.at[n])
        for n, (src, dst) in enumerate(zip(fields_in, fields))
    ]
    for load in loads:
        load.start()

    east = lax.rem(lon + 1, lon_count)
    west = lax.rem(lon + lon_count - 1, lon_count)
    up_lat = jnp.where(is_top, lat, lat + 1)
    down_lat = jnp.maximum(lat - 1, 0)
    up_lon = jnp.where(is_top, lon_count - 1 - lon, lon)
    fold_e = lax.rem(2 * lon_count - 2 - lon, lon_count)
    fold_w = lax.rem(lon_count - lon, lon_count)
    up_e = jnp.where(is_top, fold_e, east)
    up_w = jnp.where(is_top, fold_w, west)
    self_e = jnp.logical_and(is_top, fold_e == lon)
    self_w = jnp.logical_and(is_top, fold_w == lon)

    core = lax.rem(lon, 2)
    chip = lon // 2
    chips = lon_count // 2
    near = 2 * lat_count
    near_at = lat * 2 + core

    def near_device(index):
        return {"lon": chip * 2 + lax.rem(index, 2), "lat": index // 2}

    def far_device(index):
        return {"lon": index * 2 + core, "lat": lat}

    barrier = pltpu.get_barrier_semaphore()

    def greet(device):
        pl.semaphore_signal(barrier, inc=1, device_id=device, device_id_type=MESH)

    greet({"lon": east, "lat": lat})
    greet({"lon": west, "lat": lat})
    greet({"lon": up_lon, "lat": up_lat})

    @pl.when(jnp.logical_not(self_e))
    def _():
        greet({"lon": up_e, "lat": up_lat})

    @pl.when(jnp.logical_not(self_w))
    def _():
        greet({"lon": up_w, "lat": up_lat})

    @pl.when(not_bottom)
    def _():
        greet({"lon": lon, "lat": down_lat})
        greet({"lon": east, "lat": down_lat})
        greet({"lon": west, "lat": down_lat})

    for j in range(1, near):
        greet(near_device(lax.rem(near_at + j, near)))
    for j in range(1, chips):
        greet(far_device(lax.rem(chip + j, chips)))

    greeted = 3 + near - 1 + chips - 1
    greeted = greeted + jnp.where(self_e, 0, 1) + jnp.where(self_w, 0, 1) + jnp.where(not_bottom, 3, 0)
    pl.semaphore_wait(barrier, greeted)

    last_in = pl.ds(rows - GHOST, GHOST)
    first_in = pl.ds(0, GHOST)
    north_ghost = pl.ds(top, GHOST)
    south_ghost = pl.ds(south, GHOST)
    up_row = pl.multiple_of(jnp.where(is_top, top, south), 8)
    up_slot = jnp.where(is_top, 1, 0)
    ups, downs = [], []
    for n, (src, dst) in enumerate(zip(fields_in, fields)):
        ups.append(pltpu.make_async_remote_copy(
            rows_at(src, last_in), rows_at(dst, pl.ds(up_row, GHOST)),
            ghost_send.at[0, n], ghost_recv.at[up_slot, n],
            device_id={"lon": up_lon, "lat": up_lat}, device_id_type=MESH,
        ))
        downs.append(pltpu.make_async_remote_copy(
            rows_at(src, first_in), rows_at(dst, north_ghost),
            ghost_send.at[1, n], ghost_recv.at[1, n],
            device_id={"lon": lon, "lat": down_lat}, device_id_type=MESH,
        ))
    for copy in ups:
        copy.start()

    @pl.when(not_bottom)
    def _():
        for copy in downs:
            copy.start()

    for load in loads:
        load.wait()

    def pack(r):
        at = pl.ds(r, 8)
        zero = jnp.zeros(tile, jnp.float32)
        parts = {"e": [zero, zero], "w": [zero, zero]}

        def put(which, slot, x):
            here = jnp.logical_and(lane >= slot, lane < slot + 8)
            parts["e"][which] = jnp.where(here, roll(x, slot + EDGE), parts["e"][which])
            parts["w"][which] = jnp.where(here, roll(x, slot + 2), parts["w"][which])

        for k in range(LEVELS):
            put(0, k * 16, tr[k, at, :])
            put(0, k * 16 + 8, ur[k, at, :])
            put(1, k * 16, vr[k, at, :])
        put(1, 8, lv[at, :].astype(jnp.float32))
        put(1, 24, fo[at, :])
        put(1, 40, st[at, :])
        for which in range(2):
            pk_e[which, at, :] = parts["e"][which]
            pk_w[which, at, :] = parts["w"][which]

    def pack_loop(i, carry):
        pack(pl.multiple_of(BASE + i * 8, 8))
        return carry

    lax.fori_loop(0, groups, pack_loop, 0)

    def strip_copy(src, dst, src_rows, dst_rows, slot, recv_slot, to_lon, to_lat):
        return pltpu.make_async_remote_copy(
            src.at[:, src_rows, :], dst.at[:, dst_rows, :],
            strip_send.at[slot], strip_recv.at[recv_slot],
            device_id={"lon": to_lon, "lat": to_lat}, device_id_type=MESH,
        )

    last_own = pl.ds(top - GHOST, GHOST)
    first_own = pl.ds(BASE, GHOST)
    go_e = strip_copy(pk_e, rc_w, own, own, 0, 0, east, lat)
    go_w = strip_copy(pk_w, rc_e, own, own, 1, 1, west, lat)
    up_e_plain = strip_copy(pk_e, rc_w, last_own, south_ghost, 2, 2, up_e, up_lat)
    up_w_plain = strip_copy(pk_w, rc_e, last_own, south_ghost, 3, 3, up_w, up_lat)
    up_e_fold = strip_copy(pk_e, rc_e, last_own, north_ghost, 2, 5, up_e, up_lat)
    up_w_fold = strip_copy(pk_w, rc_w, last_own, north_ghost, 3, 4, up_w, up_lat)
    up_e_self = pltpu.make_async_copy(
        pk_e.at[:, last_own, :], rc_e.at[:, north_ghost, :], strip_recv.at[5])
    up_w_self = pltpu.make_async_copy(
        pk_w.at[:, last_own, :], rc_w.at[:, north_ghost, :], strip_recv.at[4])
    down_e = strip_copy(pk_e, rc_w, first_own, north_ghost, 4, 4, east, down_lat)
    down_w = strip_copy(pk_w, rc_e, first_own, north_ghost, 5, 5, west, down_lat)
    go_e.start()
    go_w.start()
    fold_e_sent = jnp.logical_and(is_top, jnp.logical_not(self_e))
    fold_w_sent = jnp.logical_and(is_top, jnp.logical_not(self_w))

    @pl.when(jnp.logical_not(is_top))
    def _():
        up_e_plain.start()
        up_w_plain.start()

    @pl.when(fold_e_sent)
    def _():
        up_e_fold.start()

    @pl.when(fold_w_sent)
    def _():
        up_w_fold.start()

    @pl.when(self_e)
    def _():
        up_e_self.start()

    @pl.when(self_w)
    def _():
        up_w_self.start()

    @pl.when(not_bottom)
    def _():
        down_e.start()
        down_w.start()

    fold_row = jnp.where(is_top, top - 1, -1)

    def tracer_rows(r, edge):
        at, up, down = pl.ds(r, 8), pl.ds(r + 1, 8), pl.ds(r - 1, 8)
        depth = lv[at, :]
        open_e = jnp.minimum(depth, roll(depth, -1))
        open_n = jnp.minimum(depth, lv[up, :])
        open_s = jnp.minimum(depth, lv[down, :])
        factor_n = factor_s = None
        if edge:
            factor_n = jnp.where(row + r == fold_row, 0.0, 1.0)
            factor_s = jnp.where(row + (r - 1) == fold_row, 0.0, 1.0)
        below = None
        summed = None
        here = tr[0, at, :]
        for k in range(LEVELS):
            vel = vr[k, at, :]
            zonal = ur[k, at, :]
            flux_e = face_flux(here, roll(here, -1), zonal, roll(zonal, -1), open_e, k)
            flux_n = face_flux(here, tr[k, up, :], vel, vr[k, up, :], open_n, k, factor_n)
            flux_s = face_flux(tr[k, down, :], here, vr[k, down, :], vel, open_s, k, factor_s)
            change = 0.0625 * ((flux_e - roll(flux_e, 1)) + (flux_n - flux_s))
            result = here + change
            if below is not None:
                result = result - below
            if k + 1 < LEVELS:
                above = tr[k + 1, at, :]
                below = jnp.where(depth > k + 1, 0.1 * (above - here), 0.0)
                result = result + below
                here = above
            nt[k, at, :] = result
            wet_part = jnp.where(depth > k, result, 0.0)
            summed = wet_part if summed is None else summed + wet_part
        total[at, :] = summed

    def inner_loop(i, carry):
        tracer_rows(pl.multiple_of(BASE + 8 + i * 8, 8), False)
        return carry

    lax.fori_loop(0, groups - 2, inner_loop, 0)

    @pl.when(not_bottom)
    def _():
        for n, dst in enumerate(fields):
            part = rows_at(dst, south_ghost)
            pltpu.make_async_copy(part, part, ghost_recv.at[0, n]).wait()
        for n, dst in ((2, rc_w), (3, rc_e)):
            part = dst.at[:, south_ghost, :]
            pltpu.make_async_copy(part, part, strip_recv.at[n]).wait()

    for n, dst in enumerate(fields):
        part = rows_at(dst, north_ghost)
        pltpu.make_async_copy(part, part, ghost_recv.at[1, n]).wait()
    for n, dst in ((4, rc_w), (5, rc_e)):
        part = dst.at[:, north_ghost, :]
        pltpu.make_async_copy(part, part, strip_recv.at[n]).wait()

    @pl.when(jnp.logical_not(not_bottom))
    def _():
        for dst in fields + (rc_w, rc_e):
            if len(dst.shape) == 3:
                dst[:, south_ghost, :] = jnp.zeros((dst.shape[0], GHOST, LANES), dst.dtype)
            else:
                dst[south_ghost, :] = jnp.zeros((GHOST, LANES), dst.dtype)

    def swap(x, bit, axis):
        size = x.shape[axis]
        index = lax.broadcasted_iota(jnp.int32, x.shape, axis)
        low = (index // bit) % 2 == 0
        return jnp.where(low, pltpu.roll(x, size - bit, axis), pltpu.roll(x, bit, axis))

    def mirror(x, bits):
        for bit in bits:
            x = swap(x, bit, 1)
        for bit in (1, 2, 4):
            x = swap(x, bit, 0)
        return x

    @pl.when(is_top)
    def _():
        bits = (1, 2, 4, 8, 16, 32, 64)
        at = north_ghost
        for k in range(LEVELS):
            tr[k, at, :] = mirror(tr[k, at, :], bits)
            ur[k, at, :] = -mirror(ur[k, at, :], bits)
            vr[k, at, :] = -mirror(vr[k, at, :], bits)
        for dst in (lv, fo, st):
            dst[at, :] = mirror(dst[at, :], bits)
        field = (lane // 8) % 2
        for dst in (rc_w, rc_e):
            a = mirror(dst[0, at, :], (1, 2, 4))
            b = mirror(dst[1, at, :], (1, 2, 4))
            dst[0, at, :] = jnp.where(field == 1, -a, a)
            dst[1, at, :] = jnp.where(field == 0, -b, b)

    pack(south)
    pack(top)
    for r in (south, BASE, top - 8, top):
        tracer_rows(r, True)

    for n, dst in ((0, rc_w), (1, rc_e)):
        part = dst.at[:, own, :]
        pltpu.make_async_copy(part, part, strip_recv.at[n]).wait()

    column = lane % 8
    side = (lane // 8) % 2
    slab = lane // 16

    def strip_fields(i, carry):
        r = pl.multiple_of(south + i * 8, 8)
        at = pl.ds(r, 8)
        both = []
        for which in range(2):
            a = jnp.where(column >= EDGE, roll(pk_w[which, at, :], 4), rc_w[which, at, :])
            b = jnp.where(column < 2, roll(pk_e[which, at, :], -4), rc_e[which, at, :])
            both.append((a, b))
        (a_w, a_e), (b_w, b_e) = both
        ts[at, :] = jnp.where(side == 0, a_w, roll(a_e, 8))
        us[at, :] = jnp.where(side == 0, roll(a_w, -8), a_e)
        vs[at, :] = jnp.where(side == 0, b_w, roll(b_e, 8))
        extra = jnp.where(side == 0, roll(b_w, -8), b_e)
        depth = jnp.where(slab == 0, extra, 0.0)
        for shift in (16, 32, 64):
            depth = depth + roll(depth, shift)
        ls[at, :] = depth

        def place(x):
            return jnp.where(
                lane < EDGE, roll(x, -10), jnp.where(lane >= LANES - EDGE, roll(x, -6), 0.0))

        basis[0, 1, at, :] = place(roll(extra, -16))
        rdiag[1, at, :] = place(roll(extra, -32))
        basis[1, 1, at, :] = place(extra)
        return carry

    lax.fori_loop(0, groups + 2, strip_fields, 0)

    level = slab.astype(jnp.float32)

    def strip_tracer(i, carry):
        r = pl.multiple_of(south + i * 8, 8)
        at, up, down = pl.ds(r, 8), pl.ds(r + 1, 8), pl.ds(r - 1, 8)
        factor_n = jnp.where(row + r == fold_row, 0.0, 1.0)
        factor_s = jnp.where(row + (r - 1) == fold_row, 0.0, 1.0)
        depth, here, zonal, vel = ls[at, :], ts[at, :], us[at, :], vs[at, :]
        open_e = jnp.minimum(depth, roll(depth, -1))
        open_n = jnp.minimum(depth, ls[up, :])
        open_s = jnp.minimum(depth, ls[down, :])
        flux_e = face_flux(here, roll(here, -1), zonal, roll(zonal, -1), open_e, level)
        flux_n = face_flux(here, ts[up, :], vel, vs[up, :], open_n, level, factor_n)
        flux_s = face_flux(ts[down, :], here, vs[down, :], vel, open_s, level, factor_s)
        change = 0.0625 * ((flux_e - roll(flux_e, 1)) + (flux_n - flux_s))
        rise = jnp.where(
            jnp.logical_and(slab < LEVELS - 1, depth > level + 1.0),
            0.1 * (roll(here, -16) - here), 0.0)
        fall = jnp.where(slab > 0, roll(rise, 16), 0.0)
        result = here + change + rise - fall
        wet_part = jnp.where(depth > level, result, 0.0)
        for shift in (16, 32, 64):
            wet_part = wet_part + roll(wet_part, shift)

        def beside(x):
            return jnp.where(lane % 16 == 5, roll(x, -4), x)

        ends = jnp.logical_or(lane == 0, lane == LANES - 1)
        packed = beside(result)
        for k in range(LEVELS):
            nt[k, at, :] = jnp.where(ends, roll(packed, -(k * 16 + 6)), nt[k, at, :])
        summed = jnp.where(ends, roll(beside(wet_part), -6), total[at, :])
        root = 8.0 ** -0.5
        main_depth = lv[at, :]
        basis[0, 0, at, :] = jnp.where(main_depth > 0, fo[at, :], 0.0) + summed * root

        def place(x):
            return jnp.where(
                lane < EDGE, roll(x, -10), jnp.where(lane >= LANES - EDGE, roll(x, -6), 0.0))

        wet = basis[1, 1, at, :] > 0.0
        basis[0, 1, at, :] = jnp.where(wet, basis[0, 1, at, :], 0.0) + place(wet_part) * root
        basis[1, 0, at, :] = main_depth.astype(jnp.float32)
        return carry

    lax.fori_loop(0, groups + 2, strip_tracer, 0)

    out_new = pltpu.make_async_copy(nt.at[:, own, :], new_out, out_sem.at[0])
    out_new.start()

    def weigh(a, b):
        return a * b / (a + b + 1.0)

    def weights_loop(i, carry):
        r = pl.multiple_of(south + i * 8, 8)
        at, up = pl.ds(r, 8), pl.ds(r + 1, 8)
        d_m, d_s = basis[1, 0, at, :], basis[1, 1, at, :]
        n_m, n_s = basis[1, 0, up, :], basis[1, 1, up, :]
        e_m, e_s = ring_east(d_m, d_s, lane)
        ne_m, ne_s = ring_east(n_m, n_s, lane)
        nw_m, nw_s = ring_west(n_m, n_s, lane)
        corner = jnp.where(row + r == fold_row, 0.0, 0.25)
        east_m, east_s = weigh(d_m, e_m), weigh(d_s, e_s)
        neast_m, neast_s = corner * weigh(d_m, ne_m), corner * weigh(d_s, ne_s)
        nwest_m, nwest_s = corner * weigh(d_m, nw_m), corner * weigh(d_s, nw_s)
        w_e[0, at, :], w_e[1, at, :] = east_m, east_s
        w_n[0, at, :], w_n[1, at, :] = weigh(d_m, n_m), weigh(d_s, n_s)
        w_ne[0, at, :], w_ne[1, at, :] = neast_m, neast_s
        w_nw[0, at, :], w_nw[1, at, :] = nwest_m, nwest_s
        w_er[0, at, :], w_er[1, at, :] = ring_west(east_m, east_s, lane)
        w_ner[0, at, :], w_ner[1, at, :] = ring_west(neast_m, neast_s, lane)
        w_nwr[0, at, :], w_nwr[1, at, :] = ring_east(nwest_m, nwest_s, lane)
        return carry

    lax.fori_loop(0, groups + 2, weights_loop, 0)

    def diagonal_loop(i, carry):
        r = pl.multiple_of(south + i * 8, 8)
        at, down = pl.ds(r, 8), pl.ds(r - 1, 8)
        for half in range(2):
            storage = st[at, :] if half == 0 else rdiag[1, at, :]
            whole = (
                storage + w_e[half, at, :] + w_er[half, at, :] + w_n[half, at, :]
                + w_n[half, down, :] + w_ne[half, at, :] + w_nw[half, at, :]
                + w_ner[half, down, :] + w_nwr[half, down, :])
            inverse = jnp.where(whole > 0.0, 1.0 / whole, 0.0)
            rdiag[half, at, :] = inverse
            if half == 0:
                diag[at, :] = whole
            basis[0, half, at, :] = basis[0, half, at, :] * inverse
        return carry

    lax.fori_loop(0, groups + 2, diagonal_loop, 0)

    gram = {}

    def neighbours_sum(k, r):
        at, up, down = pl.ds(r, 8), pl.ds(r + 1, 8), pl.ds(r - 1, 8)
        sums, to_west, to_east = [], [], []
        for half in range(2):
            x = basis[k, half, at, :]
            x_n = basis[k, half, up, :]
            x_s = basis[k, half, down, :]
            to_east.append(
                w_e[half, at, :] * x + w_ne[half, down, :] * x_s + w_nwr[half, at, :] * x_n)
            to_west.append(
                w_er[half, at, :] * x + w_nw[half, down, :] * x_s + w_ner[half, at, :] * x_n)
            sums.append(w_n[half, at, :] * x_n + w_n[half, down, :] * x_s)
        from_west = ring_west(to_east[0], to_east[1], lane)
        from_east = ring_east(to_west[0], to_west[1], lane)
        return [sums[h] + from_west[h] + from_east[h] for h in range(2)]

    def apply_rows(k, r):
        at = pl.ds(r, 8)
        sums = neighbours_sum(k, r)
        out = []
        for half in range(2):
            x = basis[k, half, at, :]
            y = rdiag[half, at, :] * sums[half]
            if SHIFT[k] != 0.0:
                y = y - SHIFT[k] * x
            if BACK[k] != 0.0:
                y = y - BACK[k] * basis[k - 1, half, at, :]
            y = GAIN[k] * y
            basis[k + 1, half, at, :] = y
            out.append(y)
        return out[0]

    zero = jnp.zeros(tile, jnp.float32)

    def first_gram(i, acc):
        at = pl.ds(pl.multiple_of(BASE + i * 8, 8), 8)
        x = basis[0, 0, at, :]
        return acc + diag[at, :] * x * x

    gram[0, 0] = lax.fori_loop(0, groups, first_gram, zero)
    for k in range(ITERS):
        if k < ITERS - 1:
            apply_rows(k, south)
            apply_rows(k, top)
        terms = [p for p in PAIRS if p[1] == k + 1]

        def apply_loop(i, accs, k=k, terms=terms):
            r = pl.multiple_of(BASE + i * 8, 8)
            at = pl.ds(r, 8)
            y = apply_rows(k, r)
            scaled = diag[at, :] * y
            return tuple(
                acc + scaled * (y if a == k + 1 else basis[a, 0, at, :])
                for acc, (a, _) in zip(accs, terms))

        sums = lax.fori_loop(0, groups, apply_loop, tuple(zero for _ in terms))
        for p, s in zip(terms, sums):
            gram[p] = s

    per_lane = [jnp.sum(gram[p], axis=0, keepdims=True) for p in PAIRS]
    per_lane = per_lane + [jnp.zeros((1, LANES), jnp.float32)] * (24 - len(per_lane))
    stacked = jnp.sum(jnp.concatenate(per_lane, axis=0), axis=1, keepdims=True)
    third = lane // 42
    folded = jnp.where(
        third == 0, stacked[0:8], jnp.where(third == 1, stacked[8:16], stacked[16:24]))

    red1[pl.ds(near_at, 1), :, :] = folded[None]
    sends = []
    for j in range(1, near):
        sends.append(pltpu.make_async_remote_copy(
            red1.at[near_at], red1.at[near_at],
            red1_send.at[j], red1_recv.at[near_at],
            device_id=near_device(lax.rem(near_at + j, near)), device_id_type=MESH,
        ))
    for copy in sends:
        copy.start()
    for j in range(1, near):
        other = lax.rem(near_at + j, near)
        part = red1.at[other]
        pltpu.make_async_copy(part, part, red1_recv.at[other]).wait()
    folded = red1[0]
    for j in range(1, near):
        folded = folded + red1[j]

    red2[pl.ds(chip, 1), :, :] = folded[None]
    far_sends = []
    for j in range(1, chips):
        far_sends.append(pltpu.make_async_remote_copy(
            red2.at[chip], red2.at[chip],
            red2_send.at[j], red2_recv.at[chip],
            device_id=far_device(lax.rem(chip + j, chips)), device_id_type=MESH,
        ))
    for copy in far_sends:
        copy.start()
    for j in range(1, chips):
        other = lax.rem(chip + j, chips)
        part = red2.at[other]
        pltpu.make_async_copy(part, part, red2_recv.at[other]).wait()
    folded = red2[0]
    for j in range(1, chips):
        folded = folded + red2[j]

    sums = {}
    for third_at in range(3):
        spread = jnp.sum(
            jnp.where(lane == third_at * 42, folded, 0.0), axis=1, keepdims=True)
        for n, p in enumerate(PAIRS):
            if n // 8 == third_at:
                sums[p] = jnp.broadcast_to(spread[n % 8:n % 8 + 1], tile)
    surface_by, scaled_by = solve(sums)

    def final_loop(i, carry):
        r = pl.multiple_of(i * 8, 8)
        at = pl.ds(pl.multiple_of(BASE + r, 8), 8)
        x = [basis[k, 0, at, :] for k in range(ITERS + 1)]
        level_at = surface_by[0] * x[0]
        left = scaled_by[0] * x[0]
        for k in range(1, ITERS + 1):
            if k < ITERS:
                level_at = level_at + surface_by[k] * x[k]
            left = left + scaled_by[k] * x[k]
        surf[pl.ds(r, 8), :] = level_at
        resid[pl.ds(r, 8), :] = diag[at, :] * left
        return carry

    lax.fori_loop(0, groups, final_loop, 0)
    out_surf = pltpu.make_async_copy(surf, surf_out, out_sem.at[1])
    out_res = pltpu.make_async_copy(resid, res_out, out_sem.at[2])
    out_surf.start()
    out_res.start()

    for copy in ups:
        copy.wait_send()
    go_e.wait_send()
    go_w.wait_send()

    @pl.when(not_bottom)
    def _():
        for copy in downs:
            copy.wait_send()
        down_e.wait_send()
        down_w.wait_send()

    @pl.when(jnp.logical_not(is_top))
    def _():
        up_e_plain.wait_send()
        up_w_plain.wait_send()

    @pl.when(fold_e_sent)
    def _():
        up_e_fold.wait_send()

    @pl.when(fold_w_sent)
    def _():
        up_w_fold.wait_send()

    for copy in sends + far_sends:
        copy.wait_send()
    out_new.wait()
    out_surf.wait()
    out_res.wait()


def local(lon_count, lat_count, tracer, east_vel, north_vel, levels, forcing, storage):
    rows = tracer.shape[1]
    padded = rows + 4 * GHOST
    flat = (padded, LANES)
    f32 = jnp.float32
    near, chips = 2 * lat_count, lon_count // 2

    def vmem(*shape, dtype=f32):
        return pltpu.VMEM(shape, dtype)

    cube = vmem(LEVELS, *flat)
    pair = vmem(2, *flat)
    plain = vmem(*flat)
    dma = pltpu.SemaphoreType.DMA
    anywhere = pl.BlockSpec(memory_space=pl.ANY)
    return pl.pallas_call(
        functools.partial(kernel, lon_count, lat_count, rows),
        out_shape=(
            jax.ShapeDtypeStruct(tracer.shape, f32),
            jax.ShapeDtypeStruct(levels.shape, f32),
            jax.ShapeDtypeStruct(levels.shape, f32),
        ),
        in_specs=[anywhere] * 6,
        out_specs=(anywhere,) * 3,
        scratch_shapes=[
            cube, cube, cube, vmem(*flat, dtype=jnp.int32), plain, plain,
            pair, pair, pair, pair,
            plain, plain, plain, plain, plain, plain,
            cube, pair, pair, pair, pair, pair, pair, pair, pair, plain,
            vmem(ITERS + 1, 2, *flat),
            vmem(rows, LANES), vmem(rows, LANES),
            vmem(near, 8, LANES), vmem(chips, 8, LANES),
            dma((6,)), dma((2, 6)), dma((2, 6)), dma((6,)), dma((6,)),
            dma((near,)), dma((near,)), dma((chips,)), dma((chips,)), dma((3,)),
        ],
        compiler_params=pltpu.CompilerParams(
            collective_id=0, has_side_effects=True, vmem_limit_bytes=40 * 2**20
        ),
        cost_estimate=pl.CostEstimate(flops=10**8, bytes_accessed=6 * 10**6, transcendentals=0),
        name="ocean_step",
    )(tracer, east_vel, north_vel, levels, forcing, storage)


def solution(mesh):
    cube, flat = P(None, "lat", "lon"), P("lat", "lon")
    return jax.shard_map(
        functools.partial(local, mesh.shape["lon"], mesh.shape["lat"]),
        mesh=mesh,
        in_specs=(cube, cube, cube, flat, flat, flat),
        out_specs=(cube, flat, flat),
        check_vma=False,
    )
```

```python
import functools

import jax
import jax.numpy as jnp
from jax import lax
from jax.experimental import pallas as pl
from jax.experimental.pallas import tpu as pltpu
from jax.sharding import PartitionSpec as P

ITERS = 5
LEVELS = 8
GHOST = 8
BASE = 2 * GHOST
LANES = 128
EDGE = 6
SCALE = 0.8
MESH = pl.DeviceIdType.MESH
PACK_STEP = 40
TRACER_STEP = 16
FIELDS_STEP = 112
STRIPS_STEP = 48
WEIGHTS_STEP = 48
DIAGONAL_STEP = 48
GRAM_STEP = 80
APPLY_STEP = 40
FINAL_STEP = 40

GAIN = (-1.0, 1.0 / SCALE, 2.0 / SCALE, 2.0 / SCALE, 2.0 / SCALE)
SHIFT = (1.0, 0.0, 0.0, 0.0, 0.0)
BACK = (0.0, 0.0, SCALE / 2, SCALE / 2, SCALE / 2)
PAIRS = tuple((i, j) for j in range(ITERS + 1) for i in range(j + 1) if (i, j) != (ITERS, ITERS))


def roll(x, shift):
    return pltpu.roll(x, shift % x.shape[-1], x.ndim - 1)


def lane_of(shape):
    return lax.broadcasted_iota(jnp.int32, shape, len(shape) - 1)


def row_of(shape):
    return lax.broadcasted_iota(jnp.int32, shape, len(shape) - 2)


def sweep(name, first, rows, step, body, start=0):
    whole = rows // step

    def chunk(i, carry):
        return body(pl.multiple_of(first + i * step, 8), step, carry)

    carry = lax.fori_loop(0, whole, chunk, start) if whole else start
    if rows % step:
        carry = body(first + whole * step, rows % step, carry)
    return carry


def remote(name, src, dst, sent, received, device):
    return pltpu.make_async_remote_copy(
        src, dst, sent, received, device_id=device, device_id_type=MESH)


def local_copy(name, src, dst, done):
    return pltpu.make_async_copy(src, dst, done)


def arrived(name, part, received):
    pltpu.make_async_copy(part, part, received).wait()


def face_flux(here, there, vel_here, vel_there, shared, level, factor=None):
    carried = (vel_here + vel_there) * (here + there)
    if factor is not None:
        carried = carried * factor
    return jnp.where(shared > level, 1.92 * (there - here) - carried, 0.0)


def ring_east(main, strip, lane):
    a, b = roll(main, -1), roll(strip, -1)
    last = lane == LANES - 1
    return jnp.where(last, b, a), jnp.where(last, a, b)


def ring_west(main, strip, lane):
    a, b = roll(main, 1), roll(strip, 1)
    first = lane == 0
    return jnp.where(first, b, a), jnp.where(first, a, b)


def solve(gram):
    size = ITERS + 1

    def product(left, right):
        total = None
        for i, a in enumerate(left):
            if a is None:
                continue
            inner = None
            for j, b in enumerate(right):
                if b is None:
                    continue
                term = gram[min(i, j), max(i, j)] * b
                inner = term if inner is None else inner + term
            total = a * inner if total is None else total + a * inner
        return total

    def operate(coeffs):
        out = [None] * size

        def add(k, value):
            out[k] = value if out[k] is None else out[k] + value

        for k in range(ITERS):
            if coeffs[k] is None:
                continue
            add(k + 1, coeffs[k] * (-1.0 / GAIN[k]))
            if SHIFT[k] != 1.0:
                add(k, coeffs[k] * (1.0 - SHIFT[k]))
            if BACK[k] != 0.0:
                add(k - 1, coeffs[k] * (-BACK[k]))
        return out

    one = jnp.ones_like(gram[0, 0])
    scaled = [one] + [None] * ITERS
    direction = list(scaled)
    surface = [None] * size
    rho = product(scaled, scaled)
    for turn in range(ITERS):
        image = operate(direction)
        step = rho / product(direction, image)
        for k in range(size):
            if direction[k] is not None:
                move = step * direction[k]
                surface[k] = move if surface[k] is None else surface[k] + move
            if image[k] is not None:
                move = step * image[k]
                scaled[k] = -move if scaled[k] is None else scaled[k] - move
        if turn == ITERS - 1:
            break
        rho_new = product(scaled, scaled)
        ratio = rho_new / rho
        direction = [
            s if d is None else s + ratio * d for s, d in zip(scaled, direction)
        ]
        rho = rho_new
    return surface[:ITERS], scaled


def kernel(
    lon_count, lat_count, rows,
    t_in, u_in, v_in, lev_in, forc_in, stor_in,
    new_out, surf_out, res_out,
    tr, ur, vr, lv, fo, st,
    pk_e, pk_w, rc_w, rc_e,
    ts, us, vs, ls, sn, total,
    nt, w_e, w_n, w_ne, w_nw, w_er, w_ner, w_nwr, rdiag, diag, basis,
    surf, resid, red1, red2,
    in_sem, ghost_send, ghost_recv, strip_send, strip_recv,
    red1_send, red1_recv, red2_send, red2_recv, out_sem,
):
    lon, lat = lax.axis_index("lon"), lax.axis_index("lat")
    is_top = lat == lat_count - 1
    not_bottom = lat > 0
    top = BASE + rows
    south = BASE - GHOST
    own = pl.ds(BASE, rows)
    tile = (8, LANES)
    lane = lane_of(tile)
    row = row_of(tile)
    reach = rows + 2 * GHOST

    def lanes(n):
        return lane_of((n, LANES))

    def row_is(r, n, which):
        return row_of((n, LANES)) + r == which

    fields_in = (t_in, u_in, v_in, lev_in, forc_in, stor_in)
    fields = (tr, ur, vr, lv, fo, st)

    def rows_at(ref, where):
        return ref.at[:, where, :] if len(ref.shape) == 3 else ref.at[where, :]

    loads = [
        pltpu.make_async_copy(src, rows_at(dst, own), in_sem.at[n])
        for n, (src, dst) in enumerate(zip(fields_in, fields))
    ]
    for load in loads:
        load.start()

    east = lax.rem(lon + 1, lon_count)
    west = lax.rem(lon + lon_count - 1, lon_count)
    up_lat = jnp.where(is_top, lat, lat + 1)
    down_lat = jnp.maximum(lat - 1, 0)
    up_lon = jnp.where(is_top, lon_count - 1 - lon, lon)
    fold_e = lax.rem(2 * lon_count - 2 - lon, lon_count)
    fold_w = lax.rem(lon_count - lon, lon_count)
    up_e = jnp.where(is_top, fold_e, east)
    up_w = jnp.where(is_top, fold_w, west)
    self_e = jnp.logical_and(is_top, fold_e == lon)
    self_w = jnp.logical_and(is_top, fold_w == lon)

    core = lax.rem(lon, 2)
    chip = lon // 2
    chips = lon_count // 2
    near = 2 * lat_count
    near_at = lat * 2 + core

    def near_device(index):
        return {"lon": chip * 2 + lax.rem(index, 2), "lat": index // 2}

    def far_device(index):
        return {"lon": index * 2 + core, "lat": lat}

    barrier = pltpu.get_barrier_semaphore()

    def greet(device):
        pl.semaphore_signal(barrier, inc=1, device_id=device, device_id_type=MESH)

    greet({"lon": east, "lat": lat})
    greet({"lon": west, "lat": lat})
    greet({"lon": up_lon, "lat": up_lat})

    @pl.when(jnp.logical_not(self_e))
    def _():
        greet({"lon": up_e, "lat": up_lat})

    @pl.when(jnp.logical_not(self_w))
    def _():
        greet({"lon": up_w, "lat": up_lat})

    @pl.when(not_bottom)
    def _():
        greet({"lon": lon, "lat": down_lat})
        greet({"lon": east, "lat": down_lat})
        greet({"lon": west, "lat": down_lat})

    for j in range(1, near):
        greet(near_device(lax.rem(near_at + j, near)))
    for j in range(1, chips):
        greet(far_device(lax.rem(chip + j, chips)))

    greeted = 3 + near - 1 + chips - 1
    greeted = greeted + jnp.where(self_e, 0, 1) + jnp.where(self_w, 0, 1) + jnp.where(not_bottom, 3, 0)
    pl.semaphore_wait(barrier, greeted)

    last_in = pl.ds(rows - GHOST, GHOST)
    first_in = pl.ds(0, GHOST)
    north_ghost = pl.ds(top, GHOST)
    south_ghost = pl.ds(south, GHOST)
    up_row = pl.multiple_of(jnp.where(is_top, top, south), 8)
    up_slot = jnp.where(is_top, 1, 0)
    ups, downs = [], []
    for n, (src, dst) in enumerate(zip(fields_in, fields)):
        ups.append(remote(
            "halo", rows_at(src, last_in), rows_at(dst, pl.ds(up_row, GHOST)),
            ghost_send.at[0, n], ghost_recv.at[up_slot, n], {"lon": up_lon, "lat": up_lat},
        ))
        downs.append(remote(
            "halo", rows_at(src, first_in), rows_at(dst, north_ghost),
            ghost_send.at[1, n], ghost_recv.at[1, n], {"lon": lon, "lat": down_lat},
        ))
    for copy in ups:
        copy.start()

    @pl.when(not_bottom)
    def _():
        for copy in downs:
            copy.start()

    for load in loads:
        load.wait()

    def pack(r, n, carry=0):
        at = pl.ds(r, n)
        lane = lanes(n)
        zero = jnp.zeros((n, LANES), jnp.float32)
        parts = {"e": [zero, zero], "w": [zero, zero]}

        def put(which, slot, x):
            here = jnp.logical_and(lane >= slot, lane < slot + 8)
            parts["e"][which] = jnp.where(here, roll(x, slot + EDGE), parts["e"][which])
            parts["w"][which] = jnp.where(here, roll(x, slot + 2), parts["w"][which])

        for k in range(LEVELS):
            put(0, k * 16, tr[k, at, :])
            put(0, k * 16 + 8, ur[k, at, :])
            put(1, k * 16, vr[k, at, :])
        put(1, 8, lv[at, :].astype(jnp.float32))
        put(1, 24, fo[at, :])
        put(1, 40, st[at, :])
        for which in range(2):
            pk_e[which, at, :] = parts["e"][which]
            pk_w[which, at, :] = parts["w"][which]
        return carry

    sweep("pack", BASE, rows, PACK_STEP, pack)

    def strip_copy(src, dst, src_rows, dst_rows, slot, recv_slot, to_lon, to_lat):
        return remote(
            "halo", src.at[:, src_rows, :], dst.at[:, dst_rows, :],
            strip_send.at[slot], strip_recv.at[recv_slot], {"lon": to_lon, "lat": to_lat},
        )

    last_own = pl.ds(top - GHOST, GHOST)
    first_own = pl.ds(BASE, GHOST)
    go_e = strip_copy(pk_e, rc_w, own, own, 0, 0, east, lat)
    go_w = strip_copy(pk_w, rc_e, own, own, 1, 1, west, lat)
    up_e_plain = strip_copy(pk_e, rc_w, last_own, south_ghost, 2, 2, up_e, up_lat)
    up_w_plain = strip_copy(pk_w, rc_e, last_own, south_ghost, 3, 3, up_w, up_lat)
    up_e_fold = strip_copy(pk_e, rc_e, last_own, north_ghost, 2, 5, up_e, up_lat)
    up_w_fold = strip_copy(pk_w, rc_w, last_own, north_ghost, 3, 4, up_w, up_lat)
    up_e_self = local_copy(
        "halo", pk_e.at[:, last_own, :], rc_e.at[:, north_ghost, :], strip_recv.at[5])
    up_w_self = local_copy(
        "halo", pk_w.at[:, last_own, :], rc_w.at[:, north_ghost, :], strip_recv.at[4])
    down_e = strip_copy(pk_e, rc_w, first_own, north_ghost, 4, 4, east, down_lat)
    down_w = strip_copy(pk_w, rc_e, first_own, north_ghost, 5, 5, west, down_lat)
    go_e.start()
    go_w.start()
    fold_e_sent = jnp.logical_and(is_top, jnp.logical_not(self_e))
    fold_w_sent = jnp.logical_and(is_top, jnp.logical_not(self_w))

    @pl.when(jnp.logical_not(is_top))
    def _():
        up_e_plain.start()
        up_w_plain.start()

    @pl.when(fold_e_sent)
    def _():
        up_e_fold.start()

    @pl.when(fold_w_sent)
    def _():
        up_w_fold.start()

    @pl.when(self_e)
    def _():
        up_e_self.start()

    @pl.when(self_w)
    def _():
        up_w_self.start()

    @pl.when(not_bottom)
    def _():
        down_e.start()
        down_w.start()

    fold_row = jnp.where(is_top, top - 1, -1)

    def tracer_rows(r, n, edge):
        at, up, down = pl.ds(r, n), pl.ds(r + 1, n), pl.ds(r - 1, n)
        depth = lv[at, :]
        open_e = jnp.minimum(depth, roll(depth, -1))
        open_n = jnp.minimum(depth, lv[up, :])
        open_s = jnp.minimum(depth, lv[down, :])
        factor_n = factor_s = None
        if edge:
            factor_n = jnp.where(row_is(r, n, fold_row), 0.0, 1.0)
            factor_s = jnp.where(row_is(r - 1, n, fold_row), 0.0, 1.0)
        below = None
        summed = None
        here = tr[0, at, :]
        for k in range(LEVELS):
            vel = vr[k, at, :]
            zonal = ur[k, at, :]
            flux_e = face_flux(here, roll(here, -1), zonal, roll(zonal, -1), open_e, k)
            flux_n = face_flux(here, tr[k, up, :], vel, vr[k, up, :], open_n, k, factor_n)
            flux_s = face_flux(tr[k, down, :], here, vr[k, down, :], vel, open_s, k, factor_s)
            change = 0.0625 * ((flux_e - roll(flux_e, 1)) + (flux_n - flux_s))
            result = here + change
            if below is not None:
                result = result - below
            if k + 1 < LEVELS:
                above = tr[k + 1, at, :]
                below = jnp.where(depth > k + 1, 0.1 * (above - here), 0.0)
                result = result + below
                here = above
            nt[k, at, :] = result
            wet_part = jnp.where(depth > k, result, 0.0)
            summed = wet_part if summed is None else summed + wet_part
        total[at, :] = summed

    def inner_rows(r, n, carry):
        tracer_rows(r, n, False)
        return carry

    sweep("tracer", BASE + 8, rows - 16, TRACER_STEP, inner_rows)

    @pl.when(not_bottom)
    def _():
        for n, dst in enumerate(fields):
            part = rows_at(dst, south_ghost)
            arrived("halo", part, ghost_recv.at[0, n])
        for n, dst in ((2, rc_w), (3, rc_e)):
            part = dst.at[:, south_ghost, :]
            arrived("halo", part, strip_recv.at[n])

    for n, dst in enumerate(fields):
        part = rows_at(dst, north_ghost)
        arrived("halo", part, ghost_recv.at[1, n])
    for n, dst in ((4, rc_w), (5, rc_e)):
        part = dst.at[:, north_ghost, :]
        arrived("halo", part, strip_recv.at[n])

    @pl.when(jnp.logical_not(not_bottom))
    def _():
        for dst in fields + (rc_w, rc_e):
            if len(dst.shape) == 3:
                dst[:, south_ghost, :] = jnp.zeros((dst.shape[0], GHOST, LANES), dst.dtype)
            else:
                dst[south_ghost, :] = jnp.zeros((GHOST, LANES), dst.dtype)

    def swap(x, bit, axis):
        size = x.shape[axis]
        index = lax.broadcasted_iota(jnp.int32, x.shape, axis)
        low = (index // bit) % 2 == 0
        return jnp.where(low, pltpu.roll(x, size - bit, axis), pltpu.roll(x, bit, axis))

    def mirror(x, bits):
        for bit in bits:
            x = swap(x, bit, 1)
        for bit in (1, 2, 4):
            x = swap(x, bit, 0)
        return x

    @pl.when(is_top)
    def _():
        bits = (1, 2, 4, 8, 16, 32, 64)
        at = north_ghost
        for k in range(LEVELS):
            tr[k, at, :] = mirror(tr[k, at, :], bits)
            ur[k, at, :] = -mirror(ur[k, at, :], bits)
            vr[k, at, :] = -mirror(vr[k, at, :], bits)
        for dst in (lv, fo, st):
            dst[at, :] = mirror(dst[at, :], bits)
        field = (lane // 8) % 2
        for dst in (rc_w, rc_e):
            a = mirror(dst[0, at, :], (1, 2, 4))
            b = mirror(dst[1, at, :], (1, 2, 4))
            dst[0, at, :] = jnp.where(field == 1, -a, a)
            dst[1, at, :] = jnp.where(field == 0, -b, b)

    pack(south, GHOST)
    pack(top, GHOST)
    tracer_rows(south, 16, True)
    tracer_rows(top - 8, 16, True)

    for n, dst in ((0, rc_w), (1, rc_e)):
        part = dst.at[:, own, :]
        arrived("halo", part, strip_recv.at[n])

    def place(x):
        lane = lanes(x.shape[0])
        return jnp.where(
            lane < EDGE, roll(x, -10), jnp.where(lane >= LANES - EDGE, roll(x, -6), 0.0))

    def strip_fields(r, n, carry):
        at = pl.ds(r, n)
        lane = lanes(n)
        column, side, slab = lane % 8, (lane // 8) % 2, lane // 16
        both = []
        for which in range(2):
            a = jnp.where(column >= EDGE, roll(pk_w[which, at, :], 4), rc_w[which, at, :])
            b = jnp.where(column < 2, roll(pk_e[which, at, :], -4), rc_e[which, at, :])
            both.append((a, b))
        (a_w, a_e), (b_w, b_e) = both
        ts[at, :] = jnp.where(side == 0, a_w, roll(a_e, 8))
        us[at, :] = jnp.where(side == 0, roll(a_w, -8), a_e)
        vs[at, :] = jnp.where(side == 0, b_w, roll(b_e, 8))
        extra = jnp.where(side == 0, roll(b_w, -8), b_e)
        depth = jnp.where(slab == 0, extra, 0.0)
        for shift in (16, 32, 64):
            depth = depth + roll(depth, shift)
        ls[at, :] = depth
        basis[0, 1, at, :] = place(roll(extra, -16))
        rdiag[1, at, :] = place(roll(extra, -32))
        basis[1, 1, at, :] = place(extra)
        return carry

    sweep("fields", south, reach, FIELDS_STEP, strip_fields)

    def strip_tracer(r, n, carry):
        at, up, down = pl.ds(r, n), pl.ds(r + 1, n), pl.ds(r - 1, n)
        lane = lanes(n)
        slab = lane // 16
        level = slab.astype(jnp.float32)
        factor_n = jnp.where(row_is(r, n, fold_row), 0.0, 1.0)
        factor_s = jnp.where(row_is(r - 1, n, fold_row), 0.0, 1.0)
        depth, here, zonal, vel = ls[at, :], ts[at, :], us[at, :], vs[at, :]
        open_e = jnp.minimum(depth, roll(depth, -1))
        open_n = jnp.minimum(depth, ls[up, :])
        open_s = jnp.minimum(depth, ls[down, :])
        flux_e = face_flux(here, roll(here, -1), zonal, roll(zonal, -1), open_e, level)
        flux_n = face_flux(here, ts[up, :], vel, vs[up, :], open_n, level, factor_n)
        flux_s = face_flux(ts[down, :], here, vs[down, :], vel, open_s, level, factor_s)
        change = 0.0625 * ((flux_e - roll(flux_e, 1)) + (flux_n - flux_s))
        rise = jnp.where(
            jnp.logical_and(slab < LEVELS - 1, depth > level + 1.0),
            0.1 * (roll(here, -16) - here), 0.0)
        fall = jnp.where(slab > 0, roll(rise, 16), 0.0)
        result = here + change + rise - fall
        wet_part = jnp.where(depth > level, result, 0.0)
        for shift in (16, 32, 64):
            wet_part = wet_part + roll(wet_part, shift)

        def beside(x):
            return jnp.where(lane % 16 == 5, roll(x, -4), x)

        ends = jnp.logical_or(lane == 0, lane == LANES - 1)
        packed = beside(result)
        for k in range(LEVELS):
            nt[k, at, :] = jnp.where(ends, roll(packed, -(k * 16 + 6)), nt[k, at, :])
        summed = jnp.where(ends, roll(beside(wet_part), -6), total[at, :])
        root = 8.0 ** -0.5
        main_depth = lv[at, :]
        basis[0, 0, at, :] = jnp.where(main_depth > 0, fo[at, :], 0.0) + summed * root
        wet = basis[1, 1, at, :] > 0.0
        basis[0, 1, at, :] = jnp.where(wet, basis[0, 1, at, :], 0.0) + place(wet_part) * root
        basis[1, 0, at, :] = main_depth.astype(jnp.float32)
        return carry

    sweep("strips", south, reach, STRIPS_STEP, strip_tracer)

    out_new = pltpu.make_async_copy(nt.at[:, own, :], new_out, out_sem.at[0])
    out_new.start()

    def weigh(a, b):
        return a * b / (a + b + 1.0)

    def weights_rows(r, n, carry):
        at, up = pl.ds(r, n), pl.ds(r + 1, n)
        lane = lanes(n)
        d_m, d_s = basis[1, 0, at, :], basis[1, 1, at, :]
        n_m, n_s = basis[1, 0, up, :], basis[1, 1, up, :]
        e_m, e_s = ring_east(d_m, d_s, lane)
        ne_m, ne_s = ring_east(n_m, n_s, lane)
        nw_m, nw_s = ring_west(n_m, n_s, lane)
        corner = jnp.where(row_is(r, n, fold_row), 0.0, 0.25)
        east_m, east_s = weigh(d_m, e_m), weigh(d_s, e_s)
        neast_m, neast_s = corner * weigh(d_m, ne_m), corner * weigh(d_s, ne_s)
        nwest_m, nwest_s = corner * weigh(d_m, nw_m), corner * weigh(d_s, nw_s)
        w_e[0, at, :], w_e[1, at, :] = east_m, east_s
        w_n[0, at, :], w_n[1, at, :] = weigh(d_m, n_m), weigh(d_s, n_s)
        w_ne[0, at, :], w_ne[1, at, :] = neast_m, neast_s
        w_nw[0, at, :], w_nw[1, at, :] = nwest_m, nwest_s
        w_er[0, at, :], w_er[1, at, :] = ring_west(east_m, east_s, lane)
        w_ner[0, at, :], w_ner[1, at, :] = ring_west(neast_m, neast_s, lane)
        w_nwr[0, at, :], w_nwr[1, at, :] = ring_east(nwest_m, nwest_s, lane)
        return carry

    sweep("weights", south, reach, WEIGHTS_STEP, weights_rows)

    def diagonal_rows(r, n, carry):
        at, down = pl.ds(r, n), pl.ds(r - 1, n)
        for half in range(2):
            storage = st[at, :] if half == 0 else rdiag[1, at, :]
            whole = (
                storage + w_e[half, at, :] + w_er[half, at, :] + w_n[half, at, :]
                + w_n[half, down, :] + w_ne[half, at, :] + w_nw[half, at, :]
                + w_ner[half, down, :] + w_nwr[half, down, :])
            inverse = jnp.where(whole > 0.0, 1.0 / whole, 0.0)
            rdiag[half, at, :] = inverse
            if half == 0:
                diag[at, :] = whole
            basis[0, half, at, :] = basis[0, half, at, :] * inverse
        return carry

    sweep("diagonal", south, reach, DIAGONAL_STEP, diagonal_rows)

    gram = {}

    def neighbours_sum(k, r, n):
        at, up, down = pl.ds(r, n), pl.ds(r + 1, n), pl.ds(r - 1, n)
        lane = lanes(n)
        sums, to_west, to_east = [], [], []
        for half in range(2):
            x = basis[k, half, at, :]
            x_n = basis[k, half, up, :]
            x_s = basis[k, half, down, :]
            to_east.append(
                w_e[half, at, :] * x + w_ne[half, down, :] * x_s + w_nwr[half, at, :] * x_n)
            to_west.append(
                w_er[half, at, :] * x + w_nw[half, down, :] * x_s + w_ner[half, at, :] * x_n)
            sums.append(w_n[half, at, :] * x_n + w_n[half, down, :] * x_s)
        from_west = ring_west(to_east[0], to_east[1], lane)
        from_east = ring_east(to_west[0], to_west[1], lane)
        return [sums[h] + from_west[h] + from_east[h] for h in range(2)]

    def apply_rows(k, r, n):
        at = pl.ds(r, n)
        sums = neighbours_sum(k, r, n)
        out = []
        for half in range(2):
            x = basis[k, half, at, :]
            y = rdiag[half, at, :] * sums[half]
            if SHIFT[k] != 0.0:
                y = y - SHIFT[k] * x
            if BACK[k] != 0.0:
                y = y - BACK[k] * basis[k - 1, half, at, :]
            y = GAIN[k] * y
            basis[k + 1, half, at, :] = y
            out.append(y)
        return out[0]

    zero = jnp.zeros(tile, jnp.float32)

    def fold_rows(x):
        return jnp.sum(x.reshape(x.shape[0] // 8, 8, LANES), axis=0)

    def first_gram(r, n, acc):
        at = pl.ds(r, n)
        x = basis[0, 0, at, :]
        return acc + fold_rows(diag[at, :] * x * x)

    gram[0, 0] = sweep("gram", BASE, rows, GRAM_STEP, first_gram, zero)
    for k in range(ITERS):
        if k < ITERS - 1:
            apply_rows(k, south, GHOST)
            apply_rows(k, top, GHOST)
        terms = [p for p in PAIRS if p[1] == k + 1]

        def apply_own(r, n, accs, k=k, terms=terms):
            at = pl.ds(r, n)
            y = apply_rows(k, r, n)
            scaled = diag[at, :] * y
            return tuple(
                acc + fold_rows(scaled * (y if a == k + 1 else basis[a, 0, at, :]))
                for acc, (a, _) in zip(accs, terms))

        sums = sweep("apply", BASE, rows, APPLY_STEP, apply_own, tuple(zero for _ in terms))
        for p, s in zip(terms, sums):
            gram[p] = s

    per_lane = [jnp.sum(gram[p], axis=0, keepdims=True) for p in PAIRS]
    per_lane = per_lane + [jnp.zeros((1, LANES), jnp.float32)] * (24 - len(per_lane))
    stacked = jnp.sum(jnp.concatenate(per_lane, axis=0), axis=1, keepdims=True)
    third = lane // 42
    folded = jnp.where(
        third == 0, stacked[0:8], jnp.where(third == 1, stacked[8:16], stacked[16:24]))

    red1[pl.ds(near_at, 1), :, :] = folded[None]
    sends = []
    for j in range(1, near):
        sends.append(remote(
            "red", red1.at[near_at], red1.at[near_at],
            red1_send.at[j], red1_recv.at[near_at], near_device(lax.rem(near_at + j, near)),
        ))
    for copy in sends:
        copy.start()
    for j in range(1, near):
        other = lax.rem(near_at + j, near)
        part = red1.at[other]
        arrived("red", part, red1_recv.at[other])
    folded = red1[0]
    for j in range(1, near):
        folded = folded + red1[j]

    red2[pl.ds(chip, 1), :, :] = folded[None]
    far_sends = []
    for j in range(1, chips):
        far_sends.append(remote(
            "red", red2.at[chip], red2.at[chip],
            red2_send.at[j], red2_recv.at[chip], far_device(lax.rem(chip + j, chips)),
        ))
    for copy in far_sends:
        copy.start()
    for j in range(1, chips):
        other = lax.rem(chip + j, chips)
        part = red2.at[other]
        arrived("red", part, red2_recv.at[other])
    folded = red2[0]
    for j in range(1, chips):
        folded = folded + red2[j]

    sums = {}
    for third_at in range(3):
        spread = jnp.sum(
            jnp.where(lane == third_at * 42, folded, 0.0), axis=1, keepdims=True)
        for n, p in enumerate(PAIRS):
            if n // 8 == third_at:
                sums[p] = jnp.broadcast_to(spread[n % 8:n % 8 + 1], tile)
    surface_by, scaled_by = solve(sums)

    surface_by = [c[0:1] for c in surface_by]
    scaled_by = [c[0:1] for c in scaled_by]

    def final_rows(r, n, carry):
        at = pl.ds(r, n)
        to = pl.ds(pl.multiple_of(r - BASE, 8), n)
        x = [basis[k, 0, at, :] for k in range(ITERS + 1)]
        level_at = surface_by[0] * x[0]
        left = scaled_by[0] * x[0]
        for k in range(1, ITERS + 1):
            if k < ITERS:
                level_at = level_at + surface_by[k] * x[k]
            left = left + scaled_by[k] * x[k]
        surf[to, :] = level_at
        resid[to, :] = diag[at, :] * left
        return carry

    sweep("final", BASE, rows, FINAL_STEP, final_rows)
    out_surf = pltpu.make_async_copy(surf, surf_out, out_sem.at[1])
    out_res = pltpu.make_async_copy(resid, res_out, out_sem.at[2])
    out_surf.start()
    out_res.start()

    for copy in ups:
        copy.wait_send()
    go_e.wait_send()
    go_w.wait_send()

    @pl.when(not_bottom)
    def _():
        for copy in downs:
            copy.wait_send()
        down_e.wait_send()
        down_w.wait_send()

    @pl.when(jnp.logical_not(is_top))
    def _():
        up_e_plain.wait_send()
        up_w_plain.wait_send()

    @pl.when(fold_e_sent)
    def _():
        up_e_fold.wait_send()

    @pl.when(fold_w_sent)
    def _():
        up_w_fold.wait_send()

    for copy in sends + far_sends:
        copy.wait_send()
    out_new.wait()
    out_surf.wait()
    out_res.wait()


def local(lon_count, lat_count, tracer, east_vel, north_vel, levels, forcing, storage):
    rows = tracer.shape[1]
    padded = rows + 4 * GHOST
    flat = (padded, LANES)
    f32 = jnp.float32
    near, chips = 2 * lat_count, lon_count // 2

    def vmem(*shape, dtype=f32):
        return pltpu.VMEM(shape, dtype)

    cube = vmem(LEVELS, *flat)
    pair = vmem(2, *flat)
    plain = vmem(*flat)
    dma = pltpu.SemaphoreType.DMA
    anywhere = pl.BlockSpec(memory_space=pl.ANY)
    return pl.pallas_call(
        functools.partial(kernel, lon_count, lat_count, rows),
        out_shape=(
            jax.ShapeDtypeStruct(tracer.shape, f32),
            jax.ShapeDtypeStruct(levels.shape, f32),
            jax.ShapeDtypeStruct(levels.shape, f32),
        ),
        in_specs=[anywhere] * 6,
        out_specs=(anywhere,) * 3,
        scratch_shapes=[
            cube, cube, cube, vmem(*flat, dtype=jnp.int32), plain, plain,
            pair, pair, pair, pair,
            plain, plain, plain, plain, plain, plain,
            cube, pair, pair, pair, pair, pair, pair, pair, pair, plain,
            vmem(ITERS + 1, 2, *flat),
            vmem(rows, LANES), vmem(rows, LANES),
            vmem(near, 8, LANES), vmem(chips, 8, LANES),
            dma((6,)), dma((2, 6)), dma((2, 6)), dma((6,)), dma((6,)),
            dma((near,)), dma((near,)), dma((chips,)), dma((chips,)), dma((3,)),
        ],
        compiler_params=pltpu.CompilerParams(
            collective_id=0, has_side_effects=True, vmem_limit_bytes=60 * 2**20
        ),
        cost_estimate=pl.CostEstimate(flops=10**8, bytes_accessed=6 * 10**6, transcendentals=0),
        name="ocean_step",
    )(tracer, east_vel, north_vel, levels, forcing, storage)


def solution(mesh):
    cube, flat = P(None, "lat", "lon"), P("lat", "lon")
    return jax.shard_map(
        functools.partial(local, mesh.shape["lon"], mesh.shape["lat"]),
        mesh=mesh,
        in_specs=(cube, cube, cube, flat, flat, flat),
        out_specs=(cube, flat, flat),
        check_vma=False,
    )
```

```python
import functools

import jax
import jax.numpy as jnp
from jax import lax
from jax.experimental import pallas as pl
from jax.experimental.pallas import tpu as pltpu
from jax.sharding import PartitionSpec as P

ITERS = 5
LEVELS = 8
GHOST = 8
BASE = 2 * GHOST
LANES = 128
EDGE = 8
PARTS = 8
SCALE = 0.8
MESH = pl.DeviceIdType.MESH
STAGES = (("core", "y"), ("x", "z"))
TRACER_STEP = 16
WEIGHTS_STEP = 112
DIAGONAL_STEP = 48
SCALED_STEP = 112
APPLY_STEP = 112
LAST_STEP = 160
FINAL_STEP = 80

GAIN = (-1.0, 1.0 / SCALE, 2.0 / SCALE, 2.0 / SCALE, 2.0 / SCALE)
SHIFT = (1.0, 0.0, 0.0, 0.0, 0.0)
BACK = (0.0, 0.0, SCALE / 2, SCALE / 2, SCALE / 2)
PAIRS = tuple((i, j) for j in range(ITERS + 1) for i in range(j + 1) if (i, j) != (ITERS, ITERS))


def roll(x, shift):
    return pltpu.roll(x, shift % x.shape[-1], x.ndim - 1)


def lane_of(shape):
    return lax.broadcasted_iota(jnp.int32, shape, len(shape) - 1)


def row_of(shape):
    return lax.broadcasted_iota(jnp.int32, shape, len(shape) - 2)


def extents(lon_count, lat_count):
    z = min(4, lon_count // 2)
    return {"core": 2, "z": z, "x": lon_count // (2 * z), "y": lat_count}


def stage_size(extent, axes):
    size = 1
    for axis in axes:
        size *= extent[axis]
    return size


def sweep(name, first, rows, step, body, start=0):
    whole = rows // step

    def chunk(i, carry):
        return body(pl.multiple_of(first + i * step, 8), step, carry)

    carry = lax.fori_loop(0, whole, chunk, start) if whole else start
    if rows % step:
        carry = body(first + whole * step, rows % step, carry)
    return carry


def remote(name, src, dst, sent, received, device):
    return pltpu.make_async_remote_copy(
        src, dst, sent, received, device_id=device, device_id_type=MESH)


def local_copy(name, src, dst, done):
    return pltpu.make_async_copy(src, dst, done)


def step(name, run):
    run()


def arrived(name, part, received):
    pltpu.make_async_copy(part, part, received).wait()


def face_flux(here, there, vel_here, vel_there, shared, level):
    carried = (vel_here + vel_there) * (here + there)
    return jnp.where(shared > level, 1.92 * (there - here) - carried, 0.0)


def ring_east(main, strip, lane):
    a, b = roll(main, -1), roll(strip, -1)
    last = lane == LANES - 1
    return jnp.where(last, b, a), jnp.where(last, a, b)


def ring_west(main, strip, lane):
    a, b = roll(main, 1), roll(strip, 1)
    first = lane == 0
    return jnp.where(first, b, a), jnp.where(first, a, b)


def solve(gram):
    size = ITERS + 1

    def product(left, right):
        total = None
        for i, a in enumerate(left):
            if a is None:
                continue
            inner = None
            for j, b in enumerate(right):
                if b is None:
                    continue
                term = gram[min(i, j), max(i, j)] * b
                inner = term if inner is None else inner + term
            total = a * inner if total is None else total + a * inner
        return total

    def operate(coeffs):
        out = [None] * size

        def add(k, value):
            out[k] = value if out[k] is None else out[k] + value

        for k in range(ITERS):
            if coeffs[k] is None:
                continue
            add(k + 1, coeffs[k] * (-1.0 / GAIN[k]))
            if SHIFT[k] != 1.0:
                add(k, coeffs[k] * (1.0 - SHIFT[k]))
            if BACK[k] != 0.0:
                add(k - 1, coeffs[k] * (-BACK[k]))
        return out

    one = jnp.ones_like(gram[0, 0])
    scaled = [one] + [None] * ITERS
    direction = list(scaled)
    surface = [None] * size
    rho = product(scaled, scaled)
    for turn in range(ITERS):
        image = operate(direction)
        step = rho / product(direction, image)
        for k in range(size):
            if direction[k] is not None:
                move = step * direction[k]
                surface[k] = move if surface[k] is None else surface[k] + move
            if image[k] is not None:
                move = step * image[k]
                scaled[k] = -move if scaled[k] is None else scaled[k] - move
        if turn == ITERS - 1:
            break
        rho_new = product(scaled, scaled)
        ratio = rho_new / rho
        direction = [
            s if d is None else s + ratio * d for s, d in zip(scaled, direction)
        ]
        rho = rho_new
    return surface[:ITERS], scaled


def kernel(
    lon_count, lat_count, rows,
    t_in, u_in, v_in, lev_in, forc_in, stor_in,
    new_out, surf_out, res_out,
    tr, ur, vr, li, fo, lv, st,
    beside_out, beside_w, beside_e, rows_out, rows_in,
    edge_out, edge_w, edge_e, edge_rows_out, edge_rows,
    flux, flux_sum, total, nt,
    w_e, w_n, w_ne, w_nw, w_er, w_ner, w_nwr, rdiag, diag, basis,
    surf, resid,
    in_sem, rows_send, rows_recv, beside_send, beside_recv, red_send, red_recv, out_sem, *boxes,
):
    lon, lat = lax.axis_index("lon"), lax.axis_index("lat")
    is_top = lat == lat_count - 1
    not_top = jnp.logical_not(is_top)
    not_bottom = lat > 0
    top = BASE + rows
    south = BASE - GHOST
    own = pl.ds(BASE, rows)
    inner = pl.ds(GHOST, rows)
    tile = (8, LANES)
    lane = lane_of(tile)
    row = row_of(tile)
    reach = rows + 2 * GHOST
    part = rows // PARTS

    def lanes(n):
        return lane_of((n, LANES))

    def row_is(r, n, which):
        return row_of((n, LANES)) + r == which

    east = lax.rem(lon + 1, lon_count)
    west = lax.rem(lon + lon_count - 1, lon_count)
    up_lat = jnp.where(is_top, lat, lat + 1)
    down_lat = jnp.maximum(lat - 1, 0)
    up_lon = jnp.where(is_top, lon_count - 1 - lon, lon)
    up_e = jnp.where(is_top, lax.rem(2 * lon_count - 2 - lon, lon_count), east)
    up_w = jnp.where(is_top, lax.rem(lon_count - lon, lon_count), west)
    self_e = jnp.logical_and(is_top, up_e == lon)
    self_w = jnp.logical_and(is_top, up_w == lon)
    other_e, other_w = jnp.logical_not(self_e), jnp.logical_not(self_w)

    extent = extents(lon_count, lat_count)
    here_at = {
        "core": lax.rem(lon, 2),
        "z": lax.rem(lon // 2, extent["z"]),
        "x": lon // (2 * extent["z"]),
        "y": lat,
    }

    def stage_peers(axes):
        place = 0
        for axis in axes:
            place = place * extent[axis] + here_at[axis]
        size = stage_size(extent, axes)
        peers = []
        for j in range(1, size):
            index = lax.rem(place + j, size)
            at = dict(here_at)
            rest = index
            for axis in reversed(axes):
                at[axis] = lax.rem(rest, extent[axis])
                rest = rest // extent[axis]
            device = {
                "lon": (at["x"] * extent["z"] + at["z"]) * 2 + at["core"], "lat": at["y"]}
            peers.append((index, device))
        return place, peers

    stages = [stage_peers(axes) for axes in STAGES]

    barrier = pltpu.get_barrier_semaphore()

    def greet(device):
        pl.semaphore_signal(barrier, inc=1, device_id=device, device_id_type=MESH)

    greet({"lon": east, "lat": lat})
    greet({"lon": west, "lat": lat})
    greet({"lon": up_lon, "lat": up_lat})

    @pl.when(other_e)
    def _():
        greet({"lon": up_e, "lat": up_lat})

    @pl.when(other_w)
    def _():
        greet({"lon": up_w, "lat": up_lat})

    @pl.when(not_bottom)
    def _():
        greet({"lon": lon, "lat": down_lat})
        greet({"lon": east, "lat": down_lat})
        greet({"lon": west, "lat": down_lat})

    loads = [
        local_copy("load", src, dst, in_sem.at[n]) for n, (src, dst) in enumerate((
            (lev_in, li), (stor_in, st.at[0, own, :]), (t_in, tr.at[:, inner, :]),
            (u_in, ur.at[:, inner, :]), (v_in, vr.at[:, inner, :]), (forc_in, fo),
        ))
    ]
    for load in loads:
        load.start()

    greeted = 3
    for _, peers in stages:
        for _, device in peers:
            greet(device)
        greeted += len(peers)
    greeted = greeted + jnp.where(self_e, 0, 1) + jnp.where(self_w, 0, 1) + jnp.where(not_bottom, 3, 0)

    nothing = jnp.zeros(tile, jnp.float32)
    for r in (south - 8, top + 8):
        at = pl.ds(r, 8)
        for half in range(2):
            for buffer in (lv, w_n, w_ne, w_nw):
                buffer[half, at, :] = nothing
            for k in range(ITERS + 1):
                basis[k, half, at, :] = nothing

    def fold(ranges):
        out = None
        for c, x in enumerate(ranges):
            moved = roll(x, EDGE + 16 * c)
            out = moved if out is None else jnp.where(lanes(part) // 16 == c, moved, out)
        return out

    def unfold(from_west, from_east):
        both = jnp.where(lanes(part) % 16 < EDGE, from_west, from_east)
        ends = jnp.logical_or(lanes(part) < EDGE, lanes(part) >= LANES - EDGE)
        return [
            jnp.where(ends, roll(both, -(EDGE + 16 * c)), 0.0) for c in range(PARTS)]

    def part_rows(c):
        return pl.ds(BASE + c * part, part)

    loads[0].wait()
    loads[1].wait()
    lv[0, own, :] = li[...].astype(jnp.float32)
    at_t, at_l, at_s = pl.ds(0, 2 * part), pl.ds(2 * part, part), pl.ds(3 * part, part)
    beside_out[at_l, :] = fold([lv[0, part_rows(c), :] for c in range(PARTS)])
    beside_out[at_s, :] = fold([st[0, part_rows(c), :] for c in range(PARTS)])
    edges = ((0, BASE, GHOST), (1, top - GHOST, GHOST + rows - 1))
    for side, r, _ in edges:
        rows_out[side, 0] = lv[0, pl.ds(r, GHOST), :]
        rows_out[side, 1] = st[0, pl.ds(r, GHOST), :]

    for load in loads[2:]:
        load.wait()

    def gather_ends(buffer, r, n):
        x = [buffer[k, pl.ds(r, n), :] for k in range(LEVELS)]
        lane = lanes(n)
        width = 2
        while len(x) > 1:
            window = jnp.logical_or(lane == 0, lane > LANES - width)
            x = [
                jnp.where(window, x[i + 1], roll(x[i], -width)) for i in range(0, len(x), 2)]
            width *= 2
        return x[0]

    def pack_ends(r, n, carry):
        out = None
        for c in range(PARTS // 2):
            for slot, buffer in enumerate((tr, ur)):
                moved = roll(gather_ends(buffer, GHOST + c * 2 * part + r, n), 32 * c + 16 * slot - 113)
                out = moved if out is None else jnp.where(
                    lanes(n) // 16 == 2 * c + slot, moved, out)
        beside_out[pl.ds(r, n), :] = out
        return carry

    sweep("ends", 0, 2 * part, part, pack_ends)
    for side, _, r in edges:
        for k in range(LEVELS):
            rows_out[side, 2, pl.ds(k, 1), :] = tr[k, pl.ds(r, 1), :]
            rows_out[side, 3, pl.ds(k, 1), :] = vr[k, pl.ds(r, 1), :]

    pl.semaphore_wait(barrier, greeted)

    def exchange(phase, beside_from, to_east, to_west, rows_from, rows_to, corners):
        def by_rows(slot, side, wide, place, to_lon, to_lat):
            src, dst = rows_from(side), rows_to.at[place]
            if not wide:
                src, dst = corners(src), corners(dst)
            return remote(
                "halo", src, dst, rows_send.at[phase, slot], rows_recv.at[phase, place],
                {"lon": to_lon, "lat": to_lat})

        go_e = remote(
            "halo", beside_from, to_east, beside_send.at[phase, 0], beside_recv.at[phase, 0],
            {"lon": east, "lat": lat})
        go_w = remote(
            "halo", beside_from, to_west, beside_send.at[phase, 1], beside_recv.at[phase, 1],
            {"lon": west, "lat": lat})
        go_up = by_rows(0, 1, True, jnp.where(is_top, 3, 0), up_lon, up_lat)
        go_up_e = by_rows(1, 1, False, jnp.where(is_top, 5, 1), up_e, up_lat)
        go_up_w = by_rows(2, 1, False, jnp.where(is_top, 4, 2), up_w, up_lat)
        go_down = by_rows(3, 0, True, 3, lon, down_lat)
        go_down_e = by_rows(4, 0, False, 4, east, down_lat)
        go_down_w = by_rows(5, 0, False, 5, west, down_lat)
        stay_e = local_copy(
            "halo", corners(rows_from(1)), corners(rows_to.at[5]), rows_recv.at[phase, 5])
        stay_w = local_copy(
            "halo", corners(rows_from(1)), corners(rows_to.at[4]), rows_recv.at[phase, 4])
        go_e.start()
        go_w.start()
        go_up.start()
        pl.when(other_e)(go_up_e.start)
        pl.when(other_w)(go_up_w.start)
        pl.when(self_e)(stay_e.start)
        pl.when(self_w)(stay_w.start)

        @pl.when(not_bottom)
        def _():
            go_down.start()
            go_down_e.start()
            go_down_w.start()

        def sent():
            go_e.wait_send()
            go_w.wait_send()
            go_up.wait_send()
            pl.when(other_e)(go_up_e.wait_send)
            pl.when(other_w)(go_up_w.wait_send)

            @pl.when(not_bottom)
            def _():
                go_down.wait_send()
                go_down_e.wait_send()
                go_down_w.wait_send()

        def received():
            arrived("halo", to_east, beside_recv.at[phase, 0])
            arrived("halo", to_west, beside_recv.at[phase, 1])
            arrived("halo", rows_to.at[3], rows_recv.at[phase, 3])
            arrived("halo", corners(rows_to.at[4]), rows_recv.at[phase, 4])
            arrived("halo", corners(rows_to.at[5]), rows_recv.at[phase, 5])

            @pl.when(not_bottom)
            def _():
                arrived("halo", rows_to.at[0], rows_recv.at[phase, 0])
                arrived("halo", corners(rows_to.at[1]), rows_recv.at[phase, 1])
                arrived("halo", corners(rows_to.at[2]), rows_recv.at[phase, 2])

        return sent, received

    first_sent, first_received = exchange(
        0, beside_out, beside_w, beside_e, lambda side: rows_out.at[side], rows_in,
        lambda ref: ref.at[pl.ds(0, 2)])

    def tracer_rows(r, n, carry):
        at, up, down = pl.ds(r, n), pl.ds(r + 1, n), pl.ds(r - 1, n)
        wide, wide_up, wide_down = (pl.ds(r + GHOST + d, n) for d in (0, 1, -1))
        depth = lv[0, wide, :]
        open_e = jnp.where(
            lanes(n) == LANES - 1, 0.0, jnp.minimum(depth, roll(depth, -1)))
        open_n = jnp.where(
            row_is(r, n, GHOST + rows - 1), 0.0, jnp.minimum(depth, lv[0, wide_up, :]))
        open_s = jnp.where(
            row_is(r, n, GHOST), 0.0, jnp.minimum(depth, lv[0, wide_down, :]))
        below = None
        summed = None
        here = tr[0, at, :]
        for k in range(LEVELS):
            vel = vr[k, at, :]
            zonal = ur[k, at, :]
            flux_e = face_flux(here, roll(here, -1), zonal, roll(zonal, -1), open_e, k)
            flux_n = face_flux(here, tr[k, up, :], vel, vr[k, up, :], open_n, k)
            flux_s = face_flux(tr[k, down, :], here, vr[k, down, :], vel, open_s, k)
            change = 0.0625 * ((flux_e - roll(flux_e, 1)) + (flux_n - flux_s))
            result = here + change
            if below is not None:
                result = result - below
            if k + 1 < LEVELS:
                above = tr[k + 1, at, :]
                below = jnp.where(depth > k + 1, 0.1 * (above - here), 0.0)
                result = result + below
                here = above
            nt[k, pl.ds(r - GHOST, n), :] = result
            wet_part = jnp.where(depth > k, result, 0.0)
            summed = wet_part if summed is None else summed + wet_part
        total[pl.ds(r - GHOST, n), :] = summed
        return carry

    sweep("tracer", GHOST, rows, TRACER_STEP, tracer_rows)

    first_received()

    def clear(buffer):
        for place in range(3):
            buffer[place] = jnp.zeros(buffer.shape[1:], buffer.dtype)

    pl.when(jnp.logical_not(not_bottom))(lambda: clear(rows_in))

    def swap(x, bit, axis):
        size = x.shape[axis]
        index = lax.broadcasted_iota(jnp.int32, x.shape, axis)
        low = (index // bit) % 2 == 0
        return jnp.where(low, pltpu.roll(x, size - bit, axis), pltpu.roll(x, bit, axis))

    def mirror_lanes(x):
        for bit in (1, 2, 4, 8, 16, 32, 64):
            x = swap(x, bit, 1)
        return x

    def mirror(x):
        x = mirror_lanes(x)
        for bit in (1, 2, 4):
            x = swap(x, bit, 0)
        return x

    @pl.when(is_top)
    def _():
        for place in (3, 4, 5):
            for field in range(2):
                rows_in[place, field] = mirror(rows_in[place, field])
        rows_in[3, 2] = mirror_lanes(rows_in[3, 2])

    level_row = row.astype(jnp.float32)
    carry_north = jnp.where(is_top, 0.0, 1.0)
    own_first, own_last = rows_out[0], rows_out[1]
    shared_n = jnp.minimum(own_last[0][7:8], rows_in[3, 0][0:1])
    flux_n = jnp.where(
        shared_n > level_row,
        0.0625 * (1.92 * (rows_in[3, 2] - own_last[2])
                  - carry_north * (own_last[3] + rows_in[3, 3]) * (own_last[2] + rows_in[3, 2])),
        0.0)
    shared_s = jnp.minimum(own_first[0][0:1], rows_in[0, 0][7:8])
    flux_s = jnp.where(
        shared_s > level_row,
        0.0625 * (1.92 * (own_first[2] - rows_in[0, 2])
                  - (own_first[3] + rows_in[0, 3]) * (own_first[2] + rows_in[0, 2])),
        0.0)
    first_own, last_own = pl.ds(0, 8), pl.ds(rows - 8, 8)
    for k in range(LEVELS):
        nt[k, last_own, :] = nt[k, last_own, :] + jnp.where(row == 7, flux_n[k:k + 1], 0.0)
        nt[k, first_own, :] = nt[k, first_own, :] - jnp.where(row == 0, flux_s[k:k + 1], 0.0)
    total[last_own, :] = total[last_own, :] + jnp.where(
        row == 7, jnp.sum(flux_n, axis=0, keepdims=True), 0.0)
    total[first_own, :] = total[first_own, :] - jnp.where(
        row == 0, jnp.sum(flux_s, axis=0, keepdims=True), 0.0)

    depths = [buffer[at_l, :] for buffer in (beside_out, beside_w, beside_e)]
    for half in range(2):
        at = pl.ds(half * part, part)
        lane_p = lanes(part)
        even = lane_p % 2 == 0
        mine, from_w, from_e = beside_out[at, :], beside_w[at, :], beside_e[at, :]
        here = jnp.where(even, mine, roll(from_w, 1))
        there = jnp.where(even, roll(from_e, -1), mine)
        carried = roll(here + there, -16) * (here + there)
        d_mine, d_w, d_e = depths
        shared = jnp.where(
            lane_p % 16 == 7, jnp.minimum(d_mine, roll(d_e, -1)),
            jnp.where(lane_p % 16 == 8, jnp.minimum(roll(d_w, 1), d_mine), 0.0))
        shared = jnp.where((lane_p // 16) % 2 == half, shared, 0.0)
        shared = roll(shared, -7 - 16 * half)
        for shift in (2, 4, 8):
            shared = shared + roll(shared, shift)
        level = ((lane_p % 16) // 2).astype(jnp.float32)
        through = jnp.where(
            jnp.logical_and(shared > level, lane_p % 32 < 16),
            0.0625 * (1.92 * (there - here) - carried), 0.0)
        through = jnp.where(even, through, -through)
        flux[at, :] = through
        for shift in (2, 4, 8):
            through = through + roll(through, -shift)
        flux_sum[at, :] = through

    def right_side(c):
        at = pl.ds(c * part, part)
        lane_p = lanes(part)
        ends = jnp.logical_or(lane_p == 0, lane_p == LANES - 1)
        across = roll(flux_sum[pl.ds((c % 2) * part, part), :], 127 - 32 * (c // 2))
        summed = total[at, :] + jnp.where(ends, across, 0.0)
        value = jnp.where(lv[0, part_rows(c), :] > 0.0, fo[at, :], 0.0) + summed * 8.0 ** -0.5
        basis[0, 0, part_rows(c), :] = value
        return value

    edge_out[...] = fold([right_side(c) for c in range(PARTS)])
    for side, r, _ in edges:
        edge_rows_out[side] = basis[0, 0, pl.ds(r, GHOST), :]
    second_sent, second_received = exchange(
        1, edge_out, edge_w, edge_e, lambda side: edge_rows_out.at[side], edge_rows,
        lambda ref: ref)

    def place_rows(buffer, get):
        for r, across, w_at, e_at in ((south, 0, 1, 2), (top, 3, 4, 5)):
            at = pl.ds(r, GHOST)
            buffer[0, at, :] = get(across)
            buffer[1, at, :] = jnp.where(
                lane < EDGE, get(e_at), jnp.where(lane >= LANES - EDGE, get(w_at), 0.0))

    for buffer, at, field in ((lv, at_l, 0), (st, at_s, 1)):
        for c, x in enumerate(unfold(beside_w[at, :], beside_e[at, :])):
            buffer[1, part_rows(c), :] = x
        place_rows(buffer, lambda place, field=field: rows_in[place, field])

    fold_row = jnp.where(is_top, top - 1, -1)

    def weigh(a, b):
        return a * b / (a + b + 1.0)

    def weights_rows(r, n, carry):
        at, up = pl.ds(r, n), pl.ds(r + 1, n)
        lane = lanes(n)
        d_m, d_s = lv[0, at, :], lv[1, at, :]
        n_m, n_s = lv[0, up, :], lv[1, up, :]
        e_m, e_s = ring_east(d_m, d_s, lane)
        ne_m, ne_s = ring_east(n_m, n_s, lane)
        nw_m, nw_s = ring_west(n_m, n_s, lane)
        corner = jnp.where(row_is(r, n, fold_row), 0.0, 0.25)
        east_m, east_s = weigh(d_m, e_m), weigh(d_s, e_s)
        neast_m, neast_s = corner * weigh(d_m, ne_m), corner * weigh(d_s, ne_s)
        nwest_m, nwest_s = corner * weigh(d_m, nw_m), corner * weigh(d_s, nw_s)
        w_e[0, at, :], w_e[1, at, :] = east_m, east_s
        w_n[0, at, :], w_n[1, at, :] = weigh(d_m, n_m), weigh(d_s, n_s)
        w_ne[0, at, :], w_ne[1, at, :] = neast_m, neast_s
        w_nw[0, at, :], w_nw[1, at, :] = nwest_m, nwest_s
        w_er[0, at, :], w_er[1, at, :] = ring_west(east_m, east_s, lane)
        w_ner[0, at, :], w_ner[1, at, :] = ring_west(neast_m, neast_s, lane)
        w_nwr[0, at, :], w_nwr[1, at, :] = ring_east(nwest_m, nwest_s, lane)
        return carry

    sweep("weights", south, reach, WEIGHTS_STEP, weights_rows)

    def diagonal_rows(r, n, carry):
        at, down = pl.ds(r, n), pl.ds(r - 1, n)
        for half in range(2):
            whole = (
                st[half, at, :] + w_e[half, at, :] + w_er[half, at, :] + w_n[half, at, :]
                + w_n[half, down, :] + w_ne[half, at, :] + w_nw[half, at, :]
                + w_ner[half, down, :] + w_nwr[half, down, :])
            rdiag[half, at, :] = jnp.where(whole > 0.0, 1.0 / whole, 0.0)
            if half == 0:
                diag[at, :] = whole
        return carry

    sweep("diagonal", south, reach, DIAGONAL_STEP, diagonal_rows)
    diag[pl.ds(south, GHOST), :] = nothing
    diag[pl.ds(top, GHOST), :] = nothing

    def ends_rows(r, n, carry):
        lane = lanes(n)
        ends = jnp.logical_or(lane == 0, lane == LANES - 1)
        across = flux[pl.ds(r, n), :]
        for c in range(PARTS // 2):
            at = pl.ds(c * 2 * part + r, n)
            for k in range(LEVELS):
                nt[k, at, :] = nt[k, at, :] + jnp.where(
                    ends, roll(across, 127 - 32 * c - 2 * k), 0.0)
        return carry

    sweep("new", 0, 2 * part, part, ends_rows)
    out_new = local_copy("out", nt, new_out, out_sem.at[0])
    out_new.start()

    second_received()
    pl.when(jnp.logical_not(not_bottom))(lambda: clear(edge_rows))

    @pl.when(is_top)
    def _():
        for place in (3, 4, 5):
            edge_rows[place] = mirror(edge_rows[place])

    for c, x in enumerate(unfold(edge_w[...], edge_e[...])):
        basis[0, 1, part_rows(c), :] = x
    place_rows(basis.at[0], lambda place: edge_rows[place])

    gram = {}

    def fold_rows(x):
        return jnp.sum(x.reshape(x.shape[0] // 8, 8, LANES), axis=0)

    def scaled_rows(r, n, acc):
        at = pl.ds(r, n)
        for half in range(2):
            x = basis[0, half, at, :]
            y = x * rdiag[half, at, :]
            basis[0, half, at, :] = y
            if half == 0:
                acc = acc + fold_rows(diag[at, :] * y * y)
        return acc

    gram[0, 0] = sweep("scaled", south, reach, SCALED_STEP, scaled_rows, nothing)

    def neighbours_sum(k, r, n, halves):
        at, up, down = pl.ds(r, n), pl.ds(r + 1, n), pl.ds(r - 1, n)
        lane = lanes(n)
        sums, to_west, to_east = [], [], []
        for half in range(2):
            x = basis[k, half, at, :]
            x_n = basis[k, half, up, :]
            x_s = basis[k, half, down, :]
            to_east.append(
                w_e[half, at, :] * x + w_ne[half, down, :] * x_s + w_nwr[half, at, :] * x_n)
            to_west.append(
                w_er[half, at, :] * x + w_nw[half, down, :] * x_s + w_ner[half, at, :] * x_n)
            if half < halves:
                sums.append(w_n[half, at, :] * x_n + w_n[half, down, :] * x_s)
        from_west = ring_west(to_east[0], to_east[1], lane)
        from_east = ring_east(to_west[0], to_west[1], lane)
        return [sums[h] + from_west[h] + from_east[h] for h in range(halves)]

    def apply_rows(k, r, n, halves):
        at = pl.ds(r, n)
        sums = neighbours_sum(k, r, n, halves)
        out = []
        for half in range(halves):
            x = basis[k, half, at, :]
            y = rdiag[half, at, :] * sums[half]
            if SHIFT[k] != 0.0:
                y = y - SHIFT[k] * x
            if BACK[k] != 0.0:
                y = y - BACK[k] * basis[k - 1, half, at, :]
            y = GAIN[k] * y
            basis[k + 1, half, at, :] = y
            out.append(y)
        return out[0]

    for k in range(ITERS):
        last = k == ITERS - 1
        terms = [p for p in PAIRS if p[1] == k + 1]

        def apply_own(r, n, accs, k=k, terms=terms, halves=1 if last else 2):
            at = pl.ds(r, n)
            y = apply_rows(k, r, n, halves)
            scaled = diag[at, :] * y
            return tuple(
                acc + fold_rows(scaled * (y if a == k + 1 else basis[a, 0, at, :]))
                for acc, (a, _) in zip(accs, terms))

        sums = sweep(
            "apply", BASE if last else south, rows if last else reach,
            LAST_STEP if last else APPLY_STEP, apply_own, tuple(nothing for _ in terms))
        for p, s in zip(terms, sums):
            gram[p] = s

    per_lane = [jnp.sum(gram[p], axis=0, keepdims=True) for p in PAIRS]
    per_lane = per_lane + [jnp.zeros((1, LANES), jnp.float32)] * (24 - len(per_lane))
    stacked = jnp.sum(jnp.concatenate(per_lane, axis=0), axis=1, keepdims=True)
    count = stacked.shape[0]
    own_lane = lane_of((count, LANES)) == row_of((count, LANES))
    summed = jnp.sum(jnp.where(own_lane, stacked, 0.0), axis=0, keepdims=True)

    sends = []
    for stage, (place, peers) in enumerate(stages):
        box = boxes[stage]
        box[pl.ds(place, 1), :, :] = summed[None]
        for n, (_, device) in enumerate(peers):
            copy = remote(
                "red", box.at[place], box.at[place],
                red_send.at[stage, n], red_recv.at[stage, place], device)
            copy.start()
            sends.append(copy)
        for index, _ in peers:
            arrived("red", box.at[index], red_recv.at[stage, index])
        summed = box[0]
        for n in range(1, len(peers) + 1):
            summed = summed + box[n]

    spread = jnp.sum(
        jnp.where(own_lane, jnp.broadcast_to(summed, (count, LANES)), 0.0),
        axis=1, keepdims=True)
    sums = {
        p: jnp.broadcast_to(spread[n:n + 1], tile) for n, p in enumerate(PAIRS)
    }
    surface_by, scaled_by = solve(sums)

    surface_by = [c[0:1] for c in surface_by]
    scaled_by = [c[0:1] for c in scaled_by]

    def final_rows(r, n, carry):
        at = pl.ds(r, n)
        to = pl.ds(pl.multiple_of(r - BASE, 8), n)
        x = [basis[k, 0, at, :] for k in range(ITERS + 1)]
        level_at = surface_by[0] * x[0]
        left = scaled_by[0] * x[0]
        for k in range(1, ITERS + 1):
            if k < ITERS:
                level_at = level_at + surface_by[k] * x[k]
            left = left + scaled_by[k] * x[k]
        surf[to, :] = level_at
        resid[to, :] = diag[at, :] * left
        return carry

    sweep("final", BASE, rows, FINAL_STEP, final_rows)
    out_surf = local_copy("out", surf, surf_out, out_sem.at[1])
    out_res = local_copy("out", resid, res_out, out_sem.at[2])
    out_surf.start()
    out_res.start()

    first_sent()
    second_sent()
    for copy in sends:
        copy.wait_send()
    out_new.wait()
    out_surf.wait()
    out_res.wait()


def local(lon_count, lat_count, tracer, east_vel, north_vel, levels, forcing, storage):
    rows = tracer.shape[1]
    flat = (rows + 4 * GHOST, LANES)
    part = rows // PARTS
    f32 = jnp.float32
    extent = extents(lon_count, lat_count)
    sizes = [stage_size(extent, axes) for axes in STAGES]

    def vmem(*shape, dtype=f32):
        return pltpu.VMEM(shape, dtype)

    cube = vmem(LEVELS, rows + 2 * GHOST, LANES)
    pair = vmem(2, *flat)
    block = vmem(rows, LANES)
    beside = vmem(4 * part, LANES)
    edge = vmem(part, LANES)
    dma = pltpu.SemaphoreType.DMA
    anywhere = pl.BlockSpec(memory_space=pl.ANY)
    outs = (
        jax.ShapeDtypeStruct(tracer.shape, f32),
        jax.ShapeDtypeStruct(levels.shape, f32),
        jax.ShapeDtypeStruct(levels.shape, f32),
    )
    return pl.pallas_call(
        functools.partial(kernel, lon_count, lat_count, rows),
        out_shape=outs,
        in_specs=[anywhere] * 6,
        out_specs=(anywhere,) * 3,
        scratch_shapes=[
            cube, cube, cube, vmem(rows, LANES, dtype=jnp.int32), block, pair, pair,
            beside, beside, beside, vmem(2, 4, 8, LANES), vmem(6, 4, 8, LANES),
            edge, edge, edge, vmem(2, 8, LANES), vmem(6, 8, LANES),
            vmem(2 * part, LANES), vmem(2 * part, LANES), block, vmem(LEVELS, rows, LANES),
            pair, pair, pair, pair, pair, pair, pair, pair, vmem(*flat),
            vmem(ITERS + 1, 2, *flat),
            block, block,
            dma((6,)), dma((2, 6)), dma((2, 6)), dma((2, 2)), dma((2, 2)),
            dma((len(sizes), max(sizes))), dma((len(sizes), max(sizes))), dma((3,)),
            *[vmem(size, 1, LANES) for size in sizes],
        ],
        compiler_params=pltpu.CompilerParams(
            collective_id=0, has_side_effects=True, vmem_limit_bytes=61 * 2**20
        ),
        cost_estimate=pl.CostEstimate(flops=10**8, bytes_accessed=6 * 10**6, transcendentals=0),
        name="ocean_step",
    )(tracer, east_vel, north_vel, levels, forcing, storage)


def solution(mesh):
    cube, flat = P(None, "lat", "lon"), P("lat", "lon")
    return jax.shard_map(
        functools.partial(local, mesh.shape["lon"], mesh.shape["lat"]),
        mesh=mesh,
        in_specs=(cube, cube, cube, flat, flat, flat),
        out_specs=(cube, flat, flat),
        check_vma=False,
    )
```

```python
import functools
import itertools

import jax
import jax.numpy as jnp
from jax import lax
from jax.experimental import pallas as pl
from jax.experimental.pallas import tpu as pltpu
from jax.sharding import PartitionSpec as P

ITERS = 5
LEVELS = 8
GHOST = 8
BASE = 2 * GHOST
LANES = 128
EDGE = 8
PARTS = 8
SCALE = 0.8
MESH = pl.DeviceIdType.MESH
STAGES = (("core", "y"), ("x", "z"))
TRACER_STEP = 16
WEIGHTS_STEP = 112
DIAGONAL_STEP = 48
SCALED_STEP = 112
APPLY_STEP = 112
LAST_STEP = 160
FINAL_STEP = 80

GAIN = (-1.0, 1.0 / SCALE, 2.0 / SCALE, 2.0 / SCALE, 2.0 / SCALE)
SHIFT = (1.0, 0.0, 0.0, 0.0, 0.0)
BACK = (0.0, 0.0, SCALE / 2, SCALE / 2, SCALE / 2)
PAIRS = tuple((i, j) for j in range(ITERS + 1) for i in range(j + 1) if (i, j) != (ITERS, ITERS))


def roll(x, shift):
    return pltpu.roll(x, shift % x.shape[-1], x.ndim - 1)


def lane_of(shape):
    return lax.broadcasted_iota(jnp.int32, shape, len(shape) - 1)


def row_of(shape):
    return lax.broadcasted_iota(jnp.int32, shape, len(shape) - 2)


def extents(lon_count, lat_count):
    z = min(4, lon_count // 2)
    return {"core": 2, "z": z, "x": lon_count // (2 * z), "y": lat_count}


def stage_size(extent, axes):
    size = 1
    for axis in axes:
        size *= extent[axis]
    return size


def sweep(name, first, rows, step, body, start=0):
    whole = rows // step

    def chunk(i, carry):
        return body(pl.multiple_of(first + i * step, 8), step, carry)

    carry = lax.fori_loop(0, whole, chunk, start) if whole else start
    if rows % step:
        carry = body(first + whole * step, rows % step, carry)
    return carry


def remote(name, src, dst, sent, received, device):
    return pltpu.make_async_remote_copy(
        src, dst, sent, received, device_id=device, device_id_type=MESH)


def local_copy(name, src, dst, done):
    return pltpu.make_async_copy(src, dst, done)


def step(name, run):
    run()


def arrived(name, part, received):
    pltpu.make_async_copy(part, part, received).wait()


def face_flux(here, there, vel_here, vel_there, shared, level):
    carried = (vel_here + vel_there) * (here + there)
    return jnp.where(shared > level, 1.92 * (there - here) - carried, 0.0)


def ring_east(main, strip, lane):
    a, b = roll(main, -1), roll(strip, -1)
    last = lane == LANES - 1
    return jnp.where(last, b, a), jnp.where(last, a, b)


def ring_west(main, strip, lane):
    a, b = roll(main, 1), roll(strip, 1)
    first = lane == 0
    return jnp.where(first, b, a), jnp.where(first, a, b)


def solve(gram):
    size = ITERS + 1

    def product(left, right):
        total = None
        for i, a in enumerate(left):
            if a is None:
                continue
            inner = None
            for j, b in enumerate(right):
                if b is None:
                    continue
                term = gram[min(i, j), max(i, j)] * b
                inner = term if inner is None else inner + term
            total = a * inner if total is None else total + a * inner
        return total

    def operate(coeffs):
        out = [None] * size

        def add(k, value):
            out[k] = value if out[k] is None else out[k] + value

        for k in range(ITERS):
            if coeffs[k] is None:
                continue
            add(k + 1, coeffs[k] * (-1.0 / GAIN[k]))
            if SHIFT[k] != 1.0:
                add(k, coeffs[k] * (1.0 - SHIFT[k]))
            if BACK[k] != 0.0:
                add(k - 1, coeffs[k] * (-BACK[k]))
        return out

    one = jnp.ones_like(gram[0, 0])
    scaled = [one] + [None] * ITERS
    direction = list(scaled)
    surface = [None] * size
    rho = product(scaled, scaled)
    for turn in range(ITERS):
        image = operate(direction)
        step = rho / product(direction, image)
        for k in range(size):
            if direction[k] is not None:
                move = step * direction[k]
                surface[k] = move if surface[k] is None else surface[k] + move
            if image[k] is not None:
                move = step * image[k]
                scaled[k] = -move if scaled[k] is None else scaled[k] - move
        if turn == ITERS - 1:
            break
        rho_new = product(scaled, scaled)
        ratio = rho_new / rho
        direction = [
            s if d is None else s + ratio * d for s, d in zip(scaled, direction)
        ]
        rho = rho_new
    return surface[:ITERS], scaled


def kernel(
    lon_count, lat_count, rows,
    t_in, u_in, v_in, lev_in, forc_in, stor_in,
    new_out, surf_out, res_out,
    tr, ur, vr, li, fo, lv, st,
    beside_out, beside_w, beside_e, rows_out, rows_in,
    edge_out, edge_w, edge_e, edge_rows_out, edge_rows,
    flux, flux_sum, total, nt,
    w_e, w_n, w_ne, w_nw, w_er, w_ner, w_nwr, rdiag, diag, basis,
    surf, resid,
    in_sem, rows_send, rows_recv, beside_send, beside_recv, red_send, red_recv, out_sem, *boxes,
):
    lon, lat = lax.axis_index("lon"), lax.axis_index("lat")
    is_top = lat == lat_count - 1
    not_top = jnp.logical_not(is_top)
    not_bottom = lat > 0
    top = BASE + rows
    south = BASE - GHOST
    own = pl.ds(BASE, rows)
    inner = pl.ds(GHOST, rows)
    tile = (8, LANES)
    lane = lane_of(tile)
    row = row_of(tile)
    reach = rows + 2 * GHOST
    part = rows // PARTS

    def lanes(n):
        return lane_of((n, LANES))

    def row_is(r, n, which):
        return row_of((n, LANES)) + r == which

    east = lax.rem(lon + 1, lon_count)
    west = lax.rem(lon + lon_count - 1, lon_count)
    up_lat = jnp.where(is_top, lat, lat + 1)
    down_lat = jnp.maximum(lat - 1, 0)
    up_lon = jnp.where(is_top, lon_count - 1 - lon, lon)
    up_e = jnp.where(is_top, lax.rem(2 * lon_count - 2 - lon, lon_count), east)
    up_w = jnp.where(is_top, lax.rem(lon_count - lon, lon_count), west)
    self_e = jnp.logical_and(is_top, up_e == lon)
    self_w = jnp.logical_and(is_top, up_w == lon)
    other_e, other_w = jnp.logical_not(self_e), jnp.logical_not(self_w)

    extent = extents(lon_count, lat_count)
    here_at = {
        "core": lax.rem(lon, 2),
        "z": lax.rem(lon // 2, extent["z"]),
        "x": lon // (2 * extent["z"]),
        "y": lat,
    }

    def stage_peers(axes):
        def index_of(at):
            index = 0
            for axis in axes:
                index = index * extent[axis] + at[axis]
            return index

        moves = sorted(
            itertools.product(*(range(extent[axis]) for axis in axes)),
            key=lambda move: -sum(min(d, extent[a] - d) for d, a in zip(move, axes)))
        peers = []
        for move in moves[:-1]:
            at = dict(here_at)
            for axis, d in zip(axes, move):
                at[axis] = lax.rem(here_at[axis] + d, extent[axis])
            device = {
                "lon": (at["x"] * extent["z"] + at["z"]) * 2 + at["core"], "lat": at["y"]}
            peers.append((index_of(at), device))
        place = index_of(here_at)
        return place, peers

    stages = [stage_peers(axes) for axes in STAGES]

    barrier = pltpu.get_barrier_semaphore()

    def greet(device):
        pl.semaphore_signal(barrier, inc=1, device_id=device, device_id_type=MESH)

    greet({"lon": east, "lat": lat})
    greet({"lon": west, "lat": lat})
    greet({"lon": up_lon, "lat": up_lat})

    @pl.when(other_e)
    def _():
        greet({"lon": up_e, "lat": up_lat})

    @pl.when(other_w)
    def _():
        greet({"lon": up_w, "lat": up_lat})

    @pl.when(not_bottom)
    def _():
        greet({"lon": lon, "lat": down_lat})
        greet({"lon": east, "lat": down_lat})
        greet({"lon": west, "lat": down_lat})

    loads = [
        local_copy("load", src, dst, in_sem.at[n]) for n, (src, dst) in enumerate((
            (lev_in, li), (stor_in, st.at[0, own, :]), (t_in, tr.at[:, inner, :]),
            (u_in, ur.at[:, inner, :]), (v_in, vr.at[:, inner, :]), (forc_in, fo),
        ))
    ]
    for load in loads:
        load.start()

    greeted = 3
    for _, peers in stages:
        for _, device in peers:
            greet(device)
        greeted += len(peers)
    greeted = greeted + jnp.where(self_e, 0, 1) + jnp.where(self_w, 0, 1) + jnp.where(not_bottom, 3, 0)

    nothing = jnp.zeros(tile, jnp.float32)
    for r in (south - 8, top + 8):
        at = pl.ds(r, 8)
        for half in range(2):
            for buffer in (lv, w_n, w_ne, w_nw):
                buffer[half, at, :] = nothing
            for k in range(ITERS + 1):
                basis[k, half, at, :] = nothing

    def fold(ranges):
        out = None
        for c, x in enumerate(ranges):
            moved = roll(x, EDGE + 16 * c)
            out = moved if out is None else jnp.where(lanes(part) // 16 == c, moved, out)
        return out

    def unfold(from_west, from_east):
        both = jnp.where(lanes(part) % 16 < EDGE, from_west, from_east)
        ends = jnp.logical_or(lanes(part) < EDGE, lanes(part) >= LANES - EDGE)
        return [
            jnp.where(ends, roll(both, -(EDGE + 16 * c)), 0.0) for c in range(PARTS)]

    def part_rows(c):
        return pl.ds(BASE + c * part, part)

    loads[0].wait()
    loads[1].wait()
    lv[0, own, :] = li[...].astype(jnp.float32)
    at_t, at_l, at_s = pl.ds(0, 2 * part), pl.ds(2 * part, part), pl.ds(3 * part, part)
    beside_out[at_l, :] = fold([lv[0, part_rows(c), :] for c in range(PARTS)])
    beside_out[at_s, :] = fold([st[0, part_rows(c), :] for c in range(PARTS)])
    edges = ((0, BASE, GHOST), (1, top - GHOST, GHOST + rows - 1))
    for side, r, _ in edges:
        rows_out[side, 0] = lv[0, pl.ds(r, GHOST), :]
        rows_out[side, 1] = st[0, pl.ds(r, GHOST), :]

    for load in loads[2:]:
        load.wait()

    def gather_ends(buffer, r, n):
        x = [buffer[k, pl.ds(r, n), :] for k in range(LEVELS)]
        lane = lanes(n)
        width = 2
        while len(x) > 1:
            window = jnp.logical_or(lane == 0, lane > LANES - width)
            x = [
                jnp.where(window, x[i + 1], roll(x[i], -width)) for i in range(0, len(x), 2)]
            width *= 2
        return x[0]

    def pack_ends(r, n, carry):
        out = None
        for c in range(PARTS // 2):
            for slot, buffer in enumerate((tr, ur)):
                moved = roll(gather_ends(buffer, GHOST + c * 2 * part + r, n), 32 * c + 16 * slot - 113)
                out = moved if out is None else jnp.where(
                    lanes(n) // 16 == 2 * c + slot, moved, out)
        beside_out[pl.ds(r, n), :] = out
        return carry

    sweep("ends", 0, 2 * part, part, pack_ends)
    for side, _, r in edges:
        for k in range(LEVELS):
            rows_out[side, 2, pl.ds(k, 1), :] = tr[k, pl.ds(r, 1), :]
            rows_out[side, 3, pl.ds(k, 1), :] = vr[k, pl.ds(r, 1), :]

    pl.semaphore_wait(barrier, greeted)

    def exchange(phase, beside_from, to_east, to_west, rows_from, rows_to, corners):
        def by_rows(slot, side, wide, place, to_lon, to_lat):
            src, dst = rows_from(side), rows_to.at[place]
            if not wide:
                src, dst = corners(src), corners(dst)
            return remote(
                "halo", src, dst, rows_send.at[phase, slot], rows_recv.at[phase, place],
                {"lon": to_lon, "lat": to_lat})

        go_e = remote(
            "halo", beside_from, to_east, beside_send.at[phase, 0], beside_recv.at[phase, 0],
            {"lon": east, "lat": lat})
        go_w = remote(
            "halo", beside_from, to_west, beside_send.at[phase, 1], beside_recv.at[phase, 1],
            {"lon": west, "lat": lat})
        go_up = by_rows(0, 1, True, jnp.where(is_top, 3, 0), up_lon, up_lat)
        go_up_e = by_rows(1, 1, False, jnp.where(is_top, 5, 1), up_e, up_lat)
        go_up_w = by_rows(2, 1, False, jnp.where(is_top, 4, 2), up_w, up_lat)
        go_down = by_rows(3, 0, True, 3, lon, down_lat)
        go_down_e = by_rows(4, 0, False, 4, east, down_lat)
        go_down_w = by_rows(5, 0, False, 5, west, down_lat)
        stay_e = local_copy(
            "halo", corners(rows_from(1)), corners(rows_to.at[5]), rows_recv.at[phase, 5])
        stay_w = local_copy(
            "halo", corners(rows_from(1)), corners(rows_to.at[4]), rows_recv.at[phase, 4])
        go_e.start()
        go_w.start()
        go_up.start()
        pl.when(other_e)(go_up_e.start)
        pl.when(other_w)(go_up_w.start)
        pl.when(self_e)(stay_e.start)
        pl.when(self_w)(stay_w.start)

        @pl.when(not_bottom)
        def _():
            go_down.start()
            go_down_e.start()
            go_down_w.start()

        def sent():
            go_e.wait_send()
            go_w.wait_send()
            go_up.wait_send()
            pl.when(other_e)(go_up_e.wait_send)
            pl.when(other_w)(go_up_w.wait_send)

            @pl.when(not_bottom)
            def _():
                go_down.wait_send()
                go_down_e.wait_send()
                go_down_w.wait_send()

        def received():
            arrived("halo", to_east, beside_recv.at[phase, 0])
            arrived("halo", to_west, beside_recv.at[phase, 1])
            arrived("halo", rows_to.at[3], rows_recv.at[phase, 3])
            arrived("halo", corners(rows_to.at[4]), rows_recv.at[phase, 4])
            arrived("halo", corners(rows_to.at[5]), rows_recv.at[phase, 5])

            @pl.when(not_bottom)
            def _():
                arrived("halo", rows_to.at[0], rows_recv.at[phase, 0])
                arrived("halo", corners(rows_to.at[1]), rows_recv.at[phase, 1])
                arrived("halo", corners(rows_to.at[2]), rows_recv.at[phase, 2])

        return sent, received

    first_sent, first_received = exchange(
        0, beside_out, beside_w, beside_e, lambda side: rows_out.at[side], rows_in,
        lambda ref: ref.at[pl.ds(0, 2)])

    def tracer_rows(r, n, carry):
        at, up, down = pl.ds(r, n), pl.ds(r + 1, n), pl.ds(r - 1, n)
        wide, wide_up, wide_down = (pl.ds(r + GHOST + d, n) for d in (0, 1, -1))
        depth = lv[0, wide, :]
        open_e = jnp.where(
            lanes(n) == LANES - 1, 0.0, jnp.minimum(depth, roll(depth, -1)))
        open_n = jnp.where(
            row_is(r, n, GHOST + rows - 1), 0.0, jnp.minimum(depth, lv[0, wide_up, :]))
        open_s = jnp.where(
            row_is(r, n, GHOST), 0.0, jnp.minimum(depth, lv[0, wide_down, :]))
        below = None
        summed = None
        here = tr[0, at, :]
        for k in range(LEVELS):
            vel = vr[k, at, :]
            zonal = ur[k, at, :]
            flux_e = face_flux(here, roll(here, -1), zonal, roll(zonal, -1), open_e, k)
            flux_n = face_flux(here, tr[k, up, :], vel, vr[k, up, :], open_n, k)
            flux_s = face_flux(tr[k, down, :], here, vr[k, down, :], vel, open_s, k)
            change = 0.0625 * ((flux_e - roll(flux_e, 1)) + (flux_n - flux_s))
            result = here + change
            if below is not None:
                result = result - below
            if k + 1 < LEVELS:
                above = tr[k + 1, at, :]
                below = jnp.where(depth > k + 1, 0.1 * (above - here), 0.0)
                result = result + below
                here = above
            nt[k, pl.ds(r - GHOST, n), :] = result
            wet_part = jnp.where(depth > k, result, 0.0)
            summed = wet_part if summed is None else summed + wet_part
        total[pl.ds(r - GHOST, n), :] = summed
        return carry

    sweep("tracer", GHOST, rows, TRACER_STEP, tracer_rows)

    first_received()

    def clear(buffer):
        for place in range(3):
            buffer[place] = jnp.zeros(buffer.shape[1:], buffer.dtype)

    pl.when(jnp.logical_not(not_bottom))(lambda: clear(rows_in))

    def swap(x, bit, axis):
        size = x.shape[axis]
        index = lax.broadcasted_iota(jnp.int32, x.shape, axis)
        low = (index // bit) % 2 == 0
        return jnp.where(low, pltpu.roll(x, size - bit, axis), pltpu.roll(x, bit, axis))

    def mirror_lanes(x):
        for bit in (1, 2, 4, 8, 16, 32, 64):
            x = swap(x, bit, 1)
        return x

    def mirror(x):
        x = mirror_lanes(x)
        for bit in (1, 2, 4):
            x = swap(x, bit, 0)
        return x

    @pl.when(is_top)
    def _():
        for place in (3, 4, 5):
            for field in range(2):
                rows_in[place, field] = mirror(rows_in[place, field])
        rows_in[3, 2] = mirror_lanes(rows_in[3, 2])

    level_row = row.astype(jnp.float32)
    carry_north = jnp.where(is_top, 0.0, 1.0)
    own_first, own_last = rows_out[0], rows_out[1]
    shared_n = jnp.minimum(own_last[0][7:8], rows_in[3, 0][0:1])
    flux_n = jnp.where(
        shared_n > level_row,
        0.0625 * (1.92 * (rows_in[3, 2] - own_last[2])
                  - carry_north * (own_last[3] + rows_in[3, 3]) * (own_last[2] + rows_in[3, 2])),
        0.0)
    shared_s = jnp.minimum(own_first[0][0:1], rows_in[0, 0][7:8])
    flux_s = jnp.where(
        shared_s > level_row,
        0.0625 * (1.92 * (own_first[2] - rows_in[0, 2])
                  - (own_first[3] + rows_in[0, 3]) * (own_first[2] + rows_in[0, 2])),
        0.0)
    first_own, last_own = pl.ds(0, 8), pl.ds(rows - 8, 8)
    for k in range(LEVELS):
        nt[k, last_own, :] = nt[k, last_own, :] + jnp.where(row == 7, flux_n[k:k + 1], 0.0)
        nt[k, first_own, :] = nt[k, first_own, :] - jnp.where(row == 0, flux_s[k:k + 1], 0.0)
    total[last_own, :] = total[last_own, :] + jnp.where(
        row == 7, jnp.sum(flux_n, axis=0, keepdims=True), 0.0)
    total[first_own, :] = total[first_own, :] - jnp.where(
        row == 0, jnp.sum(flux_s, axis=0, keepdims=True), 0.0)

    depths = [buffer[at_l, :] for buffer in (beside_out, beside_w, beside_e)]
    for half in range(2):
        at = pl.ds(half * part, part)
        lane_p = lanes(part)
        even = lane_p % 2 == 0
        mine, from_w, from_e = beside_out[at, :], beside_w[at, :], beside_e[at, :]
        here = jnp.where(even, mine, roll(from_w, 1))
        there = jnp.where(even, roll(from_e, -1), mine)
        carried = roll(here + there, -16) * (here + there)
        d_mine, d_w, d_e = depths
        shared = jnp.where(
            lane_p % 16 == 7, jnp.minimum(d_mine, roll(d_e, -1)),
            jnp.where(lane_p % 16 == 8, jnp.minimum(roll(d_w, 1), d_mine), 0.0))
        shared = jnp.where((lane_p // 16) % 2 == half, shared, 0.0)
        shared = roll(shared, -7 - 16 * half)
        for shift in (2, 4, 8):
            shared = shared + roll(shared, shift)
        level = ((lane_p % 16) // 2).astype(jnp.float32)
        through = jnp.where(
            jnp.logical_and(shared > level, lane_p % 32 < 16),
            0.0625 * (1.92 * (there - here) - carried), 0.0)
        through = jnp.where(even, through, -through)
        flux[at, :] = through
        for shift in (2, 4, 8):
            through = through + roll(through, -shift)
        flux_sum[at, :] = through

    def right_side(c):
        at = pl.ds(c * part, part)
        lane_p = lanes(part)
        ends = jnp.logical_or(lane_p == 0, lane_p == LANES - 1)
        across = roll(flux_sum[pl.ds((c % 2) * part, part), :], 127 - 32 * (c // 2))
        summed = total[at, :] + jnp.where(ends, across, 0.0)
        value = jnp.where(lv[0, part_rows(c), :] > 0.0, fo[at, :], 0.0) + summed * 8.0 ** -0.5
        basis[0, 0, part_rows(c), :] = value
        return value

    edge_out[...] = fold([right_side(c) for c in range(PARTS)])
    for side, r, _ in edges:
        edge_rows_out[side] = basis[0, 0, pl.ds(r, GHOST), :]
    second_sent, second_received = exchange(
        1, edge_out, edge_w, edge_e, lambda side: edge_rows_out.at[side], edge_rows,
        lambda ref: ref)

    def place_rows(buffer, get):
        for r, across, w_at, e_at in ((south, 0, 1, 2), (top, 3, 4, 5)):
            at = pl.ds(r, GHOST)
            buffer[0, at, :] = get(across)
            buffer[1, at, :] = jnp.where(
                lane < EDGE, get(e_at), jnp.where(lane >= LANES - EDGE, get(w_at), 0.0))

    for buffer, at, field in ((lv, at_l, 0), (st, at_s, 1)):
        for c, x in enumerate(unfold(beside_w[at, :], beside_e[at, :])):
            buffer[1, part_rows(c), :] = x
        place_rows(buffer, lambda place, field=field: rows_in[place, field])

    fold_row = jnp.where(is_top, top - 1, -1)

    def weigh(a, b):
        return a * b / (a + b + 1.0)

    def weights_rows(r, n, carry):
        at, up = pl.ds(r, n), pl.ds(r + 1, n)
        lane = lanes(n)
        d_m, d_s = lv[0, at, :], lv[1, at, :]
        n_m, n_s = lv[0, up, :], lv[1, up, :]
        e_m, e_s = ring_east(d_m, d_s, lane)
        ne_m, ne_s = ring_east(n_m, n_s, lane)
        nw_m, nw_s = ring_west(n_m, n_s, lane)
        corner = jnp.where(row_is(r, n, fold_row), 0.0, 0.25)
        east_m, east_s = weigh(d_m, e_m), weigh(d_s, e_s)
        neast_m, neast_s = corner * weigh(d_m, ne_m), corner * weigh(d_s, ne_s)
        nwest_m, nwest_s = corner * weigh(d_m, nw_m), corner * weigh(d_s, nw_s)
        w_e[0, at, :], w_e[1, at, :] = east_m, east_s
        w_n[0, at, :], w_n[1, at, :] = weigh(d_m, n_m), weigh(d_s, n_s)
        w_ne[0, at, :], w_ne[1, at, :] = neast_m, neast_s
        w_nw[0, at, :], w_nw[1, at, :] = nwest_m, nwest_s
        w_er[0, at, :], w_er[1, at, :] = ring_west(east_m, east_s, lane)
        w_ner[0, at, :], w_ner[1, at, :] = ring_west(neast_m, neast_s, lane)
        w_nwr[0, at, :], w_nwr[1, at, :] = ring_east(nwest_m, nwest_s, lane)
        return carry

    sweep("weights", south, reach, WEIGHTS_STEP, weights_rows)

    def diagonal_rows(r, n, carry):
        at, down = pl.ds(r, n), pl.ds(r - 1, n)
        for half in range(2):
            whole = (
                st[half, at, :] + w_e[half, at, :] + w_er[half, at, :] + w_n[half, at, :]
                + w_n[half, down, :] + w_ne[half, at, :] + w_nw[half, at, :]
                + w_ner[half, down, :] + w_nwr[half, down, :])
            rdiag[half, at, :] = jnp.where(whole > 0.0, 1.0 / whole, 0.0)
            if half == 0:
                diag[at, :] = whole
        return carry

    sweep("diagonal", south, reach, DIAGONAL_STEP, diagonal_rows)
    diag[pl.ds(south, GHOST), :] = nothing
    diag[pl.ds(top, GHOST), :] = nothing

    def ends_rows(r, n, carry):
        lane = lanes(n)
        ends = jnp.logical_or(lane == 0, lane == LANES - 1)
        across = flux[pl.ds(r, n), :]
        for c in range(PARTS // 2):
            at = pl.ds(c * 2 * part + r, n)
            for k in range(LEVELS):
                nt[k, at, :] = nt[k, at, :] + jnp.where(
                    ends, roll(across, 127 - 32 * c - 2 * k), 0.0)
        return carry

    sweep("new", 0, 2 * part, part, ends_rows)
    out_new = local_copy("out", nt, new_out, out_sem.at[0])
    out_new.start()

    second_received()
    pl.when(jnp.logical_not(not_bottom))(lambda: clear(edge_rows))

    @pl.when(is_top)
    def _():
        for place in (3, 4, 5):
            edge_rows[place] = mirror(edge_rows[place])

    for c, x in enumerate(unfold(edge_w[...], edge_e[...])):
        basis[0, 1, part_rows(c), :] = x
    place_rows(basis.at[0], lambda place: edge_rows[place])

    gram = {}

    def fold_rows(x):
        return jnp.sum(x.reshape(x.shape[0] // 8, 8, LANES), axis=0)

    def scaled_rows(r, n, acc):
        at = pl.ds(r, n)
        for half in range(2):
            x = basis[0, half, at, :]
            y = x * rdiag[half, at, :]
            basis[0, half, at, :] = y
            if half == 0:
                acc = acc + fold_rows(diag[at, :] * y * y)
        return acc

    gram[0, 0] = sweep("scaled", south, reach, SCALED_STEP, scaled_rows, nothing)

    def neighbours_sum(k, r, n, halves):
        at, up, down = pl.ds(r, n), pl.ds(r + 1, n), pl.ds(r - 1, n)
        lane = lanes(n)
        sums, to_west, to_east = [], [], []
        for half in range(2):
            x = basis[k, half, at, :]
            x_n = basis[k, half, up, :]
            x_s = basis[k, half, down, :]
            to_east.append(
                w_e[half, at, :] * x + w_ne[half, down, :] * x_s + w_nwr[half, at, :] * x_n)
            to_west.append(
                w_er[half, at, :] * x + w_nw[half, down, :] * x_s + w_ner[half, at, :] * x_n)
            if half < halves:
                sums.append(w_n[half, at, :] * x_n + w_n[half, down, :] * x_s)
        from_west = ring_west(to_east[0], to_east[1], lane)
        from_east = ring_east(to_west[0], to_west[1], lane)
        return [sums[h] + from_west[h] + from_east[h] for h in range(halves)]

    def apply_rows(k, r, n, halves):
        at = pl.ds(r, n)
        sums = neighbours_sum(k, r, n, halves)
        out = []
        for half in range(halves):
            x = basis[k, half, at, :]
            y = rdiag[half, at, :] * sums[half]
            if SHIFT[k] != 0.0:
                y = y - SHIFT[k] * x
            if BACK[k] != 0.0:
                y = y - BACK[k] * basis[k - 1, half, at, :]
            y = GAIN[k] * y
            basis[k + 1, half, at, :] = y
            out.append(y)
        return out[0]

    for k in range(ITERS):
        last = k == ITERS - 1
        terms = [p for p in PAIRS if p[1] == k + 1]

        def apply_own(r, n, accs, k=k, terms=terms, halves=1 if last else 2):
            at = pl.ds(r, n)
            y = apply_rows(k, r, n, halves)
            scaled = diag[at, :] * y
            return tuple(
                acc + fold_rows(scaled * (y if a == k + 1 else basis[a, 0, at, :]))
                for acc, (a, _) in zip(accs, terms))

        sums = sweep(
            "apply", BASE if last else south, rows if last else reach,
            LAST_STEP if last else APPLY_STEP, apply_own, tuple(nothing for _ in terms))
        for p, s in zip(terms, sums):
            gram[p] = s

    per_lane = [jnp.sum(gram[p], axis=0, keepdims=True) for p in PAIRS]
    per_lane = per_lane + [jnp.zeros((1, LANES), jnp.float32)] * (24 - len(per_lane))
    stacked = jnp.sum(jnp.concatenate(per_lane, axis=0), axis=1, keepdims=True)
    count = stacked.shape[0]
    own_lane = lane_of((count, LANES)) == row_of((count, LANES))
    summed = jnp.sum(jnp.where(own_lane, stacked, 0.0), axis=0, keepdims=True)

    sends = []
    for stage, (place, peers) in enumerate(stages):
        box = boxes[stage]
        box[pl.ds(place, 1), :, :] = summed[None]
        for n, (_, device) in enumerate(peers):
            copy = remote(
                "red", box.at[place], box.at[place],
                red_send.at[stage, n], red_recv.at[stage, place], device)
            copy.start()
            sends.append(copy)
        for index, _ in peers:
            arrived("red", box.at[index], red_recv.at[stage, index])
        summed = box[0]
        for n in range(1, len(peers) + 1):
            summed = summed + box[n]

    spread = jnp.sum(
        jnp.where(own_lane, jnp.broadcast_to(summed, (count, LANES)), 0.0),
        axis=1, keepdims=True)
    sums = {
        p: jnp.broadcast_to(spread[n:n + 1], tile) for n, p in enumerate(PAIRS)
    }
    surface_by, scaled_by = solve(sums)

    surface_by = [c[0:1] for c in surface_by]
    scaled_by = [c[0:1] for c in scaled_by]

    def final_rows(r, n, carry):
        at = pl.ds(r, n)
        to = pl.ds(pl.multiple_of(r - BASE, 8), n)
        x = [basis[k, 0, at, :] for k in range(ITERS + 1)]
        level_at = surface_by[0] * x[0]
        left = scaled_by[0] * x[0]
        for k in range(1, ITERS + 1):
            if k < ITERS:
                level_at = level_at + surface_by[k] * x[k]
            left = left + scaled_by[k] * x[k]
        surf[to, :] = level_at
        resid[to, :] = diag[at, :] * left
        return carry

    sweep("final", BASE, rows, FINAL_STEP, final_rows)
    out_surf = local_copy("out", surf, surf_out, out_sem.at[1])
    out_res = local_copy("out", resid, res_out, out_sem.at[2])
    out_surf.start()
    out_res.start()

    first_sent()
    second_sent()
    for copy in sends:
        copy.wait_send()
    out_new.wait()
    out_surf.wait()
    out_res.wait()


def hand_over(new, surf, res, new_out, surf_out, res_out, cube, flat, in_sem, out_sem):
    pieces = [(surf, flat.at[0], surf_out), (res, flat.at[1], res_out)] + [
        (new.at[k], cube.at[k], new_out.at[k]) for k in range(LEVELS)]
    reads = [pltpu.make_async_copy(a, b, in_sem.at[n]) for n, (a, b, _) in enumerate(pieces)]
    writes = [pltpu.make_async_copy(b, c, out_sem.at[n]) for n, (_, b, c) in enumerate(pieces)]
    for read in reads:
        read.start()
    for read, write in zip(reads, writes):
        read.wait()
        write.start()
    for write in writes:
        write.wait()


def local(lon_count, lat_count, tracer, east_vel, north_vel, levels, forcing, storage):
    rows = tracer.shape[1]
    flat = (rows + 4 * GHOST, LANES)
    part = rows // PARTS
    f32 = jnp.float32
    extent = extents(lon_count, lat_count)
    sizes = [stage_size(extent, axes) for axes in STAGES]

    def vmem(*shape, dtype=f32):
        return pltpu.VMEM(shape, dtype)

    cube = vmem(LEVELS, rows + 2 * GHOST, LANES)
    pair = vmem(2, *flat)
    block = vmem(rows, LANES)
    beside = vmem(4 * part, LANES)
    edge = vmem(part, LANES)
    dma = pltpu.SemaphoreType.DMA
    anywhere = pl.BlockSpec(memory_space=pl.ANY)
    outs = (
        jax.ShapeDtypeStruct(tracer.shape, f32),
        jax.ShapeDtypeStruct(levels.shape, f32),
        jax.ShapeDtypeStruct(levels.shape, f32),
    )
    results = pl.pallas_call(
        functools.partial(kernel, lon_count, lat_count, rows),
        out_shape=outs,
        in_specs=[anywhere] * 6,
        out_specs=(anywhere,) * 3,
        scratch_shapes=[
            cube, cube, cube, vmem(rows, LANES, dtype=jnp.int32), block, pair, pair,
            beside, beside, beside, vmem(2, 4, 8, LANES), vmem(6, 4, 8, LANES),
            edge, edge, edge, vmem(2, 8, LANES), vmem(6, 8, LANES),
            vmem(2 * part, LANES), vmem(2 * part, LANES), block, vmem(LEVELS, rows, LANES),
            pair, pair, pair, pair, pair, pair, pair, pair, vmem(*flat),
            vmem(ITERS + 1, 2, *flat),
            block, block,
            dma((6,)), dma((2, 6)), dma((2, 6)), dma((2, 2)), dma((2, 2)),
            dma((len(sizes), max(sizes))), dma((len(sizes), max(sizes))), dma((3,)),
            *[vmem(size, 1, LANES) for size in sizes],
        ],
        compiler_params=pltpu.CompilerParams(
            collective_id=0, has_side_effects=True, vmem_limit_bytes=61 * 2**20
        ),
        cost_estimate=pl.CostEstimate(flops=10**8, bytes_accessed=6 * 10**6, transcendentals=0),
        name="ocean_step",
    )(tracer, east_vel, north_vel, levels, forcing, storage)
    return pl.pallas_call(
        hand_over,
        out_shape=outs,
        in_specs=[anywhere] * 3,
        out_specs=(anywhere,) * 3,
        scratch_shapes=[
            vmem(*tracer.shape), vmem(2, rows, LANES),
            dma((LEVELS + 2,)), dma((LEVELS + 2,)),
        ],
        compiler_params=pltpu.CompilerParams(vmem_limit_bytes=61 * 2**20),
        name="hand_over",
    )(*results)


def solution(mesh):
    cube, flat = P(None, "lat", "lon"), P("lat", "lon")
    return jax.shard_map(
        functools.partial(local, mesh.shape["lon"], mesh.shape["lat"]),
        mesh=mesh,
        in_specs=(cube, cube, cube, flat, flat, flat),
        out_specs=(cube, flat, flat),
        check_vma=False,
    )
```

```python
import functools
import itertools

import jax
import jax.numpy as jnp
from jax import lax
from jax.experimental import pallas as pl
from jax.experimental.pallas import tpu as pltpu
from jax.sharding import PartitionSpec as P

ITERS = 5
LEVELS = 8
GHOST = 8
BASE = 2 * GHOST
LANES = 128
EDGE = 8
PARTS = 8
SCALE = 0.8
MESH = pl.DeviceIdType.MESH
STAGES = (("core", "y"), ("x", "z"))
TRACER_STEP = 16
WEIGHTS_STEP = 112
DIAGONAL_STEP = 48
SCALED_STEP = 112
APPLY_STEP = 112
LAST_STEP = 160
FINAL_STEP = 80

GAIN = (-1.0, 1.0 / SCALE, 2.0 / SCALE, 2.0 / SCALE, 2.0 / SCALE)
SHIFT = (1.0, 0.0, 0.0, 0.0, 0.0)
BACK = (0.0, 0.0, SCALE / 2, SCALE / 2, SCALE / 2)
PAIRS = tuple((i, j) for j in range(ITERS + 1) for i in range(j + 1) if (i, j) != (ITERS, ITERS))


def roll(x, shift):
    return pltpu.roll(x, shift % x.shape[-1], x.ndim - 1)


def lane_of(shape):
    return lax.broadcasted_iota(jnp.int32, shape, len(shape) - 1)


def row_of(shape):
    return lax.broadcasted_iota(jnp.int32, shape, len(shape) - 2)


def extents(lon_count, lat_count):
    z = min(4, lon_count // 2)
    return {"core": 2, "z": z, "x": lon_count // (2 * z), "y": lat_count}


def stage_size(extent, axes):
    size = 1
    for axis in axes:
        size *= extent[axis]
    return size


def sweep(name, first, rows, step, body, start=0):
    whole = rows // step

    def chunk(i, carry):
        return body(pl.multiple_of(first + i * step, 8), step, carry)

    carry = lax.fori_loop(0, whole, chunk, start) if whole else start
    if rows % step:
        carry = body(first + whole * step, rows % step, carry)
    return carry


def remote(name, src, dst, sent, received, device):
    return pltpu.make_async_remote_copy(
        src, dst, sent, received, device_id=device, device_id_type=MESH)


def local_copy(name, src, dst, done):
    return pltpu.make_async_copy(src, dst, done)


def step(name, run):
    run()


def arrived(name, part, received):
    pltpu.make_async_copy(part, part, received).wait()


def face_flux(here, there, vel_here, vel_there, shared, level):
    carried = (vel_here + vel_there) * (here + there)
    return jnp.where(shared > level, 1.92 * (there - here) - carried, 0.0)


def ring_east(main, strip, lane):
    a, b = roll(main, -1), roll(strip, -1)
    last = lane == LANES - 1
    return jnp.where(last, b, a), jnp.where(last, a, b)


def ring_west(main, strip, lane):
    a, b = roll(main, 1), roll(strip, 1)
    first = lane == 0
    return jnp.where(first, b, a), jnp.where(first, a, b)


def solve(gram):
    size = ITERS + 1

    def product(left, right):
        total = None
        for i, a in enumerate(left):
            if a is None:
                continue
            inner = None
            for j, b in enumerate(right):
                if b is None:
                    continue
                term = gram[min(i, j), max(i, j)] * b
                inner = term if inner is None else inner + term
            total = a * inner if total is None else total + a * inner
        return total

    def operate(coeffs):
        out = [None] * size

        def add(k, value):
            out[k] = value if out[k] is None else out[k] + value

        for k in range(ITERS):
            if coeffs[k] is None:
                continue
            add(k + 1, coeffs[k] * (-1.0 / GAIN[k]))
            if SHIFT[k] != 1.0:
                add(k, coeffs[k] * (1.0 - SHIFT[k]))
            if BACK[k] != 0.0:
                add(k - 1, coeffs[k] * (-BACK[k]))
        return out

    one = jnp.ones_like(gram[0, 0])
    scaled = [one] + [None] * ITERS
    direction = list(scaled)
    surface = [None] * size
    rho = product(scaled, scaled)
    for turn in range(ITERS):
        image = operate(direction)
        step = rho / product(direction, image)
        for k in range(size):
            if direction[k] is not None:
                move = step * direction[k]
                surface[k] = move if surface[k] is None else surface[k] + move
            if image[k] is not None:
                move = step * image[k]
                scaled[k] = -move if scaled[k] is None else scaled[k] - move
        if turn == ITERS - 1:
            break
        rho_new = product(scaled, scaled)
        ratio = rho_new / rho
        direction = [
            s if d is None else s + ratio * d for s, d in zip(scaled, direction)
        ]
        rho = rho_new
    return surface[:ITERS], scaled


def kernel(
    lon_count, lat_count, rows,
    t_in, u_in, v_in, lev_in, forc_in, stor_in,
    new_out, surf_out, res_out,
    tr, ur, vr, li, fo, lv, st,
    beside_out, beside_w, beside_e, rows_out, rows_in,
    ends_out, ends_w, ends_e, vel_out, vel_send, vel_in, folded_out,
    edge_out, edge_w, edge_e, edge_rows_out, edge_rows,
    flux, flux_sum, total, nt,
    w_e, w_n, w_ne, w_nw, w_er, w_ner, w_nwr, rdiag, diag, basis,
    surf, resid,
    in_sem, rows_send, rows_recv, beside_send, beside_recv, red_send, red_recv, out_sem, *boxes,
):
    lon, lat = lax.axis_index("lon"), lax.axis_index("lat")
    is_top = lat == lat_count - 1
    not_top = jnp.logical_not(is_top)
    not_bottom = lat > 0
    top = BASE + rows
    south = BASE - GHOST
    own = pl.ds(BASE, rows)
    inner = pl.ds(GHOST, rows)
    tile = (8, LANES)
    lane = lane_of(tile)
    row = row_of(tile)
    reach = rows + 2 * GHOST
    part = rows // PARTS

    def lanes(n):
        return lane_of((n, LANES))

    def row_is(r, n, which):
        return row_of((n, LANES)) + r == which

    loads = [
        local_copy("load", src, dst, in_sem.at[n]) for n, (src, dst) in enumerate((
            (lev_in, li), (stor_in, st.at[0, own, :]), (t_in, tr.at[:, inner, :]),
            (u_in, ur.at[:, inner, :]), (v_in, vr.at[:, inner, :]), (forc_in, fo),
        ))
    ]
    for load in loads:
        load.start()

    east = lax.rem(lon + 1, lon_count)
    west = lax.rem(lon + lon_count - 1, lon_count)
    up_lat = jnp.where(is_top, lat, lat + 1)
    down_lat = jnp.maximum(lat - 1, 0)
    up_lon = jnp.where(is_top, lon_count - 1 - lon, lon)
    up_e = jnp.where(is_top, lax.rem(2 * lon_count - 2 - lon, lon_count), east)
    up_w = jnp.where(is_top, lax.rem(lon_count - lon, lon_count), west)
    self_e = jnp.logical_and(is_top, up_e == lon)
    self_w = jnp.logical_and(is_top, up_w == lon)
    other_e, other_w = jnp.logical_not(self_e), jnp.logical_not(self_w)

    extent = extents(lon_count, lat_count)
    here_at = {
        "core": lax.rem(lon, 2),
        "z": lax.rem(lon // 2, extent["z"]),
        "x": lon // (2 * extent["z"]),
        "y": lat,
    }

    def stage_peers(axes):
        def index_of(at):
            index = 0
            for axis in axes:
                index = index * extent[axis] + at[axis]
            return index

        moves = sorted(
            itertools.product(*(range(extent[axis]) for axis in axes)),
            key=lambda move: -sum(min(d, extent[a] - d) for d, a in zip(move, axes)))
        peers = []
        for move in moves[:-1]:
            at = dict(here_at)
            for axis, d in zip(axes, move):
                at[axis] = lax.rem(here_at[axis] + d, extent[axis])
            device = {
                "lon": (at["x"] * extent["z"] + at["z"]) * 2 + at["core"], "lat": at["y"]}
            peers.append((index_of(at), device))
        place = index_of(here_at)
        return place, peers

    stages = [stage_peers(axes) for axes in STAGES]

    barrier = pltpu.get_barrier_semaphore()

    def greet(device):
        pl.semaphore_signal(barrier, inc=1, device_id=device, device_id_type=MESH)

    greet({"lon": east, "lat": lat})
    greet({"lon": west, "lat": lat})
    greet({"lon": up_lon, "lat": up_lat})

    @pl.when(other_e)
    def _():
        greet({"lon": up_e, "lat": up_lat})

    @pl.when(other_w)
    def _():
        greet({"lon": up_w, "lat": up_lat})

    @pl.when(not_bottom)
    def _():
        greet({"lon": lon, "lat": down_lat})
        greet({"lon": east, "lat": down_lat})
        greet({"lon": west, "lat": down_lat})

    greeted = 3
    for _, peers in stages:
        for _, device in peers:
            greet(device)
        greeted += len(peers)
    greeted = greeted + jnp.where(self_e, 0, 1) + jnp.where(self_w, 0, 1) + jnp.where(not_bottom, 3, 0)

    def fold(ranges):
        out = None
        for c, x in enumerate(ranges):
            moved = roll(x, EDGE + 16 * c)
            out = moved if out is None else jnp.where(lanes(part) // 16 == c, moved, out)
        return out

    def unfold(from_west, from_east):
        both = jnp.where(lanes(part) % 16 < EDGE, from_west, from_east)
        ends = jnp.logical_or(lanes(part) < EDGE, lanes(part) >= LANES - EDGE)
        return [
            jnp.where(ends, roll(both, -(EDGE + 16 * c)), 0.0) for c in range(PARTS)]

    def part_rows(c):
        return pl.ds(BASE + c * part, part)

    loads[0].wait()
    loads[1].wait()
    lv[0, own, :] = li[...].astype(jnp.float32)
    at_l, at_s = pl.ds(0, part), pl.ds(part, part)
    beside_out[at_l, :] = fold([lv[0, part_rows(c), :] for c in range(PARTS)])
    beside_out[at_s, :] = fold([st[0, part_rows(c), :] for c in range(PARTS)])
    edges = ((0, BASE, GHOST), (1, top - GHOST, GHOST + rows - 1))
    for side, r, _ in edges:
        rows_out[side, 0] = lv[0, pl.ds(r, GHOST), :]
        rows_out[side, 1] = st[0, pl.ds(r, GHOST), :]

    def exchange(phase, beside_from, to_east, to_west, rows_from, rows_to, corners, before=None):
        def by_rows(slot, side, place, to_lon, to_lat):
            return remote(
                "halo", rows_from.at[side], rows_to.at[place],
                rows_send.at[phase, slot], rows_recv.at[phase, place],
                {"lon": to_lon, "lat": to_lat})

        go_e = remote(
            "halo", beside_from, to_east, beside_send.at[phase, 0], beside_recv.at[phase, 0],
            {"lon": east, "lat": lat})
        go_w = remote(
            "halo", beside_from, to_west, beside_send.at[phase, 1], beside_recv.at[phase, 1],
            {"lon": west, "lat": lat})
        go_up = by_rows(0, 1, jnp.where(is_top, 3, 0), up_lon, up_lat)
        go_down = by_rows(3, 0, 3, lon, down_lat)
        if corners:
            go_up_e = by_rows(1, 1, jnp.where(is_top, 5, 1), up_e, up_lat)
            go_up_w = by_rows(2, 1, jnp.where(is_top, 4, 2), up_w, up_lat)
            go_down_e = by_rows(4, 0, 4, east, down_lat)
            go_down_w = by_rows(5, 0, 5, west, down_lat)
            stay_e = local_copy(
                "halo", rows_from.at[1], rows_to.at[5], rows_recv.at[phase, 5])
            stay_w = local_copy(
                "halo", rows_from.at[1], rows_to.at[4], rows_recv.at[phase, 4])
        go_e.start()
        go_w.start()
        if before is not None:
            before()
        if corners:
            pl.when(other_e)(go_up_e.start)
            pl.when(other_w)(go_up_w.start)
            pl.when(self_e)(stay_e.start)
            pl.when(self_w)(stay_w.start)

            @pl.when(not_bottom)
            def _():
                go_down_e.start()
                go_down_w.start()
        go_up.start()
        pl.when(not_bottom)(go_down.start)

        def sent():
            go_e.wait_send()
            go_w.wait_send()
            go_up.wait_send()
            pl.when(not_bottom)(go_down.wait_send)
            if corners:
                pl.when(other_e)(go_up_e.wait_send)
                pl.when(other_w)(go_up_w.wait_send)

                @pl.when(not_bottom)
                def _():
                    go_down_e.wait_send()
                    go_down_w.wait_send()

        def received():
            arrived("halo", to_east, beside_recv.at[phase, 0])
            arrived("halo", to_west, beside_recv.at[phase, 1])
            for place in (3, 4, 5) if corners else (3,):
                arrived("halo", rows_to.at[place], rows_recv.at[phase, place])

            @pl.when(not_bottom)
            def _():
                for place in (0, 1, 2) if corners else (0,):
                    arrived("halo", rows_to.at[place], rows_recv.at[phase, place])

        return sent, received

    loads[2].wait()
    loads[3].wait()

    def gather_ends(buffer, r, n):
        x = [buffer[k, pl.ds(r, n), :] for k in range(LEVELS)]
        lane = lanes(n)
        width = 2
        while len(x) > 1:
            window = jnp.logical_or(lane == 0, lane > LANES - width)
            x = [
                jnp.where(window, x[i + 1], roll(x[i], -width)) for i in range(0, len(x), 2)]
            width *= 2
        return x[0]

    def pack_ends(r, n, carry):
        out = None
        for c in range(PARTS // 2):
            for slot, buffer in enumerate((tr, ur)):
                moved = roll(gather_ends(buffer, GHOST + c * 2 * part + r, n), 32 * c + 16 * slot - 113)
                out = moved if out is None else jnp.where(
                    lanes(n) // 16 == 2 * c + slot, moved, out)
        ends_out[pl.ds(r, n), :] = out
        return carry

    sweep("ends", 0, 2 * part, part, pack_ends)
    def swap(x, bit, bits, axis):
        size = x.shape[axis]
        index = (lax.broadcasted_iota(jnp.int32, x.shape, axis) // bit) % bits
        out = None
        for p in range(bits):
            moved = pltpu.roll(x, ((2 * p - bits + 1) * bit) % size, axis)
            out = moved if out is None else jnp.where(index == p, moved, out)
        return out

    def mirror_lanes(x):
        for bit, bits in ((1, 4), (4, 4), (16, 4), (64, 2)):
            x = swap(x, bit, bits, 1)
        return x

    def mirror(x):
        return swap(mirror_lanes(x), 1, 8, 0)

    def end_rows():
        loads[4].wait()
        for side, _, r in edges:
            for k in range(LEVELS):
                vel_out[side, 0, pl.ds(k, 1), :] = tr[k, pl.ds(r, 1), :]
                vel_out[side, 1, pl.ds(k, 1), :] = vr[k, pl.ds(r, 1), :]

        @pl.when(is_top)
        def _():
            folded_out[...] = mirror_lanes(vel_out[1, 0])

        @pl.when(not_top)
        def _():
            folded_out[...] = vel_out[1, 0]

        vel_send[0] = vel_out[0]
        vel_send[1, 0] = folded_out[...]
        vel_send[1, 1] = vel_out[1, 1]

    pl.semaphore_wait(barrier, greeted)

    depth_sent, depth_received = exchange(
        0, beside_out, beside_w, beside_e, rows_out, rows_in, True)
    ends_sent, ends_received = exchange(
        1, ends_out, ends_w, ends_e, vel_send, vel_in, False, end_rows)

    nothing = jnp.zeros(tile, jnp.float32)
    for r in (south - 8, top + 8):
        at = pl.ds(r, 8)
        for half in range(2):
            for buffer in (lv, w_n, w_ne, w_nw):
                buffer[half, at, :] = nothing
            for k in range(ITERS + 1):
                basis[k, half, at, :] = nothing

    def tracer_rows(r, n, carry):
        at, up, down = pl.ds(r, n), pl.ds(r + 1, n), pl.ds(r - 1, n)
        wide, wide_up, wide_down = (pl.ds(r + GHOST + d, n) for d in (0, 1, -1))
        depth = lv[0, wide, :]
        open_e = jnp.where(
            lanes(n) == LANES - 1, 0.0, jnp.minimum(depth, roll(depth, -1)))
        open_n = jnp.where(
            row_is(r, n, GHOST + rows - 1), 0.0, jnp.minimum(depth, lv[0, wide_up, :]))
        open_s = jnp.where(
            row_is(r, n, GHOST), 0.0, jnp.minimum(depth, lv[0, wide_down, :]))
        below = None
        summed = None
        here = tr[0, at, :]
        for k in range(LEVELS):
            vel = vr[k, at, :]
            zonal = ur[k, at, :]
            flux_e = face_flux(here, roll(here, -1), zonal, roll(zonal, -1), open_e, k)
            flux_n = face_flux(here, tr[k, up, :], vel, vr[k, up, :], open_n, k)
            flux_s = face_flux(tr[k, down, :], here, vr[k, down, :], vel, open_s, k)
            change = 0.0625 * ((flux_e - roll(flux_e, 1)) + (flux_n - flux_s))
            result = here + change
            if below is not None:
                result = result - below
            if k + 1 < LEVELS:
                above = tr[k + 1, at, :]
                below = jnp.where(depth > k + 1, 0.1 * (above - here), 0.0)
                result = result + below
                here = above
            nt[k, pl.ds(r - GHOST, n), :] = result
            wet_part = jnp.where(depth > k, result, 0.0)
            summed = wet_part if summed is None else summed + wet_part
        total[pl.ds(r - GHOST, n), :] = summed
        return carry

    sweep("tracer", GHOST, rows, TRACER_STEP, tracer_rows)

    depth_received()

    def clear(buffer):
        for place in range(buffer.shape[0] // 2):
            buffer[place] = jnp.zeros(buffer.shape[1:], buffer.dtype)

    pl.when(jnp.logical_not(not_bottom))(lambda: clear(rows_in))

    @pl.when(is_top)
    def _():
        for place in (3, 4, 5):
            for field in range(2):
                rows_in[place, field] = mirror(rows_in[place, field])

    shared_n = jnp.minimum(rows_out[1, 0][7:8], rows_in[3, 0][0:1])
    shared_s = jnp.minimum(rows_out[0, 0][0:1], rows_in[0, 0][7:8])
    lane_p = lanes(part)
    even = lane_p % 2 == 0
    d_mine, d_w, d_e = (buffer[at_l, :] for buffer in (beside_out, beside_w, beside_e))
    both = jnp.where(
        lane_p % 16 == 7, jnp.minimum(d_mine, roll(d_e, -1)),
        jnp.where(lane_p % 16 == 8, jnp.minimum(roll(d_w, 1), d_mine), 0.0))
    for half in range(2):
        shared = jnp.where((lane_p // 16) % 2 == half, both, 0.0)
        shared = roll(shared, -7 - 16 * half)
        for shift in (2, 4, 8):
            shared = shared + roll(shared, shift)
        flux[pl.ds(half * part, part), :] = shared

    ends_received()
    pl.when(jnp.logical_not(not_bottom))(lambda: clear(vel_in))

    level_row = row.astype(jnp.float32)
    carry_north = jnp.where(is_top, 0.0, 1.0)
    own_first, own_last = vel_out[0], vel_out[1]
    flux_n = jnp.where(
        shared_n > level_row,
        0.0625 * (1.92 * (vel_in[3, 0] - own_last[0])
                  - carry_north * (own_last[1] + vel_in[3, 1]) * (own_last[0] + vel_in[3, 0])),
        0.0)
    flux_s = jnp.where(
        shared_s > level_row,
        0.0625 * (1.92 * (own_first[0] - vel_in[0, 0])
                  - (own_first[1] + vel_in[0, 1]) * (own_first[0] + vel_in[0, 0])),
        0.0)
    first_own, last_own = pl.ds(0, 8), pl.ds(rows - 8, 8)
    total[last_own, :] = total[last_own, :] + jnp.where(
        row == 7, jnp.sum(flux_n, axis=0, keepdims=True), 0.0)
    total[first_own, :] = total[first_own, :] - jnp.where(
        row == 0, jnp.sum(flux_s, axis=0, keepdims=True), 0.0)

    for half in range(2):
        at = pl.ds(half * part, part)
        mine, from_w, from_e = ends_out[at, :], ends_w[at, :], ends_e[at, :]
        here = jnp.where(even, mine, roll(from_w, 1))
        there = jnp.where(even, roll(from_e, -1), mine)
        carried = roll(here + there, -16) * (here + there)
        level = ((lane_p % 16) // 2).astype(jnp.float32)
        through = jnp.where(
            jnp.logical_and(flux[at, :] > level, lane_p % 32 < 16),
            0.0625 * (1.92 * (there - here) - carried), 0.0)
        through = jnp.where(even, through, -through)
        flux[at, :] = through
        for shift in (2, 4, 8):
            through = through + roll(through, -shift)
        flux_sum[at, :] = through

    def right_side(c):
        at = pl.ds(c * part, part)
        lane_p = lanes(part)
        ends = jnp.logical_or(lane_p == 0, lane_p == LANES - 1)
        across = roll(flux_sum[pl.ds((c % 2) * part, part), :], 127 - 32 * (c // 2))
        summed = total[at, :] + jnp.where(ends, across, 0.0)
        value = jnp.where(lv[0, part_rows(c), :] > 0.0, fo[at, :], 0.0) + summed * 8.0 ** -0.5
        basis[0, 0, part_rows(c), :] = value
        return value

    loads[5].wait()
    edge_out[...] = fold([right_side(c) for c in range(PARTS)])
    for side, r, _ in edges:
        edge_rows_out[side] = basis[0, 0, pl.ds(r, GHOST), :]
    side_sent, side_received = exchange(
        2, edge_out, edge_w, edge_e, edge_rows_out, edge_rows, True)

    def place_rows(buffer, get):
        for r, across, w_at, e_at in ((south, 0, 1, 2), (top, 3, 4, 5)):
            at = pl.ds(r, GHOST)
            buffer[0, at, :] = get(across)
            buffer[1, at, :] = jnp.where(
                lane < EDGE, get(e_at), jnp.where(lane >= LANES - EDGE, get(w_at), 0.0))

    for buffer, at, field in ((lv, at_l, 0), (st, at_s, 1)):
        for c, x in enumerate(unfold(beside_w[at, :], beside_e[at, :])):
            buffer[1, part_rows(c), :] = x
        place_rows(buffer, lambda place, field=field: rows_in[place, field])

    fold_row = jnp.where(is_top, top - 1, -1)

    def weigh(a, b):
        return a * b / (a + b + 1.0)

    def weights_rows(r, n, carry):
        at, up = pl.ds(r, n), pl.ds(r + 1, n)
        lane = lanes(n)
        d_m, d_s = lv[0, at, :], lv[1, at, :]
        n_m, n_s = lv[0, up, :], lv[1, up, :]
        e_m, e_s = ring_east(d_m, d_s, lane)
        ne_m, ne_s = ring_east(n_m, n_s, lane)
        nw_m, nw_s = ring_west(n_m, n_s, lane)
        corner = jnp.where(row_is(r, n, fold_row), 0.0, 0.25)
        east_m, east_s = weigh(d_m, e_m), weigh(d_s, e_s)
        neast_m, neast_s = corner * weigh(d_m, ne_m), corner * weigh(d_s, ne_s)
        nwest_m, nwest_s = corner * weigh(d_m, nw_m), corner * weigh(d_s, nw_s)
        w_e[0, at, :], w_e[1, at, :] = east_m, east_s
        w_n[0, at, :], w_n[1, at, :] = weigh(d_m, n_m), weigh(d_s, n_s)
        w_ne[0, at, :], w_ne[1, at, :] = neast_m, neast_s
        w_nw[0, at, :], w_nw[1, at, :] = nwest_m, nwest_s
        w_er[0, at, :], w_er[1, at, :] = ring_west(east_m, east_s, lane)
        w_ner[0, at, :], w_ner[1, at, :] = ring_west(neast_m, neast_s, lane)
        w_nwr[0, at, :], w_nwr[1, at, :] = ring_east(nwest_m, nwest_s, lane)
        return carry

    sweep("weights", south, reach, WEIGHTS_STEP, weights_rows)

    def diagonal_rows(r, n, carry):
        at, down = pl.ds(r, n), pl.ds(r - 1, n)
        for half in range(2):
            whole = (
                st[half, at, :] + w_e[half, at, :] + w_er[half, at, :] + w_n[half, at, :]
                + w_n[half, down, :] + w_ne[half, at, :] + w_nw[half, at, :]
                + w_ner[half, down, :] + w_nwr[half, down, :])
            rdiag[half, at, :] = jnp.where(whole > 0.0, 1.0 / whole, 0.0)
            if half == 0:
                diag[at, :] = whole
        return carry

    sweep("diagonal", south, reach, DIAGONAL_STEP, diagonal_rows)
    diag[pl.ds(south, GHOST), :] = nothing
    diag[pl.ds(top, GHOST), :] = nothing

    def ends_rows(r, n, carry):
        lane = lanes(n)
        ends = jnp.logical_or(lane == 0, lane == LANES - 1)
        across = flux[pl.ds(r, n), :]
        for c in range(PARTS // 2):
            at = pl.ds(c * 2 * part + r, n)
            for k in range(LEVELS):
                nt[k, at, :] = nt[k, at, :] + jnp.where(
                    ends, roll(across, 127 - 32 * c - 2 * k), 0.0)
        return carry

    sweep("new", 0, 2 * part, part, ends_rows)
    for k in range(LEVELS):
        nt[k, last_own, :] = nt[k, last_own, :] + jnp.where(row == 7, flux_n[k:k + 1], 0.0)
        nt[k, first_own, :] = nt[k, first_own, :] - jnp.where(row == 0, flux_s[k:k + 1], 0.0)
    out_new = local_copy("out", nt, new_out, out_sem.at[0])
    out_new.start()

    side_received()
    pl.when(jnp.logical_not(not_bottom))(lambda: clear(edge_rows))

    @pl.when(is_top)
    def _():
        for place in (3, 4, 5):
            edge_rows[place] = mirror(edge_rows[place])

    for c, x in enumerate(unfold(edge_w[...], edge_e[...])):
        basis[0, 1, part_rows(c), :] = x
    place_rows(basis.at[0], lambda place: edge_rows[place])

    gram = {}

    def fold_rows(x):
        return jnp.sum(x.reshape(x.shape[0] // 8, 8, LANES), axis=0)

    def scaled_rows(r, n, acc):
        at = pl.ds(r, n)
        for half in range(2):
            x = basis[0, half, at, :]
            y = x * rdiag[half, at, :]
            basis[0, half, at, :] = y
            if half == 0:
                acc = acc + fold_rows(diag[at, :] * y * y)
        return acc

    gram[0, 0] = sweep("scaled", south, reach, SCALED_STEP, scaled_rows, nothing)

    def neighbours_sum(k, r, n, halves):
        at, up, down = pl.ds(r, n), pl.ds(r + 1, n), pl.ds(r - 1, n)
        lane = lanes(n)
        sums, to_west, to_east = [], [], []
        for half in range(2):
            x = basis[k, half, at, :]
            x_n = basis[k, half, up, :]
            x_s = basis[k, half, down, :]
            to_east.append(
                w_e[half, at, :] * x + w_ne[half, down, :] * x_s + w_nwr[half, at, :] * x_n)
            to_west.append(
                w_er[half, at, :] * x + w_nw[half, down, :] * x_s + w_ner[half, at, :] * x_n)
            if half < halves:
                sums.append(w_n[half, at, :] * x_n + w_n[half, down, :] * x_s)
        from_west = ring_west(to_east[0], to_east[1], lane)
        from_east = ring_east(to_west[0], to_west[1], lane)
        return [sums[h] + from_west[h] + from_east[h] for h in range(halves)]

    def apply_rows(k, r, n, halves):
        at = pl.ds(r, n)
        sums = neighbours_sum(k, r, n, halves)
        out = []
        for half in range(halves):
            x = basis[k, half, at, :]
            y = rdiag[half, at, :] * sums[half]
            if SHIFT[k] != 0.0:
                y = y - SHIFT[k] * x
            if BACK[k] != 0.0:
                y = y - BACK[k] * basis[k - 1, half, at, :]
            y = GAIN[k] * y
            basis[k + 1, half, at, :] = y
            out.append(y)
        return out[0]

    for k in range(ITERS):
        last = k == ITERS - 1
        terms = [p for p in PAIRS if p[1] == k + 1]

        def apply_own(r, n, accs, k=k, terms=terms, halves=1 if last else 2):
            at = pl.ds(r, n)
            y = apply_rows(k, r, n, halves)
            scaled = diag[at, :] * y
            return tuple(
                acc + fold_rows(scaled * (y if a == k + 1 else basis[a, 0, at, :]))
                for acc, (a, _) in zip(accs, terms))

        sums = sweep(
            "apply", BASE if last else south, rows if last else reach,
            LAST_STEP if last else APPLY_STEP, apply_own, tuple(nothing for _ in terms))
        for p, s in zip(terms, sums):
            gram[p] = s

    per_lane = [jnp.sum(gram[p], axis=0, keepdims=True) for p in PAIRS]
    per_lane = per_lane + [jnp.zeros((1, LANES), jnp.float32)] * (24 - len(per_lane))
    stacked = jnp.sum(jnp.concatenate(per_lane, axis=0), axis=1, keepdims=True)
    count = stacked.shape[0]
    own_lane = lane_of((count, LANES)) == row_of((count, LANES))
    summed = jnp.sum(jnp.where(own_lane, stacked, 0.0), axis=0, keepdims=True)

    sends = []
    for stage, (place, peers) in enumerate(stages):
        box = boxes[stage]
        box[pl.ds(place, 1), :, :] = summed[None]
        for n, (_, device) in enumerate(peers):
            copy = remote(
                "red", box.at[place], box.at[place],
                red_send.at[stage, n], red_recv.at[stage, place], device)
            copy.start()
            sends.append(copy)
        for index, _ in peers:
            arrived("red", box.at[index], red_recv.at[stage, index])
        summed = box[0]
        for n in range(1, len(peers) + 1):
            summed = summed + box[n]

    spread = jnp.sum(
        jnp.where(own_lane, jnp.broadcast_to(summed, (count, LANES)), 0.0),
        axis=1, keepdims=True)
    sums = {
        p: jnp.broadcast_to(spread[n:n + 1], tile) for n, p in enumerate(PAIRS)
    }
    surface_by, scaled_by = solve(sums)

    surface_by = [c[0:1] for c in surface_by]
    scaled_by = [c[0:1] for c in scaled_by]

    def final_rows(r, n, carry):
        at = pl.ds(r, n)
        to = pl.ds(pl.multiple_of(r - BASE, 8), n)
        x = [basis[k, 0, at, :] for k in range(ITERS + 1)]
        level_at = surface_by[0] * x[0]
        left = scaled_by[0] * x[0]
        for k in range(1, ITERS + 1):
            if k < ITERS:
                level_at = level_at + surface_by[k] * x[k]
            left = left + scaled_by[k] * x[k]
        surf[to, :] = level_at
        resid[to, :] = diag[at, :] * left
        return carry

    sweep("final", BASE, rows, FINAL_STEP, final_rows)
    out_surf = local_copy("out", surf, surf_out, out_sem.at[1])
    out_res = local_copy("out", resid, res_out, out_sem.at[2])
    out_surf.start()
    out_res.start()

    depth_sent()
    ends_sent()
    side_sent()
    for copy in sends:
        copy.wait_send()
    out_new.wait()
    out_surf.wait()
    out_res.wait()


def hand_over(new, surf, res, new_out, surf_out, res_out, cube, flat, in_sem, out_sem):
    pieces = [(surf, flat.at[0], surf_out), (res, flat.at[1], res_out)] + [
        (new.at[k], cube.at[k], new_out.at[k]) for k in range(LEVELS)]
    reads = [pltpu.make_async_copy(a, b, in_sem.at[n]) for n, (a, b, _) in enumerate(pieces)]
    writes = [pltpu.make_async_copy(b, c, out_sem.at[n]) for n, (_, b, c) in enumerate(pieces)]
    for read in reads:
        read.start()
    for read, write in zip(reads, writes):
        read.wait()
        write.start()
    for write in writes:
        write.wait()


def local(lon_count, lat_count, tracer, east_vel, north_vel, levels, forcing, storage):
    rows = tracer.shape[1]
    flat = (rows + 4 * GHOST, LANES)
    part = rows // PARTS
    f32 = jnp.float32
    extent = extents(lon_count, lat_count)
    sizes = [stage_size(extent, axes) for axes in STAGES]

    def vmem(*shape, dtype=f32):
        return pltpu.VMEM(shape, dtype)

    cube = vmem(LEVELS, rows + 2 * GHOST, LANES)
    pair = vmem(2, *flat)
    block = vmem(rows, LANES)
    beside = vmem(2 * part, LANES)
    edge = vmem(part, LANES)
    dma = pltpu.SemaphoreType.DMA
    anywhere = pl.BlockSpec(memory_space=pl.ANY)
    outs = (
        jax.ShapeDtypeStruct(tracer.shape, f32),
        jax.ShapeDtypeStruct(levels.shape, f32),
        jax.ShapeDtypeStruct(levels.shape, f32),
    )
    results = pl.pallas_call(
        functools.partial(kernel, lon_count, lat_count, rows),
        out_shape=outs,
        in_specs=[anywhere] * 6,
        out_specs=(anywhere,) * 3,
        scratch_shapes=[
            cube, cube, cube, vmem(rows, LANES, dtype=jnp.int32), block, pair, pair,
            beside, beside, beside, vmem(2, 2, 8, LANES), vmem(6, 2, 8, LANES),
            beside, beside, beside, vmem(2, 2, 8, LANES), vmem(2, 2, 8, LANES),
            vmem(6, 2, 8, LANES), vmem(8, LANES),
            edge, edge, edge, vmem(2, 8, LANES), vmem(6, 8, LANES),
            vmem(2 * part, LANES), vmem(2 * part, LANES), block, vmem(LEVELS, rows, LANES),
            pair, pair, pair, pair, pair, pair, pair, pair, vmem(*flat),
            vmem(ITERS + 1, 2, *flat),
            block, block,
            dma((6,)), dma((3, 6)), dma((3, 6)), dma((3, 2)), dma((3, 2)),
            dma((len(sizes), max(sizes))), dma((len(sizes), max(sizes))), dma((3,)),
            *[vmem(size, 1, LANES) for size in sizes],
        ],
        compiler_params=pltpu.CompilerParams(
            collective_id=0, has_side_effects=True, vmem_limit_bytes=61 * 2**20
        ),
        cost_estimate=pl.CostEstimate(flops=10**8, bytes_accessed=6 * 10**6, transcendentals=0),
        name="ocean_step",
    )(tracer, east_vel, north_vel, levels, forcing, storage)
    return pl.pallas_call(
        hand_over,
        out_shape=outs,
        in_specs=[anywhere] * 3,
        out_specs=(anywhere,) * 3,
        scratch_shapes=[
            vmem(*tracer.shape), vmem(2, rows, LANES),
            dma((LEVELS + 2,)), dma((LEVELS + 2,)),
        ],
        compiler_params=pltpu.CompilerParams(vmem_limit_bytes=61 * 2**20),
        name="hand_over",
    )(*results)


def solution(mesh):
    cube, flat = P(None, "lat", "lon"), P("lat", "lon")
    return jax.shard_map(
        functools.partial(local, mesh.shape["lon"], mesh.shape["lat"]),
        mesh=mesh,
        in_specs=(cube, cube, cube, flat, flat, flat),
        out_specs=(cube, flat, flat),
        check_vma=False,
    )
```

```python
import functools
import itertools

import jax
import jax.numpy as jnp
from jax import lax
from jax.experimental import pallas as pl
from jax.experimental.pallas import tpu as pltpu
from jax.sharding import PartitionSpec as P

ITERS = 5
LEVELS = 8
GHOST = 8
BASE = 2 * GHOST
LANES = 128
EDGE = 8
PARTS = 8
SCALE = 0.8
MESH = pl.DeviceIdType.MESH
STAGES = (("core", "y"), ("x", "z"))
TRACER_STEP = 32
WEIGHTS_STEP = 168
DIAGONAL_STEP = 48
SCALED_STEP = 336
APPLY_STEP = 168
LAST_STEP = 320
FINAL_STEP = 80

GAIN = (-1.0, 1.0 / SCALE, 2.0 / SCALE, 2.0 / SCALE, 2.0 / SCALE)
SHIFT = (1.0, 0.0, 0.0, 0.0, 0.0)
BACK = (0.0, 0.0, SCALE / 2, SCALE / 2, SCALE / 2)
PAIRS = tuple((i, j) for j in range(ITERS + 1) for i in range(j + 1) if (i, j) != (ITERS, ITERS))


def roll(x, shift):
    return pltpu.roll(x, shift % x.shape[-1], x.ndim - 1)


def lane_of(shape):
    return lax.broadcasted_iota(jnp.int32, shape, len(shape) - 1)


def row_of(shape):
    return lax.broadcasted_iota(jnp.int32, shape, len(shape) - 2)


def extents(lon_count, lat_count):
    z = min(4, lon_count // 2)
    return {"core": 2, "z": z, "x": lon_count // (2 * z), "y": lat_count}


def stage_size(extent, axes):
    size = 1
    for axis in axes:
        size *= extent[axis]
    return size


def sweep(name, first, rows, step, body, start=0):
    whole = rows // step

    def chunk(i, carry):
        return body(pl.multiple_of(first + i * step, 8), step, carry)

    carry = lax.fori_loop(0, whole, chunk, start) if whole else start
    if rows % step:
        carry = body(first + whole * step, rows % step, carry)
    return carry


def remote(name, src, dst, sent, received, device):
    return pltpu.make_async_remote_copy(
        src, dst, sent, received, device_id=device, device_id_type=MESH)


def local_copy(name, src, dst, done):
    return pltpu.make_async_copy(src, dst, done)


def step(name, run):
    run()


def arrived(name, part, received):
    pltpu.make_async_copy(part, part, received).wait()


def face_flux(here, there, vel_here, vel_there, shared, level):
    carried = (vel_here + vel_there) * (here + there)
    return jnp.where(shared > level, 1.92 * (there - here) - carried, 0.0)


def ring_east(main, strip, lane):
    a, b = roll(main, -1), roll(strip, -1)
    last = lane == LANES - 1
    return jnp.where(last, b, a), jnp.where(last, a, b)


def ring_west(main, strip, lane):
    a, b = roll(main, 1), roll(strip, 1)
    first = lane == 0
    return jnp.where(first, b, a), jnp.where(first, a, b)


def solve(gram):
    size = ITERS + 1

    def product(left, right):
        total = None
        for i, a in enumerate(left):
            if a is None:
                continue
            inner = None
            for j, b in enumerate(right):
                if b is None:
                    continue
                term = gram[min(i, j), max(i, j)] * b
                inner = term if inner is None else inner + term
            total = a * inner if total is None else total + a * inner
        return total

    def operate(coeffs):
        out = [None] * size

        def add(k, value):
            out[k] = value if out[k] is None else out[k] + value

        for k in range(ITERS):
            if coeffs[k] is None:
                continue
            add(k + 1, coeffs[k] * (-1.0 / GAIN[k]))
            if SHIFT[k] != 1.0:
                add(k, coeffs[k] * (1.0 - SHIFT[k]))
            if BACK[k] != 0.0:
                add(k - 1, coeffs[k] * (-BACK[k]))
        return out

    one = jnp.ones_like(gram[0, 0])
    scaled = [one] + [None] * ITERS
    direction = list(scaled)
    surface = [None] * size
    rho = product(scaled, scaled)
    for turn in range(ITERS):
        image = operate(direction)
        step = rho / product(direction, image)
        for k in range(size):
            if direction[k] is not None:
                move = step * direction[k]
                surface[k] = move if surface[k] is None else surface[k] + move
            if image[k] is not None:
                move = step * image[k]
                scaled[k] = -move if scaled[k] is None else scaled[k] - move
        if turn == ITERS - 1:
            break
        rho_new = product(scaled, scaled)
        ratio = rho_new / rho
        direction = [
            s if d is None else s + ratio * d for s, d in zip(scaled, direction)
        ]
        rho = rho_new
    return surface[:ITERS], scaled


def kernel(
    lon_count, lat_count, rows,
    t_in, u_in, v_in, lev_in, forc_in, stor_in,
    new_out, surf_out, res_out,
    tr, ur, vr, li, fo, lv, st,
    beside_out, beside_w, beside_e, rows_out, rows_in,
    ends_out, ends_w, ends_e, vel_out, vel_send, vel_in, folded_out,
    edge_out, edge_w, edge_e, edge_rows_out, edge_rows,
    flux, flux_sum, total, nt,
    w_e, w_n, w_ne, w_nw, w_er, w_ner, w_nwr, rdiag, diag, basis,
    surf, resid,
    in_sem, rows_send, rows_recv, beside_send, beside_recv, red_send, red_recv, out_sem, *boxes,
):
    lon, lat = lax.axis_index("lon"), lax.axis_index("lat")
    is_top = lat == lat_count - 1
    not_top = jnp.logical_not(is_top)
    not_bottom = lat > 0
    top = BASE + rows
    south = BASE - GHOST
    own = pl.ds(BASE, rows)
    inner = pl.ds(GHOST, rows)
    tile = (8, LANES)
    lane = lane_of(tile)
    row = row_of(tile)
    reach = rows + 2 * GHOST
    part = rows // PARTS

    def lanes(n):
        return lane_of((n, LANES))

    def row_is(r, n, which):
        return row_of((n, LANES)) + r == which

    loads = [
        local_copy("load", src, dst, in_sem.at[n]) for n, (src, dst) in enumerate((
            (lev_in, li), (stor_in, st.at[0, own, :]), (t_in, tr.at[:, inner, :]),
            (u_in, ur.at[:, inner, :]), (v_in, vr.at[:, inner, :]), (forc_in, fo),
        ))
    ]
    for load in loads:
        load.start()

    east = lax.rem(lon + 1, lon_count)
    west = lax.rem(lon + lon_count - 1, lon_count)
    up_lat = jnp.where(is_top, lat, lat + 1)
    down_lat = jnp.maximum(lat - 1, 0)
    up_lon = jnp.where(is_top, lon_count - 1 - lon, lon)
    up_e = jnp.where(is_top, lax.rem(2 * lon_count - 2 - lon, lon_count), east)
    up_w = jnp.where(is_top, lax.rem(lon_count - lon, lon_count), west)
    self_e = jnp.logical_and(is_top, up_e == lon)
    self_w = jnp.logical_and(is_top, up_w == lon)
    other_e, other_w = jnp.logical_not(self_e), jnp.logical_not(self_w)

    extent = extents(lon_count, lat_count)
    here_at = {
        "core": lax.rem(lon, 2),
        "z": lax.rem(lon // 2, extent["z"]),
        "x": lon // (2 * extent["z"]),
        "y": lat,
    }

    def stage_peers(axes):
        def index_of(at):
            index = 0
            for axis in axes:
                index = index * extent[axis] + at[axis]
            return index

        moves = sorted(
            itertools.product(*(range(extent[axis]) for axis in axes)),
            key=lambda move: -sum(min(d, extent[a] - d) for d, a in zip(move, axes)))
        peers = []
        for move in moves[:-1]:
            at = dict(here_at)
            for axis, d in zip(axes, move):
                at[axis] = lax.rem(here_at[axis] + d, extent[axis])
            device = {
                "lon": (at["x"] * extent["z"] + at["z"]) * 2 + at["core"], "lat": at["y"]}
            peers.append((index_of(at), device))
        place = index_of(here_at)
        return place, peers

    stages = [stage_peers(axes) for axes in STAGES]

    barrier = pltpu.get_barrier_semaphore()

    def greet(device):
        pl.semaphore_signal(barrier, inc=1, device_id=device, device_id_type=MESH)

    greet({"lon": east, "lat": lat})
    greet({"lon": west, "lat": lat})
    greet({"lon": up_lon, "lat": up_lat})

    @pl.when(other_e)
    def _():
        greet({"lon": up_e, "lat": up_lat})

    @pl.when(other_w)
    def _():
        greet({"lon": up_w, "lat": up_lat})

    @pl.when(not_bottom)
    def _():
        greet({"lon": lon, "lat": down_lat})
        greet({"lon": east, "lat": down_lat})
        greet({"lon": west, "lat": down_lat})

    greeted = 3
    for _, peers in stages:
        for _, device in peers:
            greet(device)
        greeted += len(peers)
    greeted = greeted + jnp.where(self_e, 0, 1) + jnp.where(self_w, 0, 1) + jnp.where(not_bottom, 3, 0)

    def fold(ranges):
        out = None
        for c, x in enumerate(ranges):
            moved = roll(x, EDGE + 16 * c)
            out = moved if out is None else jnp.where(lanes(part) // 16 == c, moved, out)
        return out

    def unfold(from_west, from_east):
        both = jnp.where(lanes(part) % 16 < EDGE, from_west, from_east)
        ends = jnp.logical_or(lanes(part) < EDGE, lanes(part) >= LANES - EDGE)
        return [
            jnp.where(ends, roll(both, -(EDGE + 16 * c)), 0.0) for c in range(PARTS)]

    def part_rows(c):
        return pl.ds(BASE + c * part, part)

    loads[0].wait()
    loads[1].wait()
    lv[0, own, :] = li[...].astype(jnp.float32)
    at_l, at_s = pl.ds(0, part), pl.ds(part, part)
    beside_out[at_l, :] = fold([lv[0, part_rows(c), :] for c in range(PARTS)])
    beside_out[at_s, :] = fold([st[0, part_rows(c), :] for c in range(PARTS)])
    edges = ((0, BASE, GHOST), (1, top - GHOST, GHOST + rows - 1))
    for side, r, _ in edges:
        rows_out[side, 0] = lv[0, pl.ds(r, GHOST), :]
        rows_out[side, 1] = st[0, pl.ds(r, GHOST), :]

    def exchange(phase, beside_from, to_east, to_west, rows_from, rows_to, corners, before=None):
        def by_rows(slot, side, place, to_lon, to_lat):
            return remote(
                "halo", rows_from.at[side], rows_to.at[place],
                rows_send.at[phase, slot], rows_recv.at[phase, place],
                {"lon": to_lon, "lat": to_lat})

        go_e = remote(
            "halo", beside_from, to_east, beside_send.at[phase, 0], beside_recv.at[phase, 0],
            {"lon": east, "lat": lat})
        go_w = remote(
            "halo", beside_from, to_west, beside_send.at[phase, 1], beside_recv.at[phase, 1],
            {"lon": west, "lat": lat})
        go_up = by_rows(0, 1, jnp.where(is_top, 3, 0), up_lon, up_lat)
        go_down = by_rows(3, 0, 3, lon, down_lat)
        if corners:
            go_up_e = by_rows(1, 1, jnp.where(is_top, 5, 1), up_e, up_lat)
            go_up_w = by_rows(2, 1, jnp.where(is_top, 4, 2), up_w, up_lat)
            go_down_e = by_rows(4, 0, 4, east, down_lat)
            go_down_w = by_rows(5, 0, 5, west, down_lat)
            stay_e = local_copy(
                "halo", rows_from.at[1], rows_to.at[5], rows_recv.at[phase, 5])
            stay_w = local_copy(
                "halo", rows_from.at[1], rows_to.at[4], rows_recv.at[phase, 4])
        go_e.start()
        go_w.start()
        if before is not None:
            before()
        if corners:
            pl.when(other_e)(go_up_e.start)
            pl.when(other_w)(go_up_w.start)
            pl.when(self_e)(stay_e.start)
            pl.when(self_w)(stay_w.start)

            @pl.when(not_bottom)
            def _():
                go_down_e.start()
                go_down_w.start()
        go_up.start()
        pl.when(not_bottom)(go_down.start)

        def sent():
            go_e.wait_send()
            go_w.wait_send()
            go_up.wait_send()
            pl.when(not_bottom)(go_down.wait_send)
            if corners:
                pl.when(other_e)(go_up_e.wait_send)
                pl.when(other_w)(go_up_w.wait_send)

                @pl.when(not_bottom)
                def _():
                    go_down_e.wait_send()
                    go_down_w.wait_send()

        def received():
            arrived("halo", to_east, beside_recv.at[phase, 0])
            arrived("halo", to_west, beside_recv.at[phase, 1])
            for place in (3, 4, 5) if corners else (3,):
                arrived("halo", rows_to.at[place], rows_recv.at[phase, place])

            @pl.when(not_bottom)
            def _():
                for place in (0, 1, 2) if corners else (0,):
                    arrived("halo", rows_to.at[place], rows_recv.at[phase, place])

        return sent, received

    loads[2].wait()
    loads[3].wait()

    def gather_ends(buffer, r, n):
        x = [buffer[k, pl.ds(r, n), :] for k in range(LEVELS)]
        lane = lanes(n)
        width = 2
        while len(x) > 1:
            window = jnp.logical_or(lane == 0, lane > LANES - width)
            x = [
                jnp.where(window, x[i + 1], roll(x[i], -width)) for i in range(0, len(x), 2)]
            width *= 2
        return x[0]

    def pack_ends(r, n, carry):
        out = None
        for c in range(PARTS // 2):
            for slot, buffer in enumerate((tr, ur)):
                moved = roll(gather_ends(buffer, GHOST + c * 2 * part + r, n), 32 * c + 16 * slot - 113)
                out = moved if out is None else jnp.where(
                    lanes(n) // 16 == 2 * c + slot, moved, out)
        ends_out[pl.ds(r, n), :] = out
        return carry

    sweep("ends", 0, 2 * part, 2 * part, pack_ends)
    def swap(x, bit, bits, axis):
        size = x.shape[axis]
        index = (lax.broadcasted_iota(jnp.int32, x.shape, axis) // bit) % bits
        out = None
        for p in range(bits):
            moved = pltpu.roll(x, ((2 * p - bits + 1) * bit) % size, axis)
            out = moved if out is None else jnp.where(index == p, moved, out)
        return out

    def mirror_lanes(x):
        for bit, bits in ((1, 4), (4, 4), (16, 4), (64, 2)):
            x = swap(x, bit, bits, 1)
        return x

    def mirror(x):
        return swap(mirror_lanes(x), 1, 8, 0)

    def end_rows():
        loads[4].wait()
        for side, _, r in edges:
            for k in range(LEVELS):
                vel_out[side, 0, pl.ds(k, 1), :] = tr[k, pl.ds(r, 1), :]
                vel_out[side, 1, pl.ds(k, 1), :] = vr[k, pl.ds(r, 1), :]

        @pl.when(is_top)
        def _():
            folded_out[...] = mirror_lanes(vel_out[1, 0])

        @pl.when(not_top)
        def _():
            folded_out[...] = vel_out[1, 0]

        vel_send[0] = vel_out[0]
        vel_send[1, 0] = folded_out[...]
        vel_send[1, 1] = vel_out[1, 1]

    pl.semaphore_wait(barrier, greeted)

    depth_sent, depth_received = exchange(
        0, beside_out, beside_w, beside_e, rows_out, rows_in, True)
    ends_sent, ends_received = exchange(
        1, ends_out, ends_w, ends_e, vel_send, vel_in, False, end_rows)

    nothing = jnp.zeros(tile, jnp.float32)
    for r in (south - 8, top + 8):
        at = pl.ds(r, 8)
        for half in range(2):
            for buffer in (lv, w_n, w_ne, w_nw):
                buffer[half, at, :] = nothing
            for k in range(ITERS + 1):
                basis[k, half, at, :] = nothing

    def tracer_rows(r, n, carry):
        at, up, down = pl.ds(r, n), pl.ds(r + 1, n), pl.ds(r - 1, n)
        wide, wide_up, wide_down = (pl.ds(r + GHOST + d, n) for d in (0, 1, -1))
        depth = lv[0, wide, :]
        open_e = jnp.where(
            lanes(n) == LANES - 1, 0.0, jnp.minimum(depth, roll(depth, -1)))
        open_n = jnp.where(
            row_is(r, n, GHOST + rows - 1), 0.0, jnp.minimum(depth, lv[0, wide_up, :]))
        open_s = jnp.where(
            row_is(r, n, GHOST), 0.0, jnp.minimum(depth, lv[0, wide_down, :]))
        below = None
        summed = None
        here = tr[0, at, :]
        for k in range(LEVELS):
            vel = vr[k, at, :]
            zonal = ur[k, at, :]
            flux_e = face_flux(here, roll(here, -1), zonal, roll(zonal, -1), open_e, k)
            flux_n = face_flux(here, tr[k, up, :], vel, vr[k, up, :], open_n, k)
            flux_s = face_flux(tr[k, down, :], here, vr[k, down, :], vel, open_s, k)
            change = 0.0625 * ((flux_e - roll(flux_e, 1)) + (flux_n - flux_s))
            result = here + change
            if below is not None:
                result = result - below
            if k + 1 < LEVELS:
                above = tr[k + 1, at, :]
                below = jnp.where(depth > k + 1, 0.1 * (above - here), 0.0)
                result = result + below
                here = above
            nt[k, pl.ds(r - GHOST, n), :] = result
            wet_part = jnp.where(depth > k, result, 0.0)
            summed = wet_part if summed is None else summed + wet_part
        total[pl.ds(r - GHOST, n), :] = summed
        return carry

    sweep("tracer", GHOST, rows, TRACER_STEP, tracer_rows)

    depth_received()

    def clear(buffer):
        for place in range(buffer.shape[0] // 2):
            buffer[place] = jnp.zeros(buffer.shape[1:], buffer.dtype)

    pl.when(jnp.logical_not(not_bottom))(lambda: clear(rows_in))

    @pl.when(is_top)
    def _():
        for place in (3, 4, 5):
            for field in range(2):
                rows_in[place, field] = mirror(rows_in[place, field])

    shared_n = jnp.minimum(rows_out[1, 0][7:8], rows_in[3, 0][0:1])
    shared_s = jnp.minimum(rows_out[0, 0][0:1], rows_in[0, 0][7:8])
    lane_p = lanes(part)
    even = lane_p % 2 == 0
    d_mine, d_w, d_e = (buffer[at_l, :] for buffer in (beside_out, beside_w, beside_e))
    both = jnp.where(
        lane_p % 16 == 7, jnp.minimum(d_mine, roll(d_e, -1)),
        jnp.where(lane_p % 16 == 8, jnp.minimum(roll(d_w, 1), d_mine), 0.0))
    for half in range(2):
        shared = jnp.where((lane_p // 16) % 2 == half, both, 0.0)
        shared = roll(shared, -7 - 16 * half)
        for shift in (2, 4, 8):
            shared = shared + roll(shared, shift)
        flux[pl.ds(half * part, part), :] = shared

    ends_received()
    pl.when(jnp.logical_not(not_bottom))(lambda: clear(vel_in))

    level_row = row.astype(jnp.float32)
    carry_north = jnp.where(is_top, 0.0, 1.0)
    own_first, own_last = vel_out[0], vel_out[1]
    flux_n = jnp.where(
        shared_n > level_row,
        0.0625 * (1.92 * (vel_in[3, 0] - own_last[0])
                  - carry_north * (own_last[1] + vel_in[3, 1]) * (own_last[0] + vel_in[3, 0])),
        0.0)
    flux_s = jnp.where(
        shared_s > level_row,
        0.0625 * (1.92 * (own_first[0] - vel_in[0, 0])
                  - (own_first[1] + vel_in[0, 1]) * (own_first[0] + vel_in[0, 0])),
        0.0)
    first_own, last_own = pl.ds(0, 8), pl.ds(rows - 8, 8)
    total[last_own, :] = total[last_own, :] + jnp.where(
        row == 7, jnp.sum(flux_n, axis=0, keepdims=True), 0.0)
    total[first_own, :] = total[first_own, :] - jnp.where(
        row == 0, jnp.sum(flux_s, axis=0, keepdims=True), 0.0)

    for half in range(2):
        at = pl.ds(half * part, part)
        mine, from_w, from_e = ends_out[at, :], ends_w[at, :], ends_e[at, :]
        here = jnp.where(even, mine, roll(from_w, 1))
        there = jnp.where(even, roll(from_e, -1), mine)
        carried = roll(here + there, -16) * (here + there)
        level = ((lane_p % 16) // 2).astype(jnp.float32)
        through = jnp.where(
            jnp.logical_and(flux[at, :] > level, lane_p % 32 < 16),
            0.0625 * (1.92 * (there - here) - carried), 0.0)
        through = jnp.where(even, through, -through)
        flux[at, :] = through
        for shift in (2, 4, 8):
            through = through + roll(through, -shift)
        flux_sum[at, :] = through

    def right_side(c):
        at = pl.ds(c * part, part)
        lane_p = lanes(part)
        ends = jnp.logical_or(lane_p == 0, lane_p == LANES - 1)
        across = roll(flux_sum[pl.ds((c % 2) * part, part), :], 127 - 32 * (c // 2))
        summed = total[at, :] + jnp.where(ends, across, 0.0)
        value = jnp.where(lv[0, part_rows(c), :] > 0.0, fo[at, :], 0.0) + summed * 8.0 ** -0.5
        basis[0, 0, part_rows(c), :] = value
        return value

    loads[5].wait()
    edge_out[...] = fold([right_side(c) for c in range(PARTS)])
    for side, r, _ in edges:
        edge_rows_out[side] = basis[0, 0, pl.ds(r, GHOST), :]
    side_sent, side_received = exchange(
        2, edge_out, edge_w, edge_e, edge_rows_out, edge_rows, True)

    def place_rows(buffer, get):
        for r, across, w_at, e_at in ((south, 0, 1, 2), (top, 3, 4, 5)):
            at = pl.ds(r, GHOST)
            buffer[0, at, :] = get(across)
            buffer[1, at, :] = jnp.where(
                lane < EDGE, get(e_at), jnp.where(lane >= LANES - EDGE, get(w_at), 0.0))

    for buffer, at, field in ((lv, at_l, 0), (st, at_s, 1)):
        for c, x in enumerate(unfold(beside_w[at, :], beside_e[at, :])):
            buffer[1, part_rows(c), :] = x
        place_rows(buffer, lambda place, field=field: rows_in[place, field])

    fold_row = jnp.where(is_top, top - 1, -1)

    def weigh(a, b):
        return a * b / (a + b + 1.0)

    def weights_rows(r, n, carry):
        at, up = pl.ds(r, n), pl.ds(r + 1, n)
        lane = lanes(n)
        d_m, d_s = lv[0, at, :], lv[1, at, :]
        n_m, n_s = lv[0, up, :], lv[1, up, :]
        e_m, e_s = ring_east(d_m, d_s, lane)
        ne_m, ne_s = ring_east(n_m, n_s, lane)
        nw_m, nw_s = ring_west(n_m, n_s, lane)
        corner = jnp.where(row_is(r, n, fold_row), 0.0, 0.25)
        east_m, east_s = weigh(d_m, e_m), weigh(d_s, e_s)
        neast_m, neast_s = corner * weigh(d_m, ne_m), corner * weigh(d_s, ne_s)
        nwest_m, nwest_s = corner * weigh(d_m, nw_m), corner * weigh(d_s, nw_s)
        w_e[0, at, :], w_e[1, at, :] = east_m, east_s
        w_n[0, at, :], w_n[1, at, :] = weigh(d_m, n_m), weigh(d_s, n_s)
        w_ne[0, at, :], w_ne[1, at, :] = neast_m, neast_s
        w_nw[0, at, :], w_nw[1, at, :] = nwest_m, nwest_s
        w_er[0, at, :], w_er[1, at, :] = ring_west(east_m, east_s, lane)
        w_ner[0, at, :], w_ner[1, at, :] = ring_west(neast_m, neast_s, lane)
        w_nwr[0, at, :], w_nwr[1, at, :] = ring_east(nwest_m, nwest_s, lane)
        return carry

    sweep("weights", south, reach, WEIGHTS_STEP, weights_rows)

    def diagonal_rows(r, n, carry):
        at, down = pl.ds(r, n), pl.ds(r - 1, n)
        for half in range(2):
            whole = (
                st[half, at, :] + w_e[half, at, :] + w_er[half, at, :] + w_n[half, at, :]
                + w_n[half, down, :] + w_ne[half, at, :] + w_nw[half, at, :]
                + w_ner[half, down, :] + w_nwr[half, down, :])
            rdiag[half, at, :] = jnp.where(whole > 0.0, 1.0 / whole, 0.0)
            if half == 0:
                diag[at, :] = whole
        return carry

    sweep("diagonal", south, reach, DIAGONAL_STEP, diagonal_rows)
    diag[pl.ds(south, GHOST), :] = nothing
    diag[pl.ds(top, GHOST), :] = nothing

    def ends_rows(r, n, carry):
        lane = lanes(n)
        ends = jnp.logical_or(lane == 0, lane == LANES - 1)
        across = flux[pl.ds(r, n), :]
        for c in range(PARTS // 2):
            at = pl.ds(c * 2 * part + r, n)
            for k in range(LEVELS):
                nt[k, at, :] = nt[k, at, :] + jnp.where(
                    ends, roll(across, 127 - 32 * c - 2 * k), 0.0)
        return carry

    sweep("new", 0, 2 * part, part, ends_rows)
    for k in range(LEVELS):
        nt[k, last_own, :] = nt[k, last_own, :] + jnp.where(row == 7, flux_n[k:k + 1], 0.0)
        nt[k, first_own, :] = nt[k, first_own, :] - jnp.where(row == 0, flux_s[k:k + 1], 0.0)
    out_new = local_copy("out", nt, new_out, out_sem.at[0])
    out_new.start()

    side_received()
    pl.when(jnp.logical_not(not_bottom))(lambda: clear(edge_rows))

    @pl.when(is_top)
    def _():
        for place in (3, 4, 5):
            edge_rows[place] = mirror(edge_rows[place])

    for c, x in enumerate(unfold(edge_w[...], edge_e[...])):
        basis[0, 1, part_rows(c), :] = x
    place_rows(basis.at[0], lambda place: edge_rows[place])

    gram = {}

    def fold_rows(x):
        return jnp.sum(x.reshape(x.shape[0] // 8, 8, LANES), axis=0)

    def scaled_rows(r, n, acc):
        at = pl.ds(r, n)
        for half in range(2):
            x = basis[0, half, at, :]
            y = x * rdiag[half, at, :]
            basis[0, half, at, :] = y
            if half == 0:
                acc = acc + fold_rows(diag[at, :] * y * y)
        return acc

    gram[0, 0] = sweep("scaled", south, reach, SCALED_STEP, scaled_rows, nothing)

    def neighbours_sum(k, r, n, halves):
        at, up, down = pl.ds(r, n), pl.ds(r + 1, n), pl.ds(r - 1, n)
        lane = lanes(n)
        sums, to_west, to_east = [], [], []
        for half in range(2):
            x = basis[k, half, at, :]
            x_n = basis[k, half, up, :]
            x_s = basis[k, half, down, :]
            to_east.append(
                w_e[half, at, :] * x + w_ne[half, down, :] * x_s + w_nwr[half, at, :] * x_n)
            to_west.append(
                w_er[half, at, :] * x + w_nw[half, down, :] * x_s + w_ner[half, at, :] * x_n)
            if half < halves:
                sums.append(w_n[half, at, :] * x_n + w_n[half, down, :] * x_s)
        from_west = ring_west(to_east[0], to_east[1], lane)
        from_east = ring_east(to_west[0], to_west[1], lane)
        return [sums[h] + from_west[h] + from_east[h] for h in range(halves)]

    def apply_rows(k, r, n, halves):
        at = pl.ds(r, n)
        sums = neighbours_sum(k, r, n, halves)
        out = []
        for half in range(halves):
            x = basis[k, half, at, :]
            y = rdiag[half, at, :] * sums[half]
            if SHIFT[k] != 0.0:
                y = y - SHIFT[k] * x
            if BACK[k] != 0.0:
                y = y - BACK[k] * basis[k - 1, half, at, :]
            y = GAIN[k] * y
            basis[k + 1, half, at, :] = y
            out.append(y)
        return out[0]

    for k in range(ITERS):
        last = k == ITERS - 1
        terms = [p for p in PAIRS if p[1] == k + 1]

        def apply_own(r, n, accs, k=k, terms=terms, halves=1 if last else 2):
            at = pl.ds(r, n)
            y = apply_rows(k, r, n, halves)
            scaled = diag[at, :] * y
            return tuple(
                acc + fold_rows(scaled * (y if a == k + 1 else basis[a, 0, at, :]))
                for acc, (a, _) in zip(accs, terms))

        sums = sweep(
            "apply", BASE if last else south, rows if last else reach,
            LAST_STEP if last else APPLY_STEP, apply_own, tuple(nothing for _ in terms))
        for p, s in zip(terms, sums):
            gram[p] = s

    per_lane = [jnp.sum(gram[p], axis=0, keepdims=True) for p in PAIRS]
    per_lane = per_lane + [jnp.zeros((1, LANES), jnp.float32)] * (24 - len(per_lane))
    stacked = jnp.sum(jnp.concatenate(per_lane, axis=0), axis=1, keepdims=True)
    count = stacked.shape[0]
    own_lane = lane_of((count, LANES)) == row_of((count, LANES))
    summed = jnp.sum(jnp.where(own_lane, stacked, 0.0), axis=0, keepdims=True)

    sends = []
    for stage, (place, peers) in enumerate(stages):
        box = boxes[stage]
        box[pl.ds(place, 1), :, :] = summed[None]
        for n, (_, device) in enumerate(peers):
            copy = remote(
                "red", box.at[place], box.at[place],
                red_send.at[stage, n], red_recv.at[stage, place], device)
            copy.start()
            sends.append(copy)
        for index, _ in peers:
            arrived("red", box.at[index], red_recv.at[stage, index])
        summed = box[0]
        for n in range(1, len(peers) + 1):
            summed = summed + box[n]

    spread = jnp.sum(
        jnp.where(own_lane, jnp.broadcast_to(summed, (count, LANES)), 0.0),
        axis=1, keepdims=True)
    sums = {
        p: jnp.broadcast_to(spread[n:n + 1], tile) for n, p in enumerate(PAIRS)
    }
    surface_by, scaled_by = solve(sums)

    surface_by = [c[0:1] for c in surface_by]
    scaled_by = [c[0:1] for c in scaled_by]

    def final_rows(r, n, carry):
        at = pl.ds(r, n)
        to = pl.ds(pl.multiple_of(r - BASE, 8), n)
        x = [basis[k, 0, at, :] for k in range(ITERS + 1)]
        level_at = surface_by[0] * x[0]
        left = scaled_by[0] * x[0]
        for k in range(1, ITERS + 1):
            if k < ITERS:
                level_at = level_at + surface_by[k] * x[k]
            left = left + scaled_by[k] * x[k]
        surf[to, :] = level_at
        resid[to, :] = diag[at, :] * left
        return carry

    sweep("final", BASE, rows, FINAL_STEP, final_rows)
    out_surf = local_copy("out", surf, surf_out, out_sem.at[1])
    out_res = local_copy("out", resid, res_out, out_sem.at[2])
    out_surf.start()
    out_res.start()

    depth_sent()
    ends_sent()
    side_sent()
    for copy in sends:
        copy.wait_send()
    out_new.wait()
    out_surf.wait()
    out_res.wait()


def hand_over(new, surf, res, new_out, surf_out, res_out, cube, flat, in_sem, out_sem):
    pieces = [(surf, flat.at[0], surf_out), (res, flat.at[1], res_out)] + [
        (new.at[k], cube.at[k], new_out.at[k]) for k in range(LEVELS)]
    reads = [pltpu.make_async_copy(a, b, in_sem.at[n]) for n, (a, b, _) in enumerate(pieces)]
    writes = [pltpu.make_async_copy(b, c, out_sem.at[n]) for n, (_, b, c) in enumerate(pieces)]
    for read in reads:
        read.start()
    for read, write in zip(reads, writes):
        read.wait()
        write.start()
    for write in writes:
        write.wait()


def local(lon_count, lat_count, tracer, east_vel, north_vel, levels, forcing, storage):
    rows = tracer.shape[1]
    flat = (rows + 4 * GHOST, LANES)
    part = rows // PARTS
    f32 = jnp.float32
    extent = extents(lon_count, lat_count)
    sizes = [stage_size(extent, axes) for axes in STAGES]

    def vmem(*shape, dtype=f32):
        return pltpu.VMEM(shape, dtype)

    cube = vmem(LEVELS, rows + 2 * GHOST, LANES)
    pair = vmem(2, *flat)
    block = vmem(rows, LANES)
    beside = vmem(2 * part, LANES)
    edge = vmem(part, LANES)
    dma = pltpu.SemaphoreType.DMA
    anywhere = pl.BlockSpec(memory_space=pl.ANY)
    outs = (
        jax.ShapeDtypeStruct(tracer.shape, f32),
        jax.ShapeDtypeStruct(levels.shape, f32),
        jax.ShapeDtypeStruct(levels.shape, f32),
    )
    results = pl.pallas_call(
        functools.partial(kernel, lon_count, lat_count, rows),
        out_shape=outs,
        in_specs=[anywhere] * 6,
        out_specs=(anywhere,) * 3,
        scratch_shapes=[
            cube, cube, cube, vmem(rows, LANES, dtype=jnp.int32), block, pair, pair,
            beside, beside, beside, vmem(2, 2, 8, LANES), vmem(6, 2, 8, LANES),
            beside, beside, beside, vmem(2, 2, 8, LANES), vmem(2, 2, 8, LANES),
            vmem(6, 2, 8, LANES), vmem(8, LANES),
            edge, edge, edge, vmem(2, 8, LANES), vmem(6, 8, LANES),
            vmem(2 * part, LANES), vmem(2 * part, LANES), block, vmem(LEVELS, rows, LANES),
            pair, pair, pair, pair, pair, pair, pair, pair, vmem(*flat),
            vmem(ITERS + 1, 2, *flat),
            block, block,
            dma((6,)), dma((3, 6)), dma((3, 6)), dma((3, 2)), dma((3, 2)),
            dma((len(sizes), max(sizes))), dma((len(sizes), max(sizes))), dma((3,)),
            *[vmem(size, 1, LANES) for size in sizes],
        ],
        compiler_params=pltpu.CompilerParams(
            collective_id=0, has_side_effects=True, vmem_limit_bytes=61 * 2**20
        ),
        cost_estimate=pl.CostEstimate(flops=10**8, bytes_accessed=6 * 10**6, transcendentals=0),
        name="ocean_step",
    )(tracer, east_vel, north_vel, levels, forcing, storage)
    return pl.pallas_call(
        hand_over,
        out_shape=outs,
        in_specs=[anywhere] * 3,
        out_specs=(anywhere,) * 3,
        scratch_shapes=[
            vmem(*tracer.shape), vmem(2, rows, LANES),
            dma((LEVELS + 2,)), dma((LEVELS + 2,)),
        ],
        compiler_params=pltpu.CompilerParams(vmem_limit_bytes=61 * 2**20),
        name="hand_over",
    )(*results)


def solution(mesh):
    cube, flat = P(None, "lat", "lon"), P("lat", "lon")
    return jax.shard_map(
        functools.partial(local, mesh.shape["lon"], mesh.shape["lat"]),
        mesh=mesh,
        in_specs=(cube, cube, cube, flat, flat, flat),
        out_specs=(cube, flat, flat),
        check_vma=False,
    )
```

```python
import functools
import itertools

import jax
import jax.numpy as jnp
from jax import lax
from jax.experimental import pallas as pl
from jax.experimental.pallas import tpu as pltpu
from jax.sharding import PartitionSpec as P

ITERS = 5
LEVELS = 8
GHOST = 8
BASE = 2 * GHOST
LANES = 128
EDGE = 8
PARTS = 8
SCALE = 0.8
MESH = pl.DeviceIdType.MESH
STAGES = (("core", "y"), ("x", "z"))
TRACER_STEP = 32
WEIGHTS_STEP = 168
DIAGONAL_STEP = 168
SCALED_STEP = 336
APPLY_STEP = 336
LAST_STEP = 320
FINAL_STEP = 320

GAIN = (-1.0, 1.0 / SCALE, 2.0 / SCALE, 2.0 / SCALE, 2.0 / SCALE)
SHIFT = (1.0, 0.0, 0.0, 0.0, 0.0)
BACK = (0.0, 0.0, SCALE / 2, SCALE / 2, SCALE / 2)
PAIRS = tuple((i, j) for j in range(ITERS + 1) for i in range(j + 1) if (i, j) != (ITERS, ITERS))


def roll(x, shift):
    return pltpu.roll(x, shift % x.shape[-1], x.ndim - 1)


def lane_of(shape):
    return lax.broadcasted_iota(jnp.int32, shape, len(shape) - 1)


def row_of(shape):
    return lax.broadcasted_iota(jnp.int32, shape, len(shape) - 2)


def extents(lon_count, lat_count):
    z = min(4, lon_count // 2)
    return {"core": 2, "z": z, "x": lon_count // (2 * z), "y": lat_count}


def stage_size(extent, axes):
    size = 1
    for axis in axes:
        size *= extent[axis]
    return size


def sweep(name, first, rows, step, body, start=0):
    whole = rows // step

    def chunk(i, carry):
        return body(pl.multiple_of(first + i * step, 8), step, carry)

    carry = lax.fori_loop(0, whole, chunk, start) if whole else start
    if rows % step:
        carry = body(first + whole * step, rows % step, carry)
    return carry


def remote(name, src, dst, sent, received, device):
    return pltpu.make_async_remote_copy(
        src, dst, sent, received, device_id=device, device_id_type=MESH)


def local_copy(name, src, dst, done):
    return pltpu.make_async_copy(src, dst, done)


def step(name, run):
    run()


def arrived(name, part, received):
    pltpu.make_async_copy(part, part, received).wait()


def face_flux(here, there, vel_here, vel_there, shared, level):
    carried = (vel_here + vel_there) * (here + there)
    return jnp.where(shared > level, 1.92 * (there - here) - carried, 0.0)


def ring_east(main, strip, lane):
    a, b = roll(main, -1), roll(strip, -1)
    last = lane == LANES - 1
    return jnp.where(last, b, a), jnp.where(last, a, b)


def ring_west(main, strip, lane):
    a, b = roll(main, 1), roll(strip, 1)
    first = lane == 0
    return jnp.where(first, b, a), jnp.where(first, a, b)


def solve(gram):
    size = ITERS + 1

    def product(left, right):
        total = None
        for i, a in enumerate(left):
            if a is None:
                continue
            inner = None
            for j, b in enumerate(right):
                if b is None:
                    continue
                term = gram[min(i, j), max(i, j)] * b
                inner = term if inner is None else inner + term
            total = a * inner if total is None else total + a * inner
        return total

    def operate(coeffs):
        out = [None] * size

        def add(k, value):
            out[k] = value if out[k] is None else out[k] + value

        for k in range(ITERS):
            if coeffs[k] is None:
                continue
            add(k + 1, coeffs[k] * (-1.0 / GAIN[k]))
            if SHIFT[k] != 1.0:
                add(k, coeffs[k] * (1.0 - SHIFT[k]))
            if BACK[k] != 0.0:
                add(k - 1, coeffs[k] * (-BACK[k]))
        return out

    one = jnp.ones_like(gram[0, 0])
    scaled = [one] + [None] * ITERS
    direction = list(scaled)
    surface = [None] * size
    rho = product(scaled, scaled)
    for turn in range(ITERS):
        image = operate(direction)
        step = rho / product(direction, image)
        for k in range(size):
            if direction[k] is not None:
                move = step * direction[k]
                surface[k] = move if surface[k] is None else surface[k] + move
            if image[k] is not None:
                move = step * image[k]
                scaled[k] = -move if scaled[k] is None else scaled[k] - move
        if turn == ITERS - 1:
            break
        rho_new = product(scaled, scaled)
        ratio = rho_new / rho
        direction = [
            s if d is None else s + ratio * d for s, d in zip(scaled, direction)
        ]
        rho = rho_new
    return surface[:ITERS], scaled


def kernel(
    lon_count, lat_count, rows,
    t_in, u_in, v_in, lev_in, forc_in, stor_in,
    new_out, surf_out, res_out,
    tr, ur, vr, li, fo, lv, st,
    beside_out, beside_w, beside_e, rows_out, rows_in,
    ends_out, ends_w, ends_e, vel_out, vel_send, vel_in, folded_out,
    edge_out, edge_w, edge_e, edge_rows_out, edge_rows,
    flux, flux_sum, total, nt,
    w_e, w_n, w_ne, w_nw, w_er, w_ner, w_nwr, rdiag, diag, basis,
    surf, resid,
    in_sem, rows_send, rows_recv, beside_send, beside_recv, red_send, red_recv, out_sem, *boxes,
):
    lon, lat = lax.axis_index("lon"), lax.axis_index("lat")
    is_top = lat == lat_count - 1
    not_top = jnp.logical_not(is_top)
    not_bottom = lat > 0
    top = BASE + rows
    south = BASE - GHOST
    own = pl.ds(BASE, rows)
    inner = pl.ds(GHOST, rows)
    tile = (8, LANES)
    lane = lane_of(tile)
    row = row_of(tile)
    reach = rows + 2 * GHOST
    part = rows // PARTS

    def lanes(n):
        return lane_of((n, LANES))

    def row_is(r, n, which):
        return row_of((n, LANES)) + r == which

    loads = [
        local_copy("load", src, dst, in_sem.at[n]) for n, (src, dst) in enumerate((
            (lev_in, li), (stor_in, st.at[0, own, :]), (t_in, tr.at[:, inner, :]),
            (u_in, ur.at[:, inner, :]), (v_in, vr.at[:, inner, :]), (forc_in, fo),
        ))
    ]
    for load in loads:
        load.start()

    east = lax.rem(lon + 1, lon_count)
    west = lax.rem(lon + lon_count - 1, lon_count)
    up_lat = jnp.where(is_top, lat, lat + 1)
    down_lat = jnp.maximum(lat - 1, 0)
    up_lon = jnp.where(is_top, lon_count - 1 - lon, lon)
    up_e = jnp.where(is_top, lax.rem(2 * lon_count - 2 - lon, lon_count), east)
    up_w = jnp.where(is_top, lax.rem(lon_count - lon, lon_count), west)
    self_e = jnp.logical_and(is_top, up_e == lon)
    self_w = jnp.logical_and(is_top, up_w == lon)
    other_e, other_w = jnp.logical_not(self_e), jnp.logical_not(self_w)

    extent = extents(lon_count, lat_count)
    here_at = {
        "core": lax.rem(lon, 2),
        "z": lax.rem(lon // 2, extent["z"]),
        "x": lon // (2 * extent["z"]),
        "y": lat,
    }

    def stage_peers(axes):
        def index_of(at):
            index = 0
            for axis in axes:
                index = index * extent[axis] + at[axis]
            return index

        moves = sorted(
            itertools.product(*(range(extent[axis]) for axis in axes)),
            key=lambda move: -sum(min(d, extent[a] - d) for d, a in zip(move, axes)))
        peers = []
        for move in moves[:-1]:
            at = dict(here_at)
            for axis, d in zip(axes, move):
                at[axis] = lax.rem(here_at[axis] + d, extent[axis])
            device = {
                "lon": (at["x"] * extent["z"] + at["z"]) * 2 + at["core"], "lat": at["y"]}
            peers.append((index_of(at), device))
        place = index_of(here_at)
        return place, peers

    stages = [stage_peers(axes) for axes in STAGES]

    barrier = pltpu.get_barrier_semaphore()

    def greet(device):
        pl.semaphore_signal(barrier, inc=1, device_id=device, device_id_type=MESH)

    greet({"lon": east, "lat": lat})
    greet({"lon": west, "lat": lat})
    greet({"lon": up_lon, "lat": up_lat})

    @pl.when(other_e)
    def _():
        greet({"lon": up_e, "lat": up_lat})

    @pl.when(other_w)
    def _():
        greet({"lon": up_w, "lat": up_lat})

    @pl.when(not_bottom)
    def _():
        greet({"lon": lon, "lat": down_lat})
        greet({"lon": east, "lat": down_lat})
        greet({"lon": west, "lat": down_lat})

    greeted = 3
    for _, peers in stages:
        for _, device in peers:
            greet(device)
        greeted += len(peers)
    greeted = greeted + jnp.where(self_e, 0, 1) + jnp.where(self_w, 0, 1) + jnp.where(not_bottom, 3, 0)

    def fold(ranges):
        out = None
        for c, x in enumerate(ranges):
            moved = roll(x, EDGE + 16 * c)
            out = moved if out is None else jnp.where(lanes(part) // 16 == c, moved, out)
        return out

    def unfold(from_west, from_east):
        both = jnp.where(lanes(part) % 16 < EDGE, from_west, from_east)
        ends = jnp.logical_or(lanes(part) < EDGE, lanes(part) >= LANES - EDGE)
        return [
            jnp.where(ends, roll(both, -(EDGE + 16 * c)), 0.0) for c in range(PARTS)]

    def part_rows(c):
        return pl.ds(BASE + c * part, part)

    loads[0].wait()
    loads[1].wait()
    lv[0, own, :] = li[...].astype(jnp.float32)
    at_l, at_s = pl.ds(0, part), pl.ds(part, part)
    beside_out[at_l, :] = fold([lv[0, part_rows(c), :] for c in range(PARTS)])
    beside_out[at_s, :] = fold([st[0, part_rows(c), :] for c in range(PARTS)])
    edges = ((0, BASE, GHOST), (1, top - GHOST, GHOST + rows - 1))
    for side, r, _ in edges:
        rows_out[side, 0] = lv[0, pl.ds(r, GHOST), :]
        rows_out[side, 1] = st[0, pl.ds(r, GHOST), :]

    def exchange(phase, beside_from, to_east, to_west, rows_from, rows_to, corners, before=None):
        def by_rows(slot, side, place, to_lon, to_lat):
            return remote(
                "halo", rows_from.at[side], rows_to.at[place],
                rows_send.at[phase, slot], rows_recv.at[phase, place],
                {"lon": to_lon, "lat": to_lat})

        go_e = remote(
            "halo", beside_from, to_east, beside_send.at[phase, 0], beside_recv.at[phase, 0],
            {"lon": east, "lat": lat})
        go_w = remote(
            "halo", beside_from, to_west, beside_send.at[phase, 1], beside_recv.at[phase, 1],
            {"lon": west, "lat": lat})
        go_up = by_rows(0, 1, jnp.where(is_top, 3, 0), up_lon, up_lat)
        go_down = by_rows(3, 0, 3, lon, down_lat)
        if corners:
            go_up_e = by_rows(1, 1, jnp.where(is_top, 5, 1), up_e, up_lat)
            go_up_w = by_rows(2, 1, jnp.where(is_top, 4, 2), up_w, up_lat)
            go_down_e = by_rows(4, 0, 4, east, down_lat)
            go_down_w = by_rows(5, 0, 5, west, down_lat)
            stay_e = local_copy(
                "halo", rows_from.at[1], rows_to.at[5], rows_recv.at[phase, 5])
            stay_w = local_copy(
                "halo", rows_from.at[1], rows_to.at[4], rows_recv.at[phase, 4])
        go_e.start()
        go_w.start()
        if before is not None:
            before()
        if corners:
            pl.when(other_e)(go_up_e.start)
            pl.when(other_w)(go_up_w.start)
            pl.when(self_e)(stay_e.start)
            pl.when(self_w)(stay_w.start)

            @pl.when(not_bottom)
            def _():
                go_down_e.start()
                go_down_w.start()
        go_up.start()
        pl.when(not_bottom)(go_down.start)

        def sent():
            go_e.wait_send()
            go_w.wait_send()
            go_up.wait_send()
            pl.when(not_bottom)(go_down.wait_send)
            if corners:
                pl.when(other_e)(go_up_e.wait_send)
                pl.when(other_w)(go_up_w.wait_send)

                @pl.when(not_bottom)
                def _():
                    go_down_e.wait_send()
                    go_down_w.wait_send()

        def received():
            arrived("halo", to_east, beside_recv.at[phase, 0])
            arrived("halo", to_west, beside_recv.at[phase, 1])
            for place in (3, 4, 5) if corners else (3,):
                arrived("halo", rows_to.at[place], rows_recv.at[phase, place])

            @pl.when(not_bottom)
            def _():
                for place in (0, 1, 2) if corners else (0,):
                    arrived("halo", rows_to.at[place], rows_recv.at[phase, place])

        return sent, received

    loads[2].wait()
    loads[3].wait()

    def gather_ends(buffer, r, n):
        x = [buffer[k, pl.ds(r, n), :] for k in range(LEVELS)]
        lane = lanes(n)
        width = 2
        while len(x) > 1:
            window = jnp.logical_or(lane == 0, lane > LANES - width)
            x = [
                jnp.where(window, x[i + 1], roll(x[i], -width)) for i in range(0, len(x), 2)]
            width *= 2
        return x[0]

    def pack_ends(r, n, carry):
        out = None
        for c in range(PARTS // 2):
            for slot, buffer in enumerate((tr, ur)):
                moved = roll(gather_ends(buffer, GHOST + c * 2 * part + r, n), 32 * c + 16 * slot - 113)
                out = moved if out is None else jnp.where(
                    lanes(n) // 16 == 2 * c + slot, moved, out)
        ends_out[pl.ds(r, n), :] = out
        return carry

    sweep("ends", 0, 2 * part, 2 * part, pack_ends)
    def swap(x, bit, bits, axis):
        size = x.shape[axis]
        index = (lax.broadcasted_iota(jnp.int32, x.shape, axis) // bit) % bits
        out = None
        for p in range(bits):
            moved = pltpu.roll(x, ((2 * p - bits + 1) * bit) % size, axis)
            out = moved if out is None else jnp.where(index == p, moved, out)
        return out

    def mirror_lanes(x):
        for bit, bits in ((1, 4), (4, 4), (16, 4), (64, 2)):
            x = swap(x, bit, bits, 1)
        return x

    def mirror(x):
        return swap(mirror_lanes(x), 1, 8, 0)

    def end_rows():
        loads[4].wait()
        for side, _, r in edges:
            for k in range(LEVELS):
                vel_out[side, 0, pl.ds(k, 1), :] = tr[k, pl.ds(r, 1), :]
                vel_out[side, 1, pl.ds(k, 1), :] = vr[k, pl.ds(r, 1), :]

        @pl.when(is_top)
        def _():
            folded_out[...] = mirror_lanes(vel_out[1, 0])

        @pl.when(not_top)
        def _():
            folded_out[...] = vel_out[1, 0]

        vel_send[0] = vel_out[0]
        vel_send[1, 0] = folded_out[...]
        vel_send[1, 1] = vel_out[1, 1]

    pl.semaphore_wait(barrier, greeted)

    depth_sent, depth_received = exchange(
        0, beside_out, beside_w, beside_e, rows_out, rows_in, True)
    ends_sent, ends_received = exchange(
        1, ends_out, ends_w, ends_e, vel_send, vel_in, False, end_rows)

    nothing = jnp.zeros(tile, jnp.float32)
    for r in (south - 8, top + 8):
        at = pl.ds(r, 8)
        for half in range(2):
            for buffer in (lv, w_n, w_ne, w_nw):
                buffer[half, at, :] = nothing
            for k in range(ITERS + 1):
                basis[k, half, at, :] = nothing

    def tracer_rows(r, n, carry):
        at, up, down = pl.ds(r, n), pl.ds(r + 1, n), pl.ds(r - 1, n)
        wide, wide_up, wide_down = (pl.ds(r + GHOST + d, n) for d in (0, 1, -1))
        depth = lv[0, wide, :]
        open_e = jnp.where(
            lanes(n) == LANES - 1, 0.0, jnp.minimum(depth, roll(depth, -1)))
        open_n = jnp.where(
            row_is(r, n, GHOST + rows - 1), 0.0, jnp.minimum(depth, lv[0, wide_up, :]))
        open_s = jnp.where(
            row_is(r, n, GHOST), 0.0, jnp.minimum(depth, lv[0, wide_down, :]))
        below = None
        summed = None
        here = tr[0, at, :]
        for k in range(LEVELS):
            vel = vr[k, at, :]
            zonal = ur[k, at, :]
            flux_e = face_flux(here, roll(here, -1), zonal, roll(zonal, -1), open_e, k)
            flux_n = face_flux(here, tr[k, up, :], vel, vr[k, up, :], open_n, k)
            flux_s = face_flux(tr[k, down, :], here, vr[k, down, :], vel, open_s, k)
            change = 0.0625 * ((flux_e - roll(flux_e, 1)) + (flux_n - flux_s))
            result = here + change
            if below is not None:
                result = result - below
            if k + 1 < LEVELS:
                above = tr[k + 1, at, :]
                below = jnp.where(depth > k + 1, 0.1 * (above - here), 0.0)
                result = result + below
                here = above
            nt[k, pl.ds(r - GHOST, n), :] = result
            wet_part = jnp.where(depth > k, result, 0.0)
            summed = wet_part if summed is None else summed + wet_part
        total[pl.ds(r - GHOST, n), :] = summed
        return carry

    sweep("tracer", GHOST, rows, TRACER_STEP, tracer_rows)

    depth_received()

    def clear(buffer):
        for place in range(buffer.shape[0] // 2):
            buffer[place] = jnp.zeros(buffer.shape[1:], buffer.dtype)

    pl.when(jnp.logical_not(not_bottom))(lambda: clear(rows_in))

    @pl.when(is_top)
    def _():
        for place in (3, 4, 5):
            for field in range(2):
                rows_in[place, field] = mirror(rows_in[place, field])

    shared_n = jnp.minimum(rows_out[1, 0][7:8], rows_in[3, 0][0:1])
    shared_s = jnp.minimum(rows_out[0, 0][0:1], rows_in[0, 0][7:8])
    lane_p = lanes(part)
    even = lane_p % 2 == 0
    d_mine, d_w, d_e = (buffer[at_l, :] for buffer in (beside_out, beside_w, beside_e))
    both = jnp.where(
        lane_p % 16 == 7, jnp.minimum(d_mine, roll(d_e, -1)),
        jnp.where(lane_p % 16 == 8, jnp.minimum(roll(d_w, 1), d_mine), 0.0))
    for half in range(2):
        shared = jnp.where((lane_p // 16) % 2 == half, both, 0.0)
        shared = roll(shared, -7 - 16 * half)
        for shift in (2, 4, 8):
            shared = shared + roll(shared, shift)
        flux[pl.ds(half * part, part), :] = shared

    ends_received()
    pl.when(jnp.logical_not(not_bottom))(lambda: clear(vel_in))

    level_row = row.astype(jnp.float32)
    carry_north = jnp.where(is_top, 0.0, 1.0)
    own_first, own_last = vel_out[0], vel_out[1]
    flux_n = jnp.where(
        shared_n > level_row,
        0.0625 * (1.92 * (vel_in[3, 0] - own_last[0])
                  - carry_north * (own_last[1] + vel_in[3, 1]) * (own_last[0] + vel_in[3, 0])),
        0.0)
    flux_s = jnp.where(
        shared_s > level_row,
        0.0625 * (1.92 * (own_first[0] - vel_in[0, 0])
                  - (own_first[1] + vel_in[0, 1]) * (own_first[0] + vel_in[0, 0])),
        0.0)
    first_own, last_own = pl.ds(0, 8), pl.ds(rows - 8, 8)
    total[last_own, :] = total[last_own, :] + jnp.where(
        row == 7, jnp.sum(flux_n, axis=0, keepdims=True), 0.0)
    total[first_own, :] = total[first_own, :] - jnp.where(
        row == 0, jnp.sum(flux_s, axis=0, keepdims=True), 0.0)

    for half in range(2):
        at = pl.ds(half * part, part)
        mine, from_w, from_e = ends_out[at, :], ends_w[at, :], ends_e[at, :]
        here = jnp.where(even, mine, roll(from_w, 1))
        there = jnp.where(even, roll(from_e, -1), mine)
        carried = roll(here + there, -16) * (here + there)
        level = ((lane_p % 16) // 2).astype(jnp.float32)
        through = jnp.where(
            jnp.logical_and(flux[at, :] > level, lane_p % 32 < 16),
            0.0625 * (1.92 * (there - here) - carried), 0.0)
        through = jnp.where(even, through, -through)
        flux[at, :] = through
        for shift in (2, 4, 8):
            through = through + roll(through, -shift)
        flux_sum[at, :] = through

    def right_side(c):
        at = pl.ds(c * part, part)
        lane_p = lanes(part)
        ends = jnp.logical_or(lane_p == 0, lane_p == LANES - 1)
        across = roll(flux_sum[pl.ds((c % 2) * part, part), :], 127 - 32 * (c // 2))
        summed = total[at, :] + jnp.where(ends, across, 0.0)
        value = jnp.where(lv[0, part_rows(c), :] > 0.0, fo[at, :], 0.0) + summed * 8.0 ** -0.5
        basis[0, 0, part_rows(c), :] = value
        return value

    loads[5].wait()
    edge_out[...] = fold([right_side(c) for c in range(PARTS)])
    for side, r, _ in edges:
        edge_rows_out[side] = basis[0, 0, pl.ds(r, GHOST), :]
    side_sent, side_received = exchange(
        2, edge_out, edge_w, edge_e, edge_rows_out, edge_rows, True)

    def place_rows(buffer, get):
        for r, across, w_at, e_at in ((south, 0, 1, 2), (top, 3, 4, 5)):
            at = pl.ds(r, GHOST)
            buffer[0, at, :] = get(across)
            buffer[1, at, :] = jnp.where(
                lane < EDGE, get(e_at), jnp.where(lane >= LANES - EDGE, get(w_at), 0.0))

    for buffer, at, field in ((lv, at_l, 0), (st, at_s, 1)):
        for c, x in enumerate(unfold(beside_w[at, :], beside_e[at, :])):
            buffer[1, part_rows(c), :] = x
        place_rows(buffer, lambda place, field=field: rows_in[place, field])

    fold_row = jnp.where(is_top, top - 1, -1)

    def weigh(a, b):
        return a * b / (a + b + 1.0)

    def weights_rows(r, n, carry):
        at, up = pl.ds(r, n), pl.ds(r + 1, n)
        lane = lanes(n)
        d_m, d_s = lv[0, at, :], lv[1, at, :]
        n_m, n_s = lv[0, up, :], lv[1, up, :]
        e_m, e_s = ring_east(d_m, d_s, lane)
        ne_m, ne_s = ring_east(n_m, n_s, lane)
        nw_m, nw_s = ring_west(n_m, n_s, lane)
        corner = jnp.where(row_is(r, n, fold_row), 0.0, 0.25)
        east_m, east_s = weigh(d_m, e_m), weigh(d_s, e_s)
        neast_m, neast_s = corner * weigh(d_m, ne_m), corner * weigh(d_s, ne_s)
        nwest_m, nwest_s = corner * weigh(d_m, nw_m), corner * weigh(d_s, nw_s)
        w_e[0, at, :], w_e[1, at, :] = east_m, east_s
        w_n[0, at, :], w_n[1, at, :] = weigh(d_m, n_m), weigh(d_s, n_s)
        w_ne[0, at, :], w_ne[1, at, :] = neast_m, neast_s
        w_nw[0, at, :], w_nw[1, at, :] = nwest_m, nwest_s
        w_er[0, at, :], w_er[1, at, :] = ring_west(east_m, east_s, lane)
        w_ner[0, at, :], w_ner[1, at, :] = ring_west(neast_m, neast_s, lane)
        w_nwr[0, at, :], w_nwr[1, at, :] = ring_east(nwest_m, nwest_s, lane)
        return carry

    sweep("weights", south, reach, WEIGHTS_STEP, weights_rows)

    def diagonal_rows(r, n, carry):
        at, down = pl.ds(r, n), pl.ds(r - 1, n)
        for half in range(2):
            whole = (
                st[half, at, :] + w_e[half, at, :] + w_er[half, at, :] + w_n[half, at, :]
                + w_n[half, down, :] + w_ne[half, at, :] + w_nw[half, at, :]
                + w_ner[half, down, :] + w_nwr[half, down, :])
            rdiag[half, at, :] = jnp.where(whole > 0.0, 1.0 / whole, 0.0)
            if half == 0:
                diag[at, :] = whole
        return carry

    sweep("diagonal", south, reach, DIAGONAL_STEP, diagonal_rows)
    diag[pl.ds(south, GHOST), :] = nothing
    diag[pl.ds(top, GHOST), :] = nothing

    def ends_rows(r, n, carry):
        lane = lanes(n)
        ends = jnp.logical_or(lane == 0, lane == LANES - 1)
        across = flux[pl.ds(r, n), :]
        for c in range(PARTS // 2):
            at = pl.ds(c * 2 * part + r, n)
            for k in range(LEVELS):
                nt[k, at, :] = nt[k, at, :] + jnp.where(
                    ends, roll(across, 127 - 32 * c - 2 * k), 0.0)
        return carry

    sweep("new", 0, 2 * part, part, ends_rows)
    for k in range(LEVELS):
        nt[k, last_own, :] = nt[k, last_own, :] + jnp.where(row == 7, flux_n[k:k + 1], 0.0)
        nt[k, first_own, :] = nt[k, first_own, :] - jnp.where(row == 0, flux_s[k:k + 1], 0.0)
    out_new = local_copy("out", nt, new_out, out_sem.at[0])
    out_new.start()

    side_received()
    pl.when(jnp.logical_not(not_bottom))(lambda: clear(edge_rows))

    @pl.when(is_top)
    def _():
        for place in (3, 4, 5):
            edge_rows[place] = mirror(edge_rows[place])

    for c, x in enumerate(unfold(edge_w[...], edge_e[...])):
        basis[0, 1, part_rows(c), :] = x
    place_rows(basis.at[0], lambda place: edge_rows[place])

    gram = {}

    def fold_rows(x):
        return jnp.sum(x.reshape(x.shape[0] // 8, 8, LANES), axis=0)

    def scaled_rows(r, n, acc):
        at = pl.ds(r, n)
        for half in range(2):
            x = basis[0, half, at, :]
            y = x * rdiag[half, at, :]
            basis[0, half, at, :] = y
            if half == 0:
                acc = acc + fold_rows(diag[at, :] * y * y)
        return acc

    gram[0, 0] = sweep("scaled", south, reach, SCALED_STEP, scaled_rows, nothing)

    def neighbours_sum(k, r, n, halves):
        at, up, down = pl.ds(r, n), pl.ds(r + 1, n), pl.ds(r - 1, n)
        lane = lanes(n)
        sums, to_west, to_east = [], [], []
        for half in range(2):
            x = basis[k, half, at, :]
            x_n = basis[k, half, up, :]
            x_s = basis[k, half, down, :]
            to_east.append(
                w_e[half, at, :] * x + w_ne[half, down, :] * x_s + w_nwr[half, at, :] * x_n)
            to_west.append(
                w_er[half, at, :] * x + w_nw[half, down, :] * x_s + w_ner[half, at, :] * x_n)
            if half < halves:
                sums.append(w_n[half, at, :] * x_n + w_n[half, down, :] * x_s)
        from_west = ring_west(to_east[0], to_east[1], lane)
        from_east = ring_east(to_west[0], to_west[1], lane)
        return [sums[h] + from_west[h] + from_east[h] for h in range(halves)]

    def apply_rows(k, r, n, halves):
        at = pl.ds(r, n)
        sums = neighbours_sum(k, r, n, halves)
        out = []
        for half in range(halves):
            x = basis[k, half, at, :]
            y = rdiag[half, at, :] * sums[half]
            if SHIFT[k] != 0.0:
                y = y - SHIFT[k] * x
            if BACK[k] != 0.0:
                y = y - BACK[k] * basis[k - 1, half, at, :]
            y = GAIN[k] * y
            basis[k + 1, half, at, :] = y
            out.append(y)
        return out[0]

    for k in range(ITERS):
        last = k == ITERS - 1
        terms = [p for p in PAIRS if p[1] == k + 1]

        def apply_own(r, n, accs, k=k, terms=terms, halves=1 if last else 2):
            at = pl.ds(r, n)
            y = apply_rows(k, r, n, halves)
            scaled = diag[at, :] * y
            return tuple(
                acc + fold_rows(scaled * (y if a == k + 1 else basis[a, 0, at, :]))
                for acc, (a, _) in zip(accs, terms))

        sums = sweep(
            "apply", BASE if last else south, rows if last else reach,
            LAST_STEP if last else APPLY_STEP, apply_own, tuple(nothing for _ in terms))
        for p, s in zip(terms, sums):
            gram[p] = s

    per_lane = [jnp.sum(gram[p], axis=0, keepdims=True) for p in PAIRS]
    per_lane = per_lane + [jnp.zeros((1, LANES), jnp.float32)] * (24 - len(per_lane))
    stacked = jnp.sum(jnp.concatenate(per_lane, axis=0), axis=1, keepdims=True)
    count = stacked.shape[0]
    own_lane = lane_of((count, LANES)) == row_of((count, LANES))
    summed = jnp.sum(jnp.where(own_lane, stacked, 0.0), axis=0, keepdims=True)

    sends = []
    for stage, (place, peers) in enumerate(stages):
        box = boxes[stage]
        box[pl.ds(place, 1), :, :] = summed[None]
        for n, (_, device) in enumerate(peers):
            copy = remote(
                "red", box.at[place], box.at[place],
                red_send.at[stage, n], red_recv.at[stage, place], device)
            copy.start()
            sends.append(copy)
        for index, _ in peers:
            arrived("red", box.at[index], red_recv.at[stage, index])
        summed = box[0]
        for n in range(1, len(peers) + 1):
            summed = summed + box[n]

    spread = jnp.sum(
        jnp.where(own_lane, jnp.broadcast_to(summed, (count, LANES)), 0.0),
        axis=1, keepdims=True)
    sums = {
        p: jnp.broadcast_to(spread[n:n + 1], tile) for n, p in enumerate(PAIRS)
    }
    surface_by, scaled_by = solve(sums)

    surface_by = [c[0:1] for c in surface_by]
    scaled_by = [c[0:1] for c in scaled_by]

    def final_rows(r, n, carry):
        at = pl.ds(r, n)
        to = pl.ds(pl.multiple_of(r - BASE, 8), n)
        x = [basis[k, 0, at, :] for k in range(ITERS + 1)]
        level_at = surface_by[0] * x[0]
        left = scaled_by[0] * x[0]
        for k in range(1, ITERS + 1):
            if k < ITERS:
                level_at = level_at + surface_by[k] * x[k]
            left = left + scaled_by[k] * x[k]
        surf[to, :] = level_at
        resid[to, :] = diag[at, :] * left
        return carry

    sweep("final", BASE, rows, FINAL_STEP, final_rows)
    out_surf = local_copy("out", surf, surf_out, out_sem.at[1])
    out_res = local_copy("out", resid, res_out, out_sem.at[2])
    out_surf.start()
    out_res.start()

    depth_sent()
    ends_sent()
    side_sent()
    for copy in sends:
        copy.wait_send()
    out_new.wait()
    out_surf.wait()
    out_res.wait()


def hand_over(new, surf, res, new_out, surf_out, res_out, cube, flat, in_sem, out_sem):
    pieces = [(surf, flat.at[0], surf_out), (res, flat.at[1], res_out)] + [
        (new.at[k], cube.at[k], new_out.at[k]) for k in range(LEVELS)]
    reads = [pltpu.make_async_copy(a, b, in_sem.at[n]) for n, (a, b, _) in enumerate(pieces)]
    writes = [pltpu.make_async_copy(b, c, out_sem.at[n]) for n, (_, b, c) in enumerate(pieces)]
    for read in reads:
        read.start()
    for read, write in zip(reads, writes):
        read.wait()
        write.start()
    for write in writes:
        write.wait()


def local(lon_count, lat_count, tracer, east_vel, north_vel, levels, forcing, storage):
    rows = tracer.shape[1]
    flat = (rows + 4 * GHOST, LANES)
    part = rows // PARTS
    f32 = jnp.float32
    extent = extents(lon_count, lat_count)
    sizes = [stage_size(extent, axes) for axes in STAGES]

    def vmem(*shape, dtype=f32):
        return pltpu.VMEM(shape, dtype)

    cube = vmem(LEVELS, rows + 2 * GHOST, LANES)
    pair = vmem(2, *flat)
    block = vmem(rows, LANES)
    beside = vmem(2 * part, LANES)
    edge = vmem(part, LANES)
    dma = pltpu.SemaphoreType.DMA
    anywhere = pl.BlockSpec(memory_space=pl.ANY)
    outs = (
        jax.ShapeDtypeStruct(tracer.shape, f32),
        jax.ShapeDtypeStruct(levels.shape, f32),
        jax.ShapeDtypeStruct(levels.shape, f32),
    )
    results = pl.pallas_call(
        functools.partial(kernel, lon_count, lat_count, rows),
        out_shape=outs,
        in_specs=[anywhere] * 6,
        out_specs=(anywhere,) * 3,
        scratch_shapes=[
            cube, cube, cube, vmem(rows, LANES, dtype=jnp.int32), block, pair, pair,
            beside, beside, beside, vmem(2, 2, 8, LANES), vmem(6, 2, 8, LANES),
            beside, beside, beside, vmem(2, 2, 8, LANES), vmem(2, 2, 8, LANES),
            vmem(6, 2, 8, LANES), vmem(8, LANES),
            edge, edge, edge, vmem(2, 8, LANES), vmem(6, 8, LANES),
            vmem(2 * part, LANES), vmem(2 * part, LANES), block, vmem(LEVELS, rows, LANES),
            pair, pair, pair, pair, pair, pair, pair, pair, vmem(*flat),
            vmem(ITERS + 1, 2, *flat),
            block, block,
            dma((6,)), dma((3, 6)), dma((3, 6)), dma((3, 2)), dma((3, 2)),
            dma((len(sizes), max(sizes))), dma((len(sizes), max(sizes))), dma((3,)),
            *[vmem(size, 1, LANES) for size in sizes],
        ],
        compiler_params=pltpu.CompilerParams(
            collective_id=0, has_side_effects=True, vmem_limit_bytes=61 * 2**20
        ),
        cost_estimate=pl.CostEstimate(flops=10**8, bytes_accessed=6 * 10**6, transcendentals=0),
        name="ocean_step",
    )(tracer, east_vel, north_vel, levels, forcing, storage)
    return pl.pallas_call(
        hand_over,
        out_shape=outs,
        in_specs=[anywhere] * 3,
        out_specs=(anywhere,) * 3,
        scratch_shapes=[
            vmem(*tracer.shape), vmem(2, rows, LANES),
            dma((LEVELS + 2,)), dma((LEVELS + 2,)),
        ],
        compiler_params=pltpu.CompilerParams(vmem_limit_bytes=61 * 2**20),
        name="hand_over",
    )(*results)


def solution(mesh):
    cube, flat = P(None, "lat", "lon"), P("lat", "lon")
    return jax.shard_map(
        functools.partial(local, mesh.shape["lon"], mesh.shape["lat"]),
        mesh=mesh,
        in_specs=(cube, cube, cube, flat, flat, flat),
        out_specs=(cube, flat, flat),
        check_vma=False,
    )
```
